512 devices in a mesh: dp: 128 (over z, y, core), group: 4 (over x).
Axes of the slice: x: 4, y: 8, z: 8, core: 2. Of those that a mesh axis runs over, the one named last changes fastest.
Arguments:
- queries: bfloat16 [2048, 32, 128], P(('dp', 'group'))
- positives: bfloat16 [2048, 64, 128], P(('dp', 'group'))
- passage_pool: bfloat16 [4096, 64, 128], P('dp')
- negative_ids: int32 [2048, 7], P(('dp', 'group')), may hold values from 0 to 4095, as said below
- storage_row: int32 [4096], replicated, may hold values from 0 to 4095, as said below
Outputs:
- losses: float32 [2048], P(('dp', 'group'))
- query_grad: float32 [2048, 32, 128], P(('dp', 'group'))
- positive_grad: float32 [2048, 64, 128], P(('dp', 'group'))
- pool_grad: float32 [4096, 64, 128], P(('dp', 'group'))
The draws below stay inside these ranges and needn't reach their ends.
Inputs may be any that keep to these rules, and one draw needn't show every extreme that they name: `storage_row`: each passage id appears exactly once. `negative_ids`: in each aligned block of 4 rows (the queries of one device), at most 2 of the 28 ids have storage_row[id] // 32 equal to any one value; in every block some value is reached exactly 2 times.
All inputs are finite; a program needn't handle non-finite values.
Results may differ from the reference program's by a relative error of at most 0.02.
Values may be sent and summed in bfloat16 or wider, within the bound.
No kernel may reach another device: no remote copies, remote signals or barrier semaphores. Data moves between devices by JAX's collectives and lax.ppermute only.
A program may use at most 128 MiB of HBM per device.

```python
import math
import jax
import jax.numpy as jnp
from jax import lax

D = 128
QT = 32
PT = 64
NEG = 7
Q_DEV = 4
P_DEV = 32
CAP = 2
QUERIES = 2048
PASSAGES = 4096
N_DP = 128
N_GROUP = 4


def layout_draw(key):
    perm_key, hot_key, class_key, noise_key, shuffle_key, row_key = jax.random.split(key, 6)
    storage = jax.random.permutation(perm_key, PASSAGES).astype(jnp.int32)
    inverse = jnp.argsort(storage).astype(jnp.int32)
    position_count = N_DP * CAP
    requests = Q_DEV * NEG
    device_total = QUERIES // Q_DEV
    position_holder = jnp.arange(position_count, dtype=jnp.int32) // CAP
    busiest_holder_rank = jax.random.randint(hot_key, (), 0, N_DP)
    holder_category = jax.random.randint(class_key, (N_DP,), 0, 4)
    holder_preference = holder_category * 1024 + jnp.where(jnp.arange(N_DP) == busiest_holder_rank, 8192, 0)
    jitter_amplitude = jax.random.randint(noise_key, (device_total, position_count), 0, 1024)
    position_rating = (jitter_amplitude + holder_preference[position_holder][None, :]) * position_count + jnp.arange(position_count, dtype=jnp.int32)[None, :]
    top_values, picked = lax.top_k(position_rating, requests)
    shuffle_score = jax.random.randint(shuffle_key, (device_total, requests), 0, 4096) * requests + jnp.arange(requests, dtype=jnp.int32)[None, :]
    shuffle = jnp.argsort(shuffle_score, axis=1)
    picked = jnp.take_along_axis(picked, shuffle, axis=1)
    local_row = jax.random.randint(row_key, (device_total, requests), 0, P_DEV)
    passage_ids = inverse[picked // CAP * P_DEV + local_row]
    return (storage, passage_ids.reshape(QUERIES, NEG).astype(jnp.int32))


def draw_storage_row(key, part):
    return layout_draw(key)[0]


def draw_negative_ids(key, part):
    return layout_draw(key)[1]


def draw_queries(key, part):
    key = jax.random.fold_in(key, 11)
    value_key, row_key, column_key = jax.random.split(key, 3)
    full_shape = (QUERIES, QT, D)
    values = jax.random.normal(value_key, full_shape, jnp.float32)
    row_scale = jnp.exp(jax.random.uniform(row_key, (QUERIES, QT, 1), jnp.float32, 0.0, math.log(10.0)))
    column_scale = jnp.exp(jax.random.uniform(column_key, (D,), jnp.float32, 0.0, math.log(3.0)))
    return (values * row_scale * column_scale).astype(jnp.bfloat16)


def draw_positives(key, part):
    key = jax.random.fold_in(key, 12)
    value_key, row_key, column_key = jax.random.split(key, 3)
    full_shape = (QUERIES, PT, D)
    values = jax.random.normal(value_key, full_shape, jnp.float32)
    row_scale = jnp.exp(jax.random.uniform(row_key, (QUERIES, PT, 1), jnp.float32, 0.0, math.log(10.0)))
    column_scale = jnp.exp(jax.random.uniform(column_key, (D,), jnp.float32, 0.0, math.log(3.0)))
    return (values * row_scale * column_scale).astype(jnp.bfloat16)


def draw_passage_pool(key, part):
    key = jax.random.fold_in(key, 13)
    value_key, row_key, column_key = jax.random.split(key, 3)
    full_shape = (PASSAGES, PT, D)
    values = jax.random.normal(value_key, full_shape, jnp.float32)
    row_scale = jnp.exp(jax.random.uniform(row_key, (PASSAGES, PT, 1), jnp.float32, 0.0, math.log(10.0)))
    column_scale = jnp.exp(jax.random.uniform(column_key, (D,), jnp.float32, 0.0, math.log(3.0)))
    return (values * row_scale * column_scale).astype(jnp.bfloat16)


def setup_inputs(seed: int = 0) -> dict:
    key_list = jax.random.split(jax.random.key(seed), 6)
    return {
        "queries": draw_queries(jax.random.fold_in(key_list[5], 71), 0),
        "positives": draw_positives(jax.random.fold_in(key_list[5], 71), 0),
        "passage_pool": draw_passage_pool(jax.random.fold_in(key_list[5], 71), 0),
        "negative_ids": draw_negative_ids(jax.random.fold_in(key_list[5], 71), 0),
        "storage_row": draw_storage_row(jax.random.fold_in(key_list[5], 71), 0),
    }


soft_temp = 0.1

def unit_rows(values):
    widened = values.astype(jnp.float32)
    return (widened / jnp.sqrt(lax.optimization_barrier(jnp.sum(widened * widened, axis=-1, keepdims=True)) + 1e-06)).astype(jnp.bfloat16)

def token_softmax(token_scores):
    exp_scores = jnp.exp(token_scores / soft_temp)
    token_total = lax.optimization_barrier(jnp.sum(exp_scores, axis=-1))
    candidate_score = lax.optimization_barrier(jnp.sum(soft_temp * jnp.log(token_total), axis=-1))
    return (candidate_score, exp_scores / token_total[..., None])

def candidate_loss(candidate_score, own_index):
    cand_count = candidate_score.shape[-1]
    own_hot = (jnp.arange(cand_count, dtype=jnp.int32) == own_index[..., None]).astype(jnp.float32)
    weights = jnp.exp(candidate_score)
    weight_sum = lax.optimization_barrier(jnp.sum(weights, axis=-1))
    query_loss = jnp.log(weight_sum) - lax.optimization_barrier(jnp.sum(candidate_score * own_hot, axis=-1))
    return (query_loss, weights / weight_sum[..., None] - own_hot)

def query_terms(one_query, candidates, own_index):
    widened_query = one_query.astype(jnp.float32)
    widened_cands = candidates.astype(jnp.float32)
    token_scores = jnp.einsum('id,cjd->cij', widened_query, widened_cands, precision=lax.Precision.HIGHEST)
    candidate_score, token_probs = token_softmax(token_scores)
    query_loss, score_grad = candidate_loss(candidate_score, own_index)
    rounded = (score_grad[:, None, None] * token_probs).astype(jnp.bfloat16)
    weight_grad = lax.optimization_barrier(rounded).astype(jnp.float32)
    query_grad = jnp.einsum('cij,cjd->id', weight_grad, widened_cands, precision=lax.Precision.HIGHEST)
    cand_grad = jnp.einsum('cij,id->cjd', weight_grad, widened_query, precision=lax.Precision.HIGHEST)
    return (query_loss, query_grad, cand_grad)

def reference(queries, positives, passage_pool, negative_ids, storage_row):
    query_unit = unit_rows(queries)
    positive_unit = unit_rows(positives)
    pool_unit = unit_rows(passage_pool)
    block_rows = Q_DEV * N_GROUP
    pool_index = jnp.take(storage_row, negative_ids, axis=0).astype(jnp.int32)

    def one_block(running, block_index):
        first_row = (block_index * block_rows).astype(jnp.int32)
        block_queries = lax.dynamic_slice_in_dim(query_unit, first_row, block_rows, 0)
        block_positives = lax.dynamic_slice_in_dim(positive_unit, first_row, block_rows, 0)
        block_pool_rows = lax.dynamic_slice_in_dim(pool_index, first_row, block_rows, 0)
        block_negatives = jnp.take(pool_unit, block_pool_rows, axis=0)

        def score_one(inputs):
            query_vectors, own_index, negatives = inputs
            candidates = jnp.concatenate([block_positives, negatives], axis=0)
            return query_terms(query_vectors, candidates, own_index)
        query_loss, query_grad, cand_grad = lax.map(score_one, (block_queries, jnp.arange(block_rows, dtype=jnp.int32), block_negatives))
        positive_grad = lax.optimization_barrier(jnp.sum(cand_grad[:, :block_rows], axis=0))
        running = running.at[block_pool_rows.reshape(-1)].add(cand_grad[:, block_rows:].reshape(-1, PT, D))
        return (running, (query_loss, query_grad, positive_grad))
    start_grad = jnp.zeros((PASSAGES, PT, D), jnp.float32)
    pool_grad, (losses, query_grad, positive_grad) = lax.scan(one_block, start_grad, jnp.arange(QUERIES // block_rows, dtype=jnp.int32))
    return (losses.reshape(QUERIES), query_grad.reshape(QUERIES, QT, D), positive_grad.reshape(QUERIES, PT, D), pool_grad)
```

```python
import jax
import jax.numpy as jnp
from jax import lax
from jax.experimental import pallas as pl
from jax.experimental.pallas import tpu as pltpu
from jax.sharding import Mesh, PartitionSpec as P

LINE = ("c", "y", "z")
N_Z, N_Y, N_C = 8, 8, 2
N_LINE = N_Z * N_Y * N_C
HALF = N_LINE // 2
QD, QT, PT, D, NEG, ROWS, GROUP = 4, 32, 64, 128, 7, 32, 4
QROWS = QD * QT
SENT = QROWS + 16
BATCH = QD * GROUP
VMEM = 48 * 1024 * 1024
F32, BF16, I32 = jnp.float32, jnp.bfloat16, jnp.int32
EXACT = lax.Precision.HIGHEST


def call(body, out_shape, in_specs, out_specs, scratch=()):
    return pl.pallas_call(
        body,
        out_shape=out_shape,
        in_specs=in_specs,
        out_specs=out_specs,
        scratch_shapes=list(scratch),
        compiler_params=pltpu.CompilerParams(vmem_limit_bytes=VMEM),
    )


def vmem():
    return pl.BlockSpec(memory_space=pltpu.VMEM)


def smem():
    return pl.BlockSpec(memory_space=pltpu.SMEM)


def unit(values):
    wide = values.astype(F32)
    return (wide * lax.rsqrt(jnp.sum(wide * wide, axis=-1, keepdims=True) + 1e-06)).astype(BF16)


def iota(shape, dim):
    return lax.broadcasted_iota(I32, shape, dim)


def dot(a, b, dims, precision=None):
    return lax.dot_general(a, b, ((dims[0], dims[1]), ((), ())), precision=precision, preferred_element_type=F32)


def token_sum_matrix():
    return (iota((QROWS, QROWS), 0) // QT == iota((QROWS, QROWS), 1) // QT).astype(F32)


def prepare(ids, storage, queries, positives, sent, pos_unit, slots, count):
    sent[0:QROWS, :] = unit(queries[...]).reshape(QROWS, D)
    pos_unit[...] = unit(positives[...])
    lane = iota((16, N_LINE), 1)
    sub = iota((16, N_LINE), 0)
    homes = []
    for q in range(QD):
        for k in range(NEG):
            home = storage[ids[q, k]]
            owner = home // ROWS
            line = (owner % 2) * HALF + ((owner // 2) % N_Y) * N_Z + owner // (2 * N_Y)
            count[line] = 0
            homes.append((line, q * ROWS + home % ROWS + 1))
    codes = jnp.zeros((16, N_LINE), F32)
    for p, (line, code) in enumerate(homes):
        rank = count[line]
        count[line] = rank + 1
        slots[p] = line * 2 + jnp.minimum(rank, 1)
        codes = jnp.where((lane == line) & (sub == rank), code.astype(F32), codes)
    sent[QROWS:SENT, :] = codes.astype(BF16)


def positive_scores(q_unit, gathered):
    cands = gathered[...].reshape(BATCH * PT, D)
    exp_scores = jnp.exp(10.0 * dot(cands, q_unit, ((1,), (1,)))).reshape(BATCH, PT, QROWS)
    total = jnp.sum(exp_scores, axis=1)
    score = 0.1 * dot(jnp.log(total), token_sum_matrix(), ((1,), (0,)), EXACT)
    return cands, exp_scores, total, score


def request(codes, line, slot):
    code = codes[line, slot]
    spot = jnp.maximum(code - 1, 0)
    return code > 0, spot // ROWS, spot % ROWS


def four(step):
    return ((step, 0), (step, 1), (step + HALF, 0), (step + HALF, 1))


def spread(packed):
    block = iota((PT, QROWS), 1) // QT
    return jnp.concatenate([jnp.where(block == b, packed, 0.0).astype(BF16) for b in range(4)], axis=0)


def query_tile(sent, line, q):
    return sent[pl.ds(pl.multiple_of(line * SENT + q * QT, 16), QT), :]


def serve(me, codes, sent, pool, own_sent, gathered, back, probs, sums, rows, exps, totals, marks, factor):
    rows[...] = unit(pool[...])
    lane = iota((1, QROWS), 1)
    block = iota((PT, QROWS), 1) // QT

    def score(step, carry):
        q_tiles, c_tiles = [], []
        mark = jnp.full((1, QROWS), -1.0, F32)
        for b, (line, slot) in enumerate(four(step)):
            valid, q, row = request(codes, line, slot)
            q_tiles.append(query_tile(sent, line, q))
            c_tiles.append(rows[row])
            mark = jnp.where((lane // QT == b) & valid, q.astype(F32), mark)
        full = dot(jnp.concatenate(c_tiles, axis=0), jnp.concatenate(q_tiles, axis=0), ((1,), (1,)))
        packed = full[0:PT]
        for b in range(1, 4):
            packed = jnp.where(block == b, full[b * PT : (b + 1) * PT], packed)
        exp_scores = jnp.exp(10.0 * packed)
        exps[step] = exp_scores
        totals[pl.ds(step, 1), :] = jnp.sum(exp_scores, axis=0, keepdims=True)
        marks[pl.ds(step, 1), :] = mark
        return carry

    lax.fori_loop(0, HALF, score, 0, unroll=4)

    total = totals[...]
    mark = marks[...]
    weight = jnp.exp(0.1 * dot(jnp.log(total), token_sum_matrix(), ((1,), (0,)), EXACT))
    weight = jnp.where(mark >= 0.0, weight, 0.0)
    factor[...] = weight / total

    first = iota((QROWS, N_LINE), 0)
    last = iota((QROWS, N_LINE), 1)
    pick = ((first % QT == 0) & (first // (2 * QT) == last // HALF)).astype(F32)
    diag = iota((HALF, N_LINE), 1) % HALF == iota((HALF, N_LINE), 0)
    q_unit = own_sent[0:QROWS, :]
    _, _, _, pos_score = positive_scores(q_unit, gathered)
    pos_weight = jnp.sum(jnp.exp(pos_score), axis=0, keepdims=True)
    parts = []
    for q in range(QD):
        of_query = dot(jnp.where(mark == float(q), weight, 0.0), pick, ((1,), (0,)), EXACT)
        part = jnp.sum(jnp.where(diag, of_query, 0.0), axis=0, keepdims=True)
        own = jnp.sum(jnp.where(lane == q * QT, pos_weight, 0.0), axis=1, keepdims=True)
        parts.append(part + jnp.where(iota((1, N_LINE), 1) == me[0], own, 0.0))
    sums[...] = jnp.broadcast_to(jnp.concatenate(parts, axis=0)[None], (N_LINE, QD, N_LINE))

    def terms(step, carry):
        packed = (exps[step] * factor[pl.ds(step, 1), :]).astype(BF16)
        probs[step] = packed
        c_tiles = [rows[request(codes, line, slot)[2]] for line, slot in four(step)]
        grads = dot(spread(packed.astype(F32)), jnp.concatenate(c_tiles, axis=0), ((0,), (0,))).astype(BF16)
        back[step] = grads[0 : 2 * QT].reshape(2, QT, D)
        back[step + HALF] = grads[2 * QT :].reshape(2, QT, D)
        return carry

    lax.fori_loop(0, HALF, terms, 0, unroll=4)


def weigh(me, codes, weight_sum, weight_inv, sent, probs, own_sent, gathered, out, query_part, losses, acc):
    acc[...] = jnp.zeros_like(acc)

    def add(step, carry):
        spots = [(line,) + request(codes, line, slot) for line, slot in four(step)]
        q_tiles = [query_tile(sent, line, q) for line, _, q, _ in spots]
        grads = dot(spread(probs[step].astype(F32)), jnp.concatenate(q_tiles, axis=0), ((1,), (0,)))
        for b, (line, _, q, row) in enumerate(spots):
            acc[row] += grads[b * PT : (b + 1) * PT] * weight_inv[q, line]
        return carry

    lax.fori_loop(0, HALF, add, 0, unroll=4)

    q_unit = own_sent[0:QROWS, :]
    cands, exp_scores, total, score = positive_scores(q_unit, gathered)
    lane = iota((1, QROWS), 1)
    own_sum = jnp.zeros((1, QROWS), F32)
    for q in range(QD):
        own_sum = jnp.where(lane // QT == q, weight_sum[q, me[0]], own_sum)
    own = (iota((BATCH, QROWS), 0) == me[1] * QD + iota((BATCH, QROWS), 1) // QT).astype(F32)
    score_grad = jnp.exp(score) / own_sum - own
    losses[...] = jnp.log(own_sum) - jnp.sum(score * own, axis=0, keepdims=True)
    weight_grad = (exp_scores * (score_grad / total)[:, None, :]).astype(BF16).reshape(BATCH * PT, QROWS)
    query_part[...] = dot(weight_grad, cands, ((0,), (0,)))
    pos_part = dot(weight_grad, q_unit, ((1,), (0,))).astype(BF16).reshape(BATCH, PT, D)
    share = ROWS // GROUP
    for g in range(GROUP):
        out[g, 0:QD] = pos_part[g * QD : (g + 1) * QD]
        out[g, QD:] = acc[g * share : (g + 1) * share].astype(BF16)


def collect(slots, weight_inv, me, query_part, arrived, out, tiles, sems):
    copies = [
        pltpu.make_async_copy(arrived.at[slots[p] // 2, slots[p] % 2], tiles.at[p], sems.at[p])
        for p in range(QD * NEG)
    ]
    for copy in copies:
        copy.start()
    for copy in copies:
        copy.wait()
    for q in range(QD):
        total = jnp.sum(tiles[q * NEG : (q + 1) * NEG].astype(F32), axis=0)
        out[q] = query_part[q * QT : (q + 1) * QT, :] + total * weight_inv[q, me[0]]


def per_device(queries, positives, passage_pool, negative_ids, storage_row):
    struct = jax.ShapeDtypeStruct
    me = jnp.stack([lax.axis_index(LINE), lax.axis_index("x")]).astype(I32)
    own_sent, pos_unit, slots = call(
        prepare,
        (struct((SENT, D), BF16), struct((QD, PT, D), BF16), struct((QD * NEG,), I32)),
        [smem(), smem(), vmem(), vmem()],
        (vmem(), vmem(), smem()),
        [pltpu.SMEM((N_LINE,), I32)],
    )(negative_ids, storage_row, queries, positives)

    sent = own_sent[None]
    for axis in ("z", "y", "c"):
        sent = lax.all_gather(sent, axis, axis=0, tiled=True)
    gathered = lax.all_gather(pos_unit, "x", axis=0, tiled=True)
    codes = lax.dynamic_index_in_dim(sent[:, QROWS : QROWS + 2, :], me[0], axis=2, keepdims=False).astype(I32)
    sent = sent.reshape(N_LINE * SENT, D)

    back, probs, sums = call(
        serve,
        (
            struct((N_LINE, 2, QT, D), BF16),
            struct((HALF, PT, QROWS), BF16),
            struct((N_LINE, QD, N_LINE), F32),
        ),
        [smem(), smem(), vmem(), vmem(), vmem(), vmem()],
        (vmem(), vmem(), vmem()),
        [
            pltpu.VMEM((ROWS, PT, D), BF16),
            pltpu.VMEM((HALF, PT, QROWS), F32),
            pltpu.VMEM((HALF, QROWS), F32),
            pltpu.VMEM((HALF, QROWS), F32),
            pltpu.VMEM((HALF, QROWS), F32),
        ],
    )(me, codes, sent, passage_pool, own_sent, gathered)

    sums_in = lax.all_to_all(sums, LINE, split_axis=0, concat_axis=0, tiled=True)
    arrived = lax.all_to_all(back, LINE, split_axis=0, concat_axis=0, tiled=True)
    weight_sum = jnp.sum(sums_in, axis=0)
    weight_inv = 1.0 / weight_sum

    parts, query_part, losses = call(
        weigh,
        (
            struct((GROUP, QD + ROWS // GROUP, PT, D), BF16),
            struct((QROWS, D), F32),
            struct((1, QROWS), F32),
        ),
        [smem(), smem(), smem(), smem(), vmem(), vmem(), vmem(), vmem()],
        (vmem(), vmem(), vmem()),
        [pltpu.VMEM((ROWS, PT, D), F32)],
    )(me, codes, weight_sum, weight_inv, sent, probs, own_sent, gathered)

    parts_in = lax.all_to_all(parts, "x", split_axis=0, concat_axis=0, tiled=True)
    total = jnp.sum(parts_in.astype(F32), axis=0)

    query_grad = call(
        collect,
        struct((QD, QT, D), F32),
        [smem(), smem(), smem(), vmem(), pl.BlockSpec(memory_space=pl.ANY)],
        vmem(),
        [pltpu.VMEM((QD * NEG, QT, D), BF16), pltpu.SemaphoreType.DMA((QD * NEG,))],
    )(slots, weight_inv, me, query_part, arrived)
    return losses.reshape(QD, QT)[:, 0], query_grad, total[:QD], total[QD:]


def solution(mesh):
    fine = Mesh(mesh.devices.reshape(N_Z, N_Y, N_C, GROUP), ("z", "y", "c", "x"))
    every, line = ("z", "y", "c", "x"), ("z", "y", "c")
    in_specs = (P(every), P(every), P(line), P(every), P())
    out_specs = (P(every), P(every), P(every), P(every))
    return jax.shard_map(per_device, mesh=fine, in_specs=in_specs, out_specs=out_specs, check_vma=False)
```

```python
import jax
import jax.numpy as jnp
from jax import lax
from jax.experimental import pallas as pl
from jax.experimental.pallas import tpu as pltpu
from jax.sharding import Mesh, PartitionSpec as P

LINE = ("c", "y", "z")
N_Z, N_Y, N_C = 8, 8, 2
N_LINE = N_Z * N_Y * N_C
HALF = N_LINE // 2
QD, QT, PT, D, NEG, ROWS, GROUP = 4, 32, 64, 128, 7, 32, 4
QROWS = QD * QT
SENT = 2 * QT + 8
BATCH = QD * GROUP
VMEM = 48 * 1024 * 1024
F32, BF16, I32 = jnp.float32, jnp.bfloat16, jnp.int32
EXACT = lax.Precision.HIGHEST


def call(body, out_shape, in_specs, out_specs, scratch=()):
    return pl.pallas_call(
        body,
        out_shape=out_shape,
        in_specs=in_specs,
        out_specs=out_specs,
        scratch_shapes=list(scratch),
        compiler_params=pltpu.CompilerParams(vmem_limit_bytes=VMEM),
    )


def vmem():
    return pl.BlockSpec(memory_space=pltpu.VMEM)


def smem():
    return pl.BlockSpec(memory_space=pltpu.SMEM)


def unit(values):
    wide = values.astype(F32)
    return (wide * lax.rsqrt(jnp.sum(wide * wide, axis=-1, keepdims=True) + 1e-06)).astype(BF16)


def iota(shape, dim):
    return lax.broadcasted_iota(I32, shape, dim)


def dot(a, b, dims, precision=None):
    return lax.dot_general(a, b, ((dims[0], dims[1]), ((), ())), precision=precision, preferred_element_type=F32)


def token_sum_matrix():
    return (iota((QROWS, QROWS), 0) // QT == iota((QROWS, QROWS), 1) // QT).astype(F32)


def prepare(ids, storage, queries, positives, sent, q_unit, pos_unit, slots, count):
    q_unit[...] = unit(queries[...])
    pos_unit[...] = unit(positives[...])
    sent[...] = jnp.zeros_like(sent)
    homes = []
    for q in range(QD):
        for k in range(NEG):
            home = storage[ids[q, k]]
            owner = home // ROWS
            line = (owner % 2) * HALF + ((owner // 2) % N_Y) * N_Z + owner // (2 * N_Y)
            count[line] = 0
            homes.append((line, q, q * ROWS + home % ROWS + 1))
    sub = iota((8, D), 0)
    for p, (line, q, code) in enumerate(homes):
        rank = jnp.minimum(count[line], 1)
        count[line] = rank + 1
        slots[p] = line * 2 + rank
        sent[line, pl.ds(pl.multiple_of(rank * QT, QT), QT), :] = q_unit[q]
        marks = sent[line, 2 * QT : SENT, :].astype(F32)
        sent[line, 2 * QT : SENT, :] = jnp.where(sub == rank, code.astype(F32), marks).astype(BF16)


def positive_scores(q_unit, gathered):
    cands = gathered[...].reshape(BATCH * PT, D)
    exp_scores = jnp.exp(10.0 * dot(cands, q_unit, ((1,), (1,)))).reshape(BATCH, PT, QROWS)
    total = jnp.sum(exp_scores, axis=1)
    score = 0.1 * dot(jnp.log(total), token_sum_matrix(), ((1,), (0,)), EXACT)
    return cands, exp_scores, total, score


def request(codes, line, slot):
    code = codes[line, slot]
    spot = jnp.maximum(code - 1, 0)
    return code > 0, spot // ROWS, spot % ROWS


def four(step):
    return ((step, 0), (step, 1), (step + HALF, 0), (step + HALF, 1))


def spread(packed):
    block = iota((PT, QROWS), 1) // QT
    return jnp.concatenate([jnp.where(block == b, packed, 0.0).astype(BF16) for b in range(4)], axis=0)


def query_tiles(sent, step):
    return jnp.concatenate([sent[step, 0 : 2 * QT], sent[step + HALF, 0 : 2 * QT]], axis=0)


def serve(me, codes, sent, pool, own_queries, gathered, back, probs, sums, rows, exps, totals, marks, factor):
    rows[...] = unit(pool[...])
    lane = iota((1, QROWS), 1)
    block = iota((PT, QROWS), 1) // QT

    def score(step, carry):
        c_tiles = []
        mark = jnp.full((1, QROWS), -1.0, F32)
        for b, (line, slot) in enumerate(four(step)):
            valid, q, row = request(codes, line, slot)
            c_tiles.append(rows[row])
            mark = jnp.where((lane // QT == b) & valid, q.astype(F32), mark)
        full = dot(jnp.concatenate(c_tiles, axis=0), query_tiles(sent, step), ((1,), (1,)))
        packed = full[0:PT]
        for b in range(1, 4):
            packed = jnp.where(block == b, full[b * PT : (b + 1) * PT], packed)
        exp_scores = jnp.exp(10.0 * packed)
        exps[step] = exp_scores
        totals[pl.ds(step, 1), :] = jnp.sum(exp_scores, axis=0, keepdims=True)
        marks[pl.ds(step, 1), :] = mark
        return carry

    lax.fori_loop(0, HALF, score, 0, unroll=4)

    total = totals[...]
    mark = marks[...]
    weight = jnp.exp(0.1 * dot(jnp.log(total), token_sum_matrix(), ((1,), (0,)), EXACT))
    weight = jnp.where(mark >= 0.0, weight, 0.0)
    factor[...] = weight / total

    first = iota((QROWS, N_LINE), 0)
    last = iota((QROWS, N_LINE), 1)
    pick = ((first % QT == 0) & (first // (2 * QT) == last // HALF)).astype(F32)
    diag = iota((HALF, N_LINE), 1) % HALF == iota((HALF, N_LINE), 0)
    q_unit = own_queries[...].reshape(QROWS, D)
    _, _, _, pos_score = positive_scores(q_unit, gathered)
    pos_weight = jnp.sum(jnp.exp(pos_score), axis=0, keepdims=True)
    parts = []
    for q in range(QD):
        of_query = dot(jnp.where(mark == float(q), weight, 0.0), pick, ((1,), (0,)), EXACT)
        part = jnp.sum(jnp.where(diag, of_query, 0.0), axis=0, keepdims=True)
        own = jnp.sum(jnp.where(lane == q * QT, pos_weight, 0.0), axis=1, keepdims=True)
        parts.append(part + jnp.where(iota((1, N_LINE), 1) == me[0], own, 0.0))
    sums[...] = jnp.concatenate(parts, axis=0)

    def terms(step, carry):
        packed = (exps[step] * factor[pl.ds(step, 1), :]).astype(BF16)
        probs[step] = packed
        c_tiles = [rows[request(codes, line, slot)[2]] for line, slot in four(step)]
        grads = dot(spread(packed.astype(F32)), jnp.concatenate(c_tiles, axis=0), ((0,), (0,))).astype(BF16)
        back[step] = grads[0 : 2 * QT].reshape(2, QT, D)
        back[step + HALF] = grads[2 * QT :].reshape(2, QT, D)
        return carry

    lax.fori_loop(0, HALF, terms, 0, unroll=4)


def weigh(me, codes, weight_sum, weight_inv, sent, probs, own_queries, gathered, kept, off1, off2, off3, query_part, losses, acc, pos_acc):
    acc[...] = jnp.zeros_like(acc)

    def add(step, carry):
        spots = [(line,) + request(codes, line, slot) for line, slot in four(step)]
        grads = dot(spread(probs[step].astype(F32)), query_tiles(sent, step), ((1,), (0,)))
        for b, (line, _, q, row) in enumerate(spots):
            acc[row] += grads[b * PT : (b + 1) * PT] * weight_inv[q, line]
        return carry

    lax.fori_loop(0, HALF, add, 0, unroll=4)

    q_unit = own_queries[...].reshape(QROWS, D)
    cands, exp_scores, total, score = positive_scores(q_unit, gathered)
    lane = iota((1, QROWS), 1)
    own_sum = jnp.zeros((1, QROWS), F32)
    for q in range(QD):
        own_sum = jnp.where(lane // QT == q, weight_sum[q, me[0]], own_sum)
    own = (iota((BATCH, QROWS), 0) == me[1] * QD + iota((BATCH, QROWS), 1) // QT).astype(F32)
    score_grad = jnp.exp(score) / own_sum - own
    losses[...] = jnp.log(own_sum) - jnp.sum(score * own, axis=0, keepdims=True)
    weight_grad = (exp_scores * (score_grad / total)[:, None, :]).astype(BF16).reshape(BATCH * PT, QROWS)
    query_part[...] = dot(weight_grad, cands, ((0,), (0,)))
    pos_acc[...] = dot(weight_grad, q_unit, ((1,), (0,))).reshape(BATCH, PT, D)
    share = ROWS // GROUP
    for ahead, out in enumerate((kept, off1, off2, off3)):
        g = (me[1] + ahead) % GROUP
        out[0:QD] = pos_acc[pl.ds(g * QD, QD)].astype(out.dtype)
        out[QD:] = acc[pl.ds(g * share, share)].astype(out.dtype)


def collect(slots, weight_inv, me, query_part, arrived, out, tiles, sems):
    copies = [
        pltpu.make_async_copy(arrived.at[slots[p] // 2, slots[p] % 2], tiles.at[p], sems.at[p])
        for p in range(QD * NEG)
    ]
    for copy in copies:
        copy.start()
    for copy in copies:
        copy.wait()
    for q in range(QD):
        total = jnp.sum(tiles[q * NEG : (q + 1) * NEG].astype(F32), axis=0)
        out[q] = query_part[q * QT : (q + 1) * QT, :] + total * weight_inv[q, me[0]]


def per_device(queries, positives, passage_pool, negative_ids, storage_row):
    struct = jax.ShapeDtypeStruct
    me = jnp.stack([lax.axis_index(LINE), lax.axis_index("x")]).astype(I32)
    sent, q_unit, pos_unit, slots = call(
        prepare,
        (
            struct((N_LINE, SENT, D), BF16),
            struct((QD, QT, D), BF16),
            struct((QD, PT, D), BF16),
            struct((QD * NEG,), I32),
        ),
        [smem(), smem(), vmem(), vmem()],
        (vmem(), vmem(), vmem(), smem()),
        [pltpu.SMEM((N_LINE,), I32)],
    )(negative_ids, storage_row, queries, positives)

    asked = lax.all_to_all(sent, LINE, split_axis=0, concat_axis=0, tiled=True)
    gathered = lax.all_gather(pos_unit, "x", axis=0, tiled=True)
    codes = asked[:, 2 * QT : 2 * QT + 2, 0].astype(I32)

    back, probs, sums = call(
        serve,
        (
            struct((N_LINE, 2, QT, D), BF16),
            struct((HALF, PT, QROWS), BF16),
            struct((QD, N_LINE), F32),
        ),
        [smem(), smem(), vmem(), vmem(), vmem(), vmem()],
        (vmem(), vmem(), vmem()),
        [
            pltpu.VMEM((ROWS, PT, D), BF16),
            pltpu.VMEM((HALF, PT, QROWS), F32),
            pltpu.VMEM((HALF, QROWS), F32),
            pltpu.VMEM((HALF, QROWS), F32),
            pltpu.VMEM((HALF, QROWS), F32),
        ],
    )(me, codes, asked, passage_pool, q_unit, gathered)

    arrived = lax.all_to_all(back, LINE, split_axis=0, concat_axis=0, tiled=True)
    weight_sum = sums
    for axis in ("z", "y", "c"):
        weight_sum = jnp.sum(lax.all_gather(weight_sum, axis, axis=0), axis=0)
    weight_inv = 1.0 / weight_sum

    block = (QD + ROWS // GROUP, PT, D)
    kept, off1, off2, off3, query_part, losses = call(
        weigh,
        (
            struct(block, F32),
            struct(block, BF16),
            struct(block, BF16),
            struct(block, BF16),
            struct((QROWS, D), F32),
            struct((1, QROWS), F32),
        ),
        [smem(), smem(), smem(), smem(), vmem(), vmem(), vmem(), vmem()],
        (vmem(),) * 6,
        [pltpu.VMEM((ROWS, PT, D), F32), pltpu.VMEM((BATCH, PT, D), F32)],
    )(me, codes, weight_sum, weight_inv, asked, probs, q_unit, gathered)

    total = kept
    for ahead, part in ((1, off1), (2, off2), (3, off3)):
        moved = lax.ppermute(part, "x", [(g, (g + ahead) % GROUP) for g in range(GROUP)])
        total = total + moved.astype(F32)

    query_grad = call(
        collect,
        struct((QD, QT, D), F32),
        [smem(), smem(), smem(), vmem(), pl.BlockSpec(memory_space=pl.ANY)],
        vmem(),
        [pltpu.VMEM((QD * NEG, QT, D), BF16), pltpu.SemaphoreType.DMA((QD * NEG,))],
    )(slots, weight_inv, me, query_part, arrived)
    return losses.reshape(QD, QT)[:, 0], query_grad, total[:QD], total[QD:]


def solution(mesh):
    fine = Mesh(mesh.devices.reshape(N_Z, N_Y, N_C, GROUP), ("z", "y", "c", "x"))
    every, line = ("z", "y", "c", "x"), ("z", "y", "c")
    in_specs = (P(every), P(every), P(line), P(every), P())
    out_specs = (P(every), P(every), P(every), P(every))
    return jax.shard_map(per_device, mesh=fine, in_specs=in_specs, out_specs=out_specs, check_vma=False)
```

```python
import jax
import jax.numpy as jnp
from jax import lax
from jax.experimental import pallas as pl
from jax.experimental.pallas import tpu as pltpu
from jax.sharding import PartitionSpec as P

N_Z, N_Y, N_C, GROUP = 8, 8, 2, 4
N_DP = N_Z * N_Y * N_C
SPOTS = N_Z * N_Y
QD, QT, PT, D, NEG, ROWS = 4, 32, 64, 128, 7, 32
QROWS = QD * QT
SENT = QROWS + 8
BATCH = QD * GROUP
SLOTS = 4
VMEM = 48 * 1024 * 1024
F32, BF16, I32 = jnp.float32, jnp.bfloat16, jnp.int32
EXACT = lax.Precision.HIGHEST
EVERY = ("dp", "group")


def device(z, y, c, x):
    return ((z * N_Y + y) * N_C + c) * GROUP + x


def along(z_core):
    z_lines = [[device(z, y, z_core, x) for z in range(N_Z)] for y in range(N_Y) for x in range(GROUP)]
    y_lines = [[device(z, y, 1 - z_core, x) for y in range(N_Y)] for z in range(N_Z) for x in range(GROUP)]
    return z_lines + y_lines


def planes():
    first = [[device(z, y, 0, x) for z in range(N_Z) for y in range(N_Y)] for x in range(GROUP)]
    second = [[device(z, y, 1, x) for y in range(N_Y) for z in range(N_Z)] for x in range(GROUP)]
    return first + second


def exchange(blocks, groups):
    return lax.all_to_all(blocks, EVERY, split_axis=0, concat_axis=0, axis_index_groups=groups, tiled=True)


def call(body, out_shape, in_specs, out_specs, scratch=()):
    return pl.pallas_call(
        body,
        out_shape=out_shape,
        in_specs=in_specs,
        out_specs=out_specs,
        scratch_shapes=list(scratch),
        compiler_params=pltpu.CompilerParams(vmem_limit_bytes=VMEM),
    )


def vmem():
    return pl.BlockSpec(memory_space=pltpu.VMEM)


def smem():
    return pl.BlockSpec(memory_space=pltpu.SMEM)


def unit(values):
    wide = values.astype(F32)
    return (wide * lax.rsqrt(jnp.sum(wide * wide, axis=-1, keepdims=True) + 1e-06)).astype(BF16)


def iota(shape, dim):
    return lax.broadcasted_iota(I32, shape, dim)


def dot(a, b, dims, precision=None):
    return lax.dot_general(a, b, ((dims[0], dims[1]), ((), ())), precision=precision, preferred_element_type=F32)


def token_sum_matrix():
    return (iota((QROWS, QROWS), 0) // QT == iota((QROWS, QROWS), 1) // QT).astype(F32)


def prepare(ids, storage, queries, positives, sent, q_unit, pos_unit, count):
    tiles = unit(queries[...])
    q_unit[...] = tiles
    pos_unit[...] = unit(positives[...])
    homes = []
    for q in range(QD):
        for k in range(NEG):
            home = storage[ids[q, k]]
            owner = home // ROWS
            lane_of = (owner % N_C) * SPOTS + owner // N_C
            count[lane_of] = 0
            homes.append((lane_of, q * ROWS + home % ROWS + 1))
    lane = iota((8, N_DP), 1)
    sub = iota((8, N_DP), 0)
    codes = jnp.zeros((8, N_DP), F32)
    for lane_of, code in homes:
        rank = count[lane_of]
        count[lane_of] = rank + 1
        codes = jnp.where((lane == lane_of) & (sub == rank), code.astype(F32), codes)
    for copy in range(N_Y):
        sent[copy, 0:QROWS, :] = tiles.reshape(QROWS, D)
        sent[copy, QROWS:SENT, :] = codes.astype(BF16)


def normalize(values, out):
    out[...] = unit(values[...])


def positive_scores(q_unit, gathered):
    cands = gathered[...].reshape(BATCH * PT, D)
    exp_scores = jnp.exp(10.0 * dot(cands, q_unit, ((1,), (1,)))).reshape(BATCH, PT, QROWS)
    total = jnp.sum(exp_scores, axis=1)
    score = 0.1 * dot(jnp.log(total), token_sum_matrix(), ((1,), (0,)), EXACT)
    return cands, exp_scores, total, score


def positive_weight(q_tiles, gathered, out):
    score = positive_scores(q_tiles[...].reshape(QROWS, D), gathered)[3]
    out[...] = jnp.sum(jnp.exp(score), axis=0, keepdims=True)


def request(codes, source, slot):
    code = codes[source, slot]
    spot = jnp.maximum(code - 1, 0)
    return code > 0, spot // ROWS, spot % ROWS


def passages(codes, own_rows, other_rows, source):
    picked = [request(codes, source, slot)[2] for slot in range(SLOTS)]
    return jnp.concatenate([own_rows[picked[0]], own_rows[picked[1]], other_rows[picked[2]], other_rows[picked[3]]], axis=0)


def asking(codes, asked, source):
    picked = [request(codes, source, slot)[1] for slot in range(SLOTS)]
    return jnp.concatenate([asked[source, pl.ds(pl.multiple_of(q * QT, QT), QT), :] for q in picked], axis=0)


def spread(packed):
    block = iota((PT, QROWS), 1) // QT
    return jnp.concatenate([jnp.where(block == b, packed, 0.0).astype(BF16) for b in range(SLOTS)], axis=0)


def score(me, codes, asked, own_rows, other_rows, pos_weight, probs, sums, exps, totals, marks, factor):
    lane = iota((1, QROWS), 1)
    block = iota((PT, QROWS), 1) // QT

    def one(source, carry):
        mark = jnp.full((1, QROWS), -1.0, F32)
        for b in range(SLOTS):
            valid, q, _ = request(codes, source, b)
            mark = jnp.where((lane // QT == b) & valid, q.astype(F32), mark)
        full = dot(passages(codes, own_rows, other_rows, source), asking(codes, asked, source), ((1,), (1,)))
        packed = full[0:PT]
        for b in range(1, SLOTS):
            packed = jnp.where(block == b, full[b * PT : (b + 1) * PT], packed)
        exp_scores = jnp.exp(10.0 * packed)
        exps[source] = exp_scores
        totals[pl.ds(source, 1), :] = jnp.sum(exp_scores, axis=0, keepdims=True)
        marks[pl.ds(source, 1), :] = mark
        return carry

    lax.fori_loop(0, SPOTS, one, 0, unroll=4)

    total = totals[...]
    mark = marks[...]
    weight = jnp.exp(0.1 * dot(jnp.log(total), token_sum_matrix(), ((1,), (0,)), EXACT))
    weight = jnp.where(mark >= 0.0, weight, 0.0)
    factor[...] = weight / total
    first = iota((SPOTS, QROWS), 1) % QT == 0
    pad = jnp.zeros((QROWS - SPOTS, QROWS), F32)
    ones = jnp.ones((8, QROWS), F32)
    parts = []
    for q in range(QD):
        mine = jnp.where((mark == float(q)) & first, weight, 0.0)
        part = dot(ones, jnp.concatenate([mine, pad], axis=0), ((1,), (1,)), EXACT)[0:1]
        own = jnp.sum(jnp.where(lane == q * QT, pos_weight[...], 0.0), axis=1, keepdims=True)
        parts.append(part + jnp.where(lane == me[0], own, 0.0))
    sums[...] = jnp.broadcast_to(jnp.concatenate(parts, axis=0)[None], (SPOTS, QD, QROWS))

    def scale(source, carry):
        probs[source] = (exps[source] * factor[pl.ds(source, 1), :]).astype(BF16)
        return carry

    lax.fori_loop(0, SPOTS, scale, 0, unroll=4)


def terms(codes, own_rows, other_rows, probs, back):
    def one(source, carry):
        grads = dot(spread(probs[source].astype(F32)), passages(codes, own_rows, other_rows, source), ((0,), (0,)))
        picked = [request(codes, source, slot)[1] for slot in range(SLOTS)]
        for q in range(QD):
            total = jnp.zeros((QT, D), F32)
            for b in range(SLOTS):
                total += grads[b * QT : (b + 1) * QT] * (picked[b] == q).astype(F32)
            back[source, q * QT : (q + 1) * QT, :] = total.astype(BF16)
        return carry

    lax.fori_loop(0, SPOTS, one, 0, unroll=4)


def weigh(me, codes, weight_sum, weight_inv, asked, probs, q_tiles, gathered, own_grad, other_grad, pos_grad, query_part, losses, other_acc):
    own_grad[...] = jnp.zeros_like(own_grad)
    other_acc[...] = jnp.zeros_like(other_acc)

    def add(source, carry):
        grads = dot(spread(probs[source].astype(F32)), asking(codes, asked, source), ((1,), (0,)))
        for b in range(SLOTS):
            _, q, row = request(codes, source, b)
            acc = own_grad if b < 2 else other_acc
            acc[row] += grads[b * PT : (b + 1) * PT] * weight_inv[q, source]
        return carry

    lax.fori_loop(0, SPOTS, add, 0, unroll=4)
    other_grad[...] = other_acc[...].astype(BF16)

    q_unit = q_tiles[...].reshape(QROWS, D)
    cands, exp_scores, total, scores = positive_scores(q_unit, gathered)
    lane = iota((1, QROWS), 1)
    own_sum = jnp.zeros((1, QROWS), F32)
    for q in range(QD):
        own_sum = jnp.where(lane // QT == q, weight_sum[q, me[0]], own_sum)
    own = (iota((BATCH, QROWS), 0) == me[1] * QD + iota((BATCH, QROWS), 1) // QT).astype(F32)
    score_grad = jnp.exp(scores) / own_sum - own
    losses[...] = jnp.log(own_sum) - jnp.sum(scores * own, axis=0, keepdims=True)
    weight_grad = (exp_scores * (score_grad / total)[:, None, :]).astype(BF16).reshape(BATCH * PT, QROWS)
    query_part[...] = dot(weight_grad, cands, ((0,), (0,)))
    pos_grad[...] = dot(weight_grad, q_unit, ((1,), (0,))).reshape(BATCH, PT, D)


def split(me, own_grad, moved, pos_grad, kept, off1, off2, off3):
    share = ROWS // GROUP
    for ahead, out in enumerate((kept, off1, off2, off3)):
        g = (me[1] + ahead) % GROUP
        out[0:QD] = pos_grad[pl.ds(g * QD, QD)].astype(out.dtype)
        rows = pl.ds(g * share, share)
        out[QD:] = (own_grad[rows] + moved[rows].astype(F32)).astype(out.dtype)


def collect(weight_inv, me, query_part, arrived, out):
    def add(source, total):
        return total + arrived[source].astype(F32)

    total = lax.fori_loop(0, SPOTS, add, jnp.zeros((QROWS, D), F32), unroll=4)
    for q in range(QD):
        rows = slice(q * QT, (q + 1) * QT)
        out[q] = query_part[rows, :] + total[rows] * weight_inv[q, me[0]]


def per_device(queries, positives, passage_pool, negative_ids, storage_row):
    struct = jax.ShapeDtypeStruct
    holder = lax.axis_index("dp")
    z, y, core = holder // (N_Y * N_C), (holder // N_C) % N_Y, holder % N_C
    source = jnp.where(core == 0, z * N_Y + y, y * N_Z + z)
    me = jnp.stack([source, lax.axis_index("group")]).astype(I32)
    swap = [(h, h ^ 1) for h in range(N_DP)]
    tiles = struct((QD, QT, D), BF16)

    sent, q_unit, pos_unit = call(
        prepare,
        (struct((N_Y, SENT, D), BF16), tiles, struct((QD, PT, D), BF16)),
        [smem(), smem(), vmem(), vmem()],
        (vmem(), vmem(), vmem()),
        [pltpu.SMEM((N_DP,), I32)],
    )(negative_ids, storage_row, queries, positives)
    asked = exchange(sent, along(1))
    asked = exchange(jnp.broadcast_to(asked[None], (N_Z, N_Y, SENT, D)), along(0)).reshape(SPOTS, SENT, D)

    own_rows = call(normalize, struct((ROWS, PT, D), BF16), [vmem()], vmem())(passage_pool)
    other_rows = lax.ppermute(own_rows, "dp", swap)
    gathered = lax.all_gather(pos_unit, "group", axis=0, tiled=True)
    pos_weight = call(positive_weight, struct((1, QROWS), F32), [vmem(), vmem()], vmem())(q_unit, gathered)

    codes = asked[:, QROWS : QROWS + 2, :]
    codes = jnp.concatenate(
        [lax.dynamic_index_in_dim(codes, c * SPOTS + holder // N_C, 2, False) for c in (core, 1 - core)], axis=1
    ).astype(I32)

    probs, sums = call(
        score,
        (struct((SPOTS, PT, QROWS), BF16), struct((SPOTS, QD, QROWS), F32)),
        [smem(), smem(), vmem(), vmem(), vmem(), vmem()],
        (vmem(), vmem()),
        [
            pltpu.VMEM((SPOTS, PT, QROWS), F32),
            pltpu.VMEM((SPOTS, QROWS), F32),
            pltpu.VMEM((SPOTS, QROWS), F32),
            pltpu.VMEM((SPOTS, QROWS), F32),
        ],
    )(me, codes, asked, own_rows, other_rows, pos_weight)
    weight_sum = jnp.sum(exchange(sums, planes()), axis=0)
    weight_inv = 1.0 / weight_sum

    back = call(
        terms, struct((SPOTS, QROWS, D), BF16), [smem(), vmem(), vmem(), vmem()], vmem()
    )(codes, own_rows, other_rows, probs)
    arrived = exchange(back, planes())

    own_grad, other_grad, pos_grad, query_part, losses = call(
        weigh,
        (
            struct((ROWS, PT, D), F32),
            struct((ROWS, PT, D), BF16),
            struct((BATCH, PT, D), F32),
            struct((QROWS, D), F32),
            struct((1, QROWS), F32),
        ),
        [smem(), smem(), smem(), smem(), vmem(), vmem(), vmem(), vmem()],
        (vmem(),) * 5,
        [pltpu.VMEM((ROWS, PT, D), F32)],
    )(me, codes, weight_sum, weight_inv, asked, probs, q_unit, gathered)

    block = (QD + ROWS // GROUP, PT, D)
    kept, off1, off2, off3 = call(
        split,
        (struct(block, F32), struct(block, BF16), struct(block, BF16), struct(block, BF16)),
        [smem(), vmem(), vmem(), vmem()],
        (vmem(),) * 4,
    )(me, own_grad, lax.ppermute(other_grad, "dp", swap), pos_grad)
    total = kept
    for ahead, part in ((1, off1), (2, off2), (3, off3)):
        moved = lax.ppermute(part, "group", [(g, (g + ahead) % GROUP) for g in range(GROUP)])
        total = total + moved.astype(F32)

    query_grad = call(
        collect, struct((QD, QT, D), F32), [smem(), smem(), vmem(), vmem()], vmem()
    )(weight_inv, me, query_part, arrived)
    return losses.reshape(QD, QT)[:, 0], query_grad, total[:QD], total[QD:]


def solution(mesh):
    in_specs = (P(EVERY), P(EVERY), P("dp"), P(EVERY), P())
    out_specs = (P(EVERY), P(EVERY), P(EVERY), P(EVERY))
    return jax.shard_map(per_device, mesh=mesh, in_specs=in_specs, out_specs=out_specs, check_vma=False)
```

```python
import jax
import jax.numpy as jnp
from jax import lax
from jax.experimental import pallas as pl
from jax.experimental.pallas import tpu as pltpu
from jax.sharding import PartitionSpec as P

N_Z, N_Y, N_C, GROUP = 8, 8, 2, 4
N_DP = N_Z * N_Y * N_C
SPOTS = N_Z * N_Y
QD, QT, PT, D, NEG, ROWS = 4, 32, 64, 128, 7, 32
QROWS = QD * QT
SENT = QROWS + 8
BATCH = QD * GROUP
SLOTS = 4
VMEM = 48 * 1024 * 1024
F32, BF16, I32 = jnp.float32, jnp.bfloat16, jnp.int32
EXACT = lax.Precision.HIGHEST
EVERY = ("dp", "group")


def device(z, y, c, x):
    return ((z * N_Y + y) * N_C + c) * GROUP + x


def along(z_core):
    z_lines = [[device(z, y, z_core, x) for z in range(N_Z)] for y in range(N_Y) for x in range(GROUP)]
    y_lines = [[device(z, y, 1 - z_core, x) for y in range(N_Y)] for z in range(N_Z) for x in range(GROUP)]
    return z_lines + y_lines


def planes():
    first = [[device(z, y, 0, x) for z in range(N_Z) for y in range(N_Y)] for x in range(GROUP)]
    second = [[device(z, y, 1, x) for y in range(N_Y) for z in range(N_Z)] for x in range(GROUP)]
    return first + second


def exchange(blocks, groups):
    return lax.all_to_all(blocks, EVERY, split_axis=0, concat_axis=0, axis_index_groups=groups, tiled=True)


def call(body, out_shape, in_specs, out_specs, scratch=()):
    return pl.pallas_call(
        body,
        out_shape=out_shape,
        in_specs=in_specs,
        out_specs=out_specs,
        scratch_shapes=list(scratch),
        compiler_params=pltpu.CompilerParams(vmem_limit_bytes=VMEM),
    )


def vmem():
    return pl.BlockSpec(memory_space=pltpu.VMEM)


def smem():
    return pl.BlockSpec(memory_space=pltpu.SMEM)


def unit(values):
    wide = values.astype(F32)
    return (wide * lax.rsqrt(jnp.sum(wide * wide, axis=-1, keepdims=True) + 1e-06)).astype(BF16)


def iota(shape, dim):
    return lax.broadcasted_iota(I32, shape, dim)


def dot(a, b, dims, precision=None):
    return lax.dot_general(a, b, ((dims[0], dims[1]), ((), ())), precision=precision, preferred_element_type=F32)


def token_sum_matrix():
    return (iota((QROWS, QROWS), 0) // QT == iota((QROWS, QROWS), 1) // QT).astype(F32)


def prepare(ids, storage, queries, positives, sent, q_unit, pos_unit, count):
    tiles = unit(queries[...])
    q_unit[...] = tiles
    pos_unit[...] = unit(positives[...])
    homes = []
    for q in range(QD):
        for k in range(NEG):
            home = storage[ids[q, k]]
            owner = home // ROWS
            lane_of = (owner % N_C) * SPOTS + owner // N_C
            count[lane_of] = 0
            homes.append((lane_of, q * ROWS + home % ROWS + 1))
    lane = iota((8, N_DP), 1)
    sub = iota((8, N_DP), 0)
    codes = jnp.zeros((8, N_DP), F32)
    for lane_of, code in homes:
        rank = count[lane_of]
        count[lane_of] = rank + 1
        codes = jnp.where((lane == lane_of) & (sub == rank), code.astype(F32), codes)
    for copy in range(N_Y):
        sent[copy, 0:QROWS, :] = tiles.reshape(QROWS, D)
        sent[copy, QROWS:SENT, :] = codes.astype(BF16)


def normalize(values, out):
    out[...] = unit(values[...])


def positive_scores(q_unit, gathered):
    cands = gathered[...].reshape(BATCH * PT, D)
    exp_scores = jnp.exp(10.0 * dot(cands, q_unit, ((1,), (1,)))).reshape(BATCH, PT, QROWS)
    total = jnp.sum(exp_scores, axis=1)
    score = 0.1 * dot(jnp.log(total), token_sum_matrix(), ((1,), (0,)), EXACT)
    return cands, exp_scores, total, score


def positive_weight(q_tiles, gathered, out):
    score = positive_scores(q_tiles[...].reshape(QROWS, D), gathered)[3]
    out[...] = jnp.sum(jnp.exp(score), axis=0, keepdims=True)


def request(codes, source, slot):
    code = codes[slot // 2, source * 8 + slot % 2]
    spot = jnp.maximum(code - 1, 0)
    return code > 0, spot // ROWS, spot % ROWS


def passages(codes, own_rows, other_rows, source):
    picked = [request(codes, source, slot)[2] for slot in range(SLOTS)]
    return jnp.concatenate([own_rows[picked[0]], own_rows[picked[1]], other_rows[picked[2]], other_rows[picked[3]]], axis=0)


def asking(codes, asked, source):
    picked = [request(codes, source, slot)[1] for slot in range(SLOTS)]
    return jnp.concatenate([asked[source, pl.ds(pl.multiple_of(q * QT, QT), QT), :] for q in picked], axis=0)


def spread(packed):
    block = iota((PT, QROWS), 1) // QT
    return jnp.concatenate([jnp.where(block == b, packed, 0.0).astype(BF16) for b in range(SLOTS)], axis=0)


def read_codes(me, asked, codes, table, sem):
    rows = asked[:, QROWS:SENT, :].reshape(SPOTS * 8, N_DP)
    which = iota((8, N_DP), 0)
    spot = jnp.where(which == 0, me[2], me[3])
    pick = ((iota((8, N_DP), 1) == spot) & (which < 2)).astype(F32).astype(BF16)
    table[...] = dot(pick, rows, ((1,), (1,))).astype(I32)
    copy = pltpu.make_async_copy(table, codes, sem)
    copy.start()
    copy.wait()


def score(me, asked, own_rows, other_rows, pos_weight, probs, sums, codes, exps, totals, marks, factor, table, sem):
    read_codes(me, asked, codes, table, sem)
    lane = iota((1, QROWS), 1)
    block = iota((PT, QROWS), 1) // QT

    def one(source, carry):
        mark = jnp.full((1, QROWS), -1.0, F32)
        for b in range(SLOTS):
            valid, q, _ = request(codes, source, b)
            mark = jnp.where((lane // QT == b) & valid, q.astype(F32), mark)
        full = dot(passages(codes, own_rows, other_rows, source), asking(codes, asked, source), ((1,), (1,)))
        packed = full[0:PT]
        for b in range(1, SLOTS):
            packed = jnp.where(block == b, full[b * PT : (b + 1) * PT], packed)
        exp_scores = jnp.exp(10.0 * packed)
        exps[source] = exp_scores
        totals[pl.ds(source, 1), :] = jnp.sum(exp_scores, axis=0, keepdims=True)
        marks[pl.ds(source, 1), :] = mark
        return carry

    lax.fori_loop(0, SPOTS, one, 0, unroll=4)

    total = totals[...]
    mark = marks[...]
    weight = jnp.exp(0.1 * dot(jnp.log(total), token_sum_matrix(), ((1,), (0,)), EXACT))
    weight = jnp.where(mark >= 0.0, weight, 0.0)
    factor[...] = weight / total
    first = iota((SPOTS, QROWS), 1) % QT == 0
    pad = jnp.zeros((QROWS - SPOTS, QROWS), F32)
    ones = jnp.ones((8, QROWS), F32)
    parts = []
    for q in range(QD):
        mine = jnp.where((mark == float(q)) & first, weight, 0.0)
        part = dot(ones, jnp.concatenate([mine, pad], axis=0), ((1,), (1,)), EXACT)[0:1]
        own = jnp.sum(jnp.where(lane == q * QT, pos_weight[...], 0.0), axis=1, keepdims=True)
        parts.append(part + jnp.where(lane == me[0], own, 0.0))
    sums[...] = jnp.broadcast_to(jnp.concatenate(parts, axis=0)[None], (SPOTS, QD, QROWS))

    def scale(source, carry):
        probs[source] = (exps[source] * factor[pl.ds(source, 1), :]).astype(BF16)
        return carry

    lax.fori_loop(0, SPOTS, scale, 0, unroll=4)


def terms(codes, own_rows, other_rows, probs, back):
    def one(source, carry):
        grads = dot(spread(probs[source].astype(F32)), passages(codes, own_rows, other_rows, source), ((0,), (0,)))
        picked = [request(codes, source, slot)[1] for slot in range(SLOTS)]
        for q in range(QD):
            total = jnp.zeros((QT, D), F32)
            for b in range(SLOTS):
                total += grads[b * QT : (b + 1) * QT] * (picked[b] == q).astype(F32)
            back[source, q * QT : (q + 1) * QT, :] = total.astype(BF16)
        return carry

    lax.fori_loop(0, SPOTS, one, 0, unroll=4)


def weigh(me, codes, weight_sum, weight_inv, asked, probs, q_tiles, gathered, own_grad, other_grad, pos_grad, query_part, losses, other_acc):
    own_grad[...] = jnp.zeros_like(own_grad)
    other_acc[...] = jnp.zeros_like(other_acc)

    def add(source, carry):
        grads = dot(spread(probs[source].astype(F32)), asking(codes, asked, source), ((1,), (0,)))
        for b in range(SLOTS):
            _, q, row = request(codes, source, b)
            acc = own_grad if b < 2 else other_acc
            acc[row] += grads[b * PT : (b + 1) * PT] * weight_inv[q, source]
        return carry

    lax.fori_loop(0, SPOTS, add, 0, unroll=4)
    other_grad[...] = other_acc[...].astype(BF16)

    q_unit = q_tiles[...].reshape(QROWS, D)
    cands, exp_scores, total, scores = positive_scores(q_unit, gathered)
    lane = iota((1, QROWS), 1)
    own_sum = jnp.zeros((1, QROWS), F32)
    for q in range(QD):
        own_sum = jnp.where(lane // QT == q, weight_sum[q, me[0]], own_sum)
    own = (iota((BATCH, QROWS), 0) == me[1] * QD + iota((BATCH, QROWS), 1) // QT).astype(F32)
    score_grad = jnp.exp(scores) / own_sum - own
    losses[...] = jnp.log(own_sum) - jnp.sum(scores * own, axis=0, keepdims=True)
    weight_grad = (exp_scores * (score_grad / total)[:, None, :]).astype(BF16).reshape(BATCH * PT, QROWS)
    query_part[...] = dot(weight_grad, cands, ((0,), (0,)))
    pos_grad[...] = dot(weight_grad, q_unit, ((1,), (0,))).reshape(BATCH, PT, D)


def split(me, own_grad, moved, pos_grad, kept, off1, off2, off3):
    share = ROWS // GROUP
    for ahead, out in enumerate((kept, off1, off2, off3)):
        g = (me[1] + ahead) % GROUP
        out[0:QD] = pos_grad[pl.ds(g * QD, QD)].astype(out.dtype)
        rows = pl.ds(g * share, share)
        out[QD:] = (own_grad[rows] + moved[rows].astype(F32)).astype(out.dtype)


def add_blocks(arrived, out):
    out[...] = jnp.sum(arrived[...].astype(F32), axis=0).astype(BF16)


def collect(weight_inv, me, query_part, arrived, out):
    total = jnp.sum(arrived[...].astype(F32), axis=0)
    for q in range(QD):
        rows = slice(q * QT, (q + 1) * QT)
        out[q] = query_part[rows, :] + total[rows] * weight_inv[q, me[0]]


def per_device(queries, positives, passage_pool, negative_ids, storage_row):
    struct = jax.ShapeDtypeStruct
    holder = lax.axis_index("dp")
    z, y, core = holder // (N_Y * N_C), (holder // N_C) % N_Y, holder % N_C
    source = jnp.where(core == 0, z * N_Y + y, y * N_Z + z)
    spot = holder // N_C
    me = jnp.stack([source, lax.axis_index("group"), core * SPOTS + spot, (1 - core) * SPOTS + spot]).astype(I32)
    swap = [(h, h ^ 1) for h in range(N_DP)]
    tiles = struct((QD, QT, D), BF16)

    sent, q_unit, pos_unit = call(
        prepare,
        (struct((N_Y, SENT, D), BF16), tiles, struct((QD, PT, D), BF16)),
        [smem(), smem(), vmem(), vmem()],
        (vmem(), vmem(), vmem()),
        [pltpu.SMEM((N_DP,), I32)],
    )(negative_ids, storage_row, queries, positives)
    asked = exchange(sent, along(1))
    asked = exchange(jnp.broadcast_to(asked[None], (N_Z, N_Y, SENT, D)), along(0)).reshape(SPOTS, SENT, D)

    own_rows = call(normalize, struct((ROWS, PT, D), BF16), [vmem()], vmem())(passage_pool)
    other_rows = lax.ppermute(own_rows, "dp", swap)
    gathered = lax.all_gather(pos_unit, "group", axis=0, tiled=True)
    pos_weight = call(positive_weight, struct((1, QROWS), F32), [vmem(), vmem()], vmem())(q_unit, gathered)

    probs, sums, codes = call(
        score,
        (struct((SPOTS, PT, QROWS), BF16), struct((SPOTS, QD, QROWS), F32), struct((8, SPOTS * 8), I32)),
        [smem(), vmem(), vmem(), vmem(), vmem()],
        (vmem(), vmem(), smem()),
        [
            pltpu.VMEM((SPOTS, PT, QROWS), F32),
            pltpu.VMEM((SPOTS, QROWS), F32),
            pltpu.VMEM((SPOTS, QROWS), F32),
            pltpu.VMEM((SPOTS, QROWS), F32),
            pltpu.VMEM((8, SPOTS * 8), I32),
            pltpu.SemaphoreType.DMA,
        ],
    )(me, asked, own_rows, other_rows, pos_weight)
    weight_sum = jnp.sum(exchange(sums, planes()), axis=0)
    weight_inv = 1.0 / weight_sum

    back = call(
        terms, struct((SPOTS, QROWS, D), BF16), [smem(), vmem(), vmem(), vmem()], vmem()
    )(codes, own_rows, other_rows, probs)
    arrived = exchange(back.reshape(N_Z, N_Y, QROWS, D), along(0))
    arrived = call(add_blocks, struct((N_Y, QROWS, D), BF16), [vmem()], vmem())(arrived)
    arrived = exchange(arrived, along(1))

    own_grad, other_grad, pos_grad, query_part, losses = call(
        weigh,
        (
            struct((ROWS, PT, D), F32),
            struct((ROWS, PT, D), BF16),
            struct((BATCH, PT, D), F32),
            struct((QROWS, D), F32),
            struct((1, QROWS), F32),
        ),
        [smem(), smem(), smem(), smem(), vmem(), vmem(), vmem(), vmem()],
        (vmem(),) * 5,
        [pltpu.VMEM((ROWS, PT, D), F32)],
    )(me, codes, weight_sum, weight_inv, asked, probs, q_unit, gathered)

    block = (QD + ROWS // GROUP, PT, D)
    kept, off1, off2, off3 = call(
        split,
        (struct(block, F32), struct(block, BF16), struct(block, BF16), struct(block, BF16)),
        [smem(), vmem(), vmem(), vmem()],
        (vmem(),) * 4,
    )(me, own_grad, lax.ppermute(other_grad, "dp", swap), pos_grad)
    total = kept
    for ahead, part in ((1, off1), (2, off2), (3, off3)):
        moved = lax.ppermute(part, "group", [(g, (g + ahead) % GROUP) for g in range(GROUP)])
        total = total + moved.astype(F32)

    query_grad = call(
        collect, struct((QD, QT, D), F32), [smem(), smem(), vmem(), vmem()], vmem()
    )(weight_inv, me, query_part, arrived)
    return losses.reshape(QD, QT)[:, 0], query_grad, total[:QD], total[QD:]


def solution(mesh):
    in_specs = (P(EVERY), P(EVERY), P("dp"), P(EVERY), P())
    out_specs = (P(EVERY), P(EVERY), P(EVERY), P(EVERY))
    return jax.shard_map(per_device, mesh=mesh, in_specs=in_specs, out_specs=out_specs, check_vma=False)
```

```python
import jax
import jax.numpy as jnp
from jax import lax
from jax.experimental import pallas as pl
from jax.experimental.pallas import tpu as pltpu
from jax.sharding import PartitionSpec as P

N_Z, N_Y, N_C, GROUP = 8, 8, 2, 4
N_DP = N_Z * N_Y * N_C
SPOTS = N_Z * N_Y
QD, QT, PT, D, NEG, ROWS = 4, 32, 64, 128, 7, 32
QROWS = QD * QT
SENT = QROWS + 8
BATCH = QD * GROUP
SLOTS = 4
CHUNKS = 8
VMEM = 48 * 1024 * 1024
F32, BF16, I32 = jnp.float32, jnp.bfloat16, jnp.int32
EXACT = lax.Precision.HIGHEST
EVERY = ("dp", "group")


def device(z, y, c, x):
    return ((z * N_Y + y) * N_C + c) * GROUP + x


def along(z_core):
    z_lines = [[device(z, y, z_core, x) for z in range(N_Z)] for y in range(N_Y) for x in range(GROUP)]
    y_lines = [[device(z, y, 1 - z_core, x) for y in range(N_Y)] for z in range(N_Z) for x in range(GROUP)]
    return z_lines + y_lines


def planes():
    first = [[device(z, y, 0, x) for z in range(N_Z) for y in range(N_Y)] for x in range(GROUP)]
    second = [[device(z, y, 1, x) for y in range(N_Y) for z in range(N_Z)] for x in range(GROUP)]
    return first + second


def exchange(blocks, groups):
    return lax.all_to_all(blocks, EVERY, split_axis=0, concat_axis=0, axis_index_groups=groups, tiled=True)


def call(body, out_shape, in_specs, out_specs, scratch=()):
    return pl.pallas_call(
        body,
        out_shape=out_shape,
        in_specs=in_specs,
        out_specs=out_specs,
        scratch_shapes=list(scratch),
        compiler_params=pltpu.CompilerParams(vmem_limit_bytes=VMEM),
    )


def vmem():
    return pl.BlockSpec(memory_space=pltpu.VMEM)


def anywhere():
    return pl.BlockSpec(memory_space=pl.ANY)


def smem():
    return pl.BlockSpec(memory_space=pltpu.SMEM)


def unit(values):
    wide = values.astype(F32)
    return (wide * lax.rsqrt(jnp.sum(wide * wide, axis=-1, keepdims=True) + 1e-06)).astype(BF16)


def iota(shape, dim):
    return lax.broadcasted_iota(I32, shape, dim)


def dot(a, b, dims, precision=None):
    return lax.dot_general(a, b, ((dims[0], dims[1]), ((), ())), precision=precision, preferred_element_type=F32)


def token_sum_matrix():
    return (iota((QROWS, QROWS), 0) // QT == iota((QROWS, QROWS), 1) // QT).astype(F32)


def fetch(pairs, sems):
    copies = [pltpu.make_async_copy(src, dst, sems.at[i]) for i, (src, dst) in enumerate(pairs)]
    for copy in copies:
        copy.start()
    return copies


def prepare(ids_in, storage_in, queries_in, positives_in, sent, q_unit, pos_unit, ids, storage, queries, positives, sems, count):
    pairs = [(storage_in, storage), (ids_in, ids), (queries_in, queries), (positives_in, positives)]
    for copy in fetch(pairs, sems):
        copy.wait()
    tiles = unit(queries[...])
    q_unit[...] = tiles
    pos_unit[...] = unit(positives[...])
    homes = []
    for q in range(QD):
        for k in range(NEG):
            home = storage[ids[q, k]]
            owner = home // ROWS
            lane_of = (owner % N_C) * SPOTS + owner // N_C
            count[lane_of] = 0
            homes.append((lane_of, q * ROWS + home % ROWS + 1))
    lane = iota((8, N_DP), 1)
    sub = iota((8, N_DP), 0)
    codes = jnp.zeros((8, N_DP), F32)
    for lane_of, code in homes:
        rank = count[lane_of]
        count[lane_of] = rank + 1
        codes = jnp.where((lane == lane_of) & (sub == rank), code.astype(F32), codes)
    for copy in range(N_Y):
        sent[copy, 0:QROWS, :] = tiles.reshape(QROWS, D)
        sent[copy, QROWS:SENT, :] = codes.astype(BF16)


def normalize(values, out):
    out[...] = unit(values[...])


def positive_scores(q_unit, gathered):
    cands = gathered[...].reshape(BATCH * PT, D)
    exp_scores = jnp.exp(10.0 * dot(cands, q_unit, ((1,), (1,)))).reshape(BATCH, PT, QROWS)
    total = jnp.sum(exp_scores, axis=1)
    score = 0.1 * dot(jnp.log(total), token_sum_matrix(), ((1,), (0,)), EXACT)
    return cands, exp_scores, total, score


def positive_weight(q_tiles, gathered, out):
    score = positive_scores(q_tiles[...].reshape(QROWS, D), gathered)[3]
    out[...] = jnp.sum(jnp.exp(score), axis=0, keepdims=True)


def request(codes, source, slot):
    code = codes[slot // 2, source * 8 + slot % 2]
    spot = jnp.maximum(code - 1, 0)
    return code > 0, spot // ROWS, spot % ROWS


def passages(codes, own_rows, other_rows, source):
    picked = [request(codes, source, slot)[2] for slot in range(SLOTS)]
    return jnp.concatenate([own_rows[picked[0]], own_rows[picked[1]], other_rows[picked[2]], other_rows[picked[3]]], axis=0)


def asking(codes, asked, source):
    picked = [request(codes, source, slot)[1] for slot in range(SLOTS)]
    return jnp.concatenate([asked[source, pl.ds(pl.multiple_of(q * QT, QT), QT), :] for q in picked], axis=0)


def spread(packed):
    block = iota((PT, QROWS), 1) // QT
    return jnp.concatenate([jnp.where(block == b, packed, 0.0).astype(BF16) for b in range(SLOTS)], axis=0)


def read_codes(me, asked, codes, table, sem):
    rows = asked[:, QROWS:SENT, :].reshape(SPOTS * 8, N_DP)
    which = iota((8, N_DP), 0)
    spot = jnp.where(which == 0, me[2], me[3])
    pick = ((iota((8, N_DP), 1) == spot) & (which < 2)).astype(F32).astype(BF16)
    table[...] = dot(pick, rows, ((1,), (1,))).astype(I32)
    copy = pltpu.make_async_copy(table, codes, sem)
    copy.start()
    copy.wait()


def score(me, asked, own_rows, other_rows, pos_weight, exps_out, factor, sums, codes, exps, totals, marks, table, sems):
    read_codes(me, asked, codes, table, sems.at[CHUNKS])
    lane = iota((1, QROWS), 1)
    block = iota((PT, QROWS), 1) // QT

    def one(source, carry):
        mark = jnp.full((1, QROWS), -1.0, F32)
        for b in range(SLOTS):
            valid, q, _ = request(codes, source, b)
            mark = jnp.where((lane // QT == b) & valid, q.astype(F32), mark)
        full = dot(passages(codes, own_rows, other_rows, source), asking(codes, asked, source), ((1,), (1,)))
        packed = full[0:PT]
        for b in range(1, SLOTS):
            packed = jnp.where(block == b, full[b * PT : (b + 1) * PT], packed)
        exp_scores = jnp.exp(10.0 * packed)
        exps[source] = exp_scores
        totals[pl.ds(source, 1), :] = jnp.sum(exp_scores, axis=0, keepdims=True)
        marks[pl.ds(source, 1), :] = mark
        return carry

    size = SPOTS // CHUNKS
    copies = []
    for chunk in range(CHUNKS):
        lax.fori_loop(chunk * size, (chunk + 1) * size, one, 0, unroll=4)
        part = pl.ds(chunk * size, size)
        copies.append(pltpu.make_async_copy(exps.at[part], exps_out.at[part], sems.at[chunk]))
        copies[-1].start()

    total = totals[...]
    mark = marks[...]
    weight = jnp.exp(0.1 * dot(jnp.log(total), token_sum_matrix(), ((1,), (0,)), EXACT))
    weight = jnp.where(mark >= 0.0, weight, 0.0)
    factor[...] = weight / total
    first = iota((SPOTS, QROWS), 1) % QT == 0
    pad = jnp.zeros((QROWS - SPOTS, QROWS), F32)
    ones = jnp.ones((8, QROWS), F32)
    parts = []
    for q in range(QD):
        mine = jnp.where((mark == float(q)) & first, weight, 0.0)
        part = dot(ones, jnp.concatenate([mine, pad], axis=0), ((1,), (1,)), EXACT)[0:1]
        own = jnp.sum(jnp.where(lane == q * QT, pos_weight[...], 0.0), axis=1, keepdims=True)
        parts.append(part + jnp.where(lane == me[0], own, 0.0))
    sums[...] = jnp.broadcast_to(jnp.concatenate(parts, axis=0)[None], (SPOTS, QD, QROWS))
    for copy in copies:
        copy.wait()


def terms(codes, own_rows, other_rows, exps, factor, probs, back):
    def one(source, carry):
        packed = exps[source] * factor[pl.ds(source, 1), :]
        probs[source] = packed.astype(BF16)
        grads = dot(spread(packed), passages(codes, own_rows, other_rows, source), ((0,), (0,)))
        picked = [request(codes, source, slot)[1] for slot in range(SLOTS)]
        for q in range(QD):
            total = jnp.zeros((QT, D), F32)
            for b in range(SLOTS):
                total += grads[b * QT : (b + 1) * QT] * (picked[b] == q).astype(F32)
            back[source, q * QT : (q + 1) * QT, :] = total.astype(BF16)
        return carry

    lax.fori_loop(0, SPOTS, one, 0, unroll=4)


def weigh(
    me, codes, sums, asked, probs, q_in, gathered_in, own_grad, other_grad, pos_grad, query_part, losses, weight_inv,
    other_acc, inverse, q_tiles, gathered, sems,
):
    later = fetch([(q_in, q_tiles), (gathered_in, gathered)], sems)
    weight_sum = jnp.sum(sums[...], axis=0)
    inverse[...] = jnp.zeros_like(inverse)
    inverse[0:QD] = 1.0 / weight_sum
    copy = pltpu.make_async_copy(inverse, weight_inv, sems.at[2])
    copy.start()
    own_grad[...] = jnp.zeros_like(own_grad)
    other_acc[...] = jnp.zeros_like(other_acc)
    copy.wait()

    def add(source, carry):
        grads = dot(spread(probs[source].astype(F32)), asking(codes, asked, source), ((1,), (0,)))
        for b in range(SLOTS):
            _, q, row = request(codes, source, b)
            acc = own_grad if b < 2 else other_acc
            acc[row] += grads[b * PT : (b + 1) * PT] * weight_inv[q, source]
        return carry

    lax.fori_loop(0, SPOTS, add, 0, unroll=4)
    other_grad[...] = other_acc[...].astype(BF16)

    for copy in later:
        copy.wait()
    q_unit = q_tiles[...].reshape(QROWS, D)
    cands, exp_scores, total, scores = positive_scores(q_unit, gathered)
    lane = iota((1, QROWS), 1)
    mine = jnp.sum(jnp.where(lane == me[0], weight_sum, 0.0), axis=1, keepdims=True)
    own_sum = jnp.zeros((1, QROWS), F32)
    for q in range(QD):
        own_sum = jnp.where(lane // QT == q, mine[q : q + 1], own_sum)
    own = (iota((BATCH, QROWS), 0) == me[1] * QD + iota((BATCH, QROWS), 1) // QT).astype(F32)
    score_grad = jnp.exp(scores) / own_sum - own
    losses[...] = jnp.log(own_sum) - jnp.sum(scores * own, axis=0, keepdims=True)
    weight_grad = (exp_scores * (score_grad / total)[:, None, :]).astype(BF16).reshape(BATCH * PT, QROWS)
    query_part[...] = dot(weight_grad, cands, ((0,), (0,)))
    pos_grad[...] = dot(weight_grad, q_unit, ((1,), (0,))).reshape(BATCH, PT, D)


def split(me, own_grad, moved, pos_grad, kept, off1, off2, off3):
    share = ROWS // GROUP
    for ahead, out in enumerate((kept, off1, off2, off3)):
        g = (me[1] + ahead) % GROUP
        out[0:QD] = pos_grad[pl.ds(g * QD, QD)].astype(out.dtype)
        rows = pl.ds(g * share, share)
        out[QD:] = (own_grad[rows] + moved[rows].astype(F32)).astype(out.dtype)


def add_blocks(arrived, after, out):
    del after
    out[...] = jnp.sum(arrived[...].astype(F32), axis=0).astype(BF16)


def collect(weight_inv, me, query_part, arrived, out):
    total = jnp.sum(arrived[...].astype(F32), axis=0)
    for q in range(QD):
        rows = slice(q * QT, (q + 1) * QT)
        out[q] = query_part[rows, :] + total[rows] * weight_inv[q, me[0]]


def per_device(queries, positives, passage_pool, negative_ids, storage_row):
    struct = jax.ShapeDtypeStruct
    holder = lax.axis_index("dp")
    z, y, core = holder // (N_Y * N_C), (holder // N_C) % N_Y, holder % N_C
    source = jnp.where(core == 0, z * N_Y + y, y * N_Z + z)
    spot = holder // N_C
    me = jnp.stack([source, lax.axis_index("group"), core * SPOTS + spot, (1 - core) * SPOTS + spot]).astype(I32)
    swap = [(h, h ^ 1) for h in range(N_DP)]
    tiles = struct((QD, QT, D), BF16)

    sent, q_unit, pos_unit = call(
        prepare,
        (struct((N_Y, SENT, D), BF16), tiles, struct((QD, PT, D), BF16)),
        [anywhere()] * 4,
        (vmem(), vmem(), vmem()),
        [
            pltpu.SMEM(negative_ids.shape, I32),
            pltpu.SMEM(storage_row.shape, I32),
            pltpu.VMEM((QD, QT, D), BF16),
            pltpu.VMEM((QD, PT, D), BF16),
            pltpu.SemaphoreType.DMA((4,)),
            pltpu.SMEM((N_DP,), I32),
        ],
    )(negative_ids, storage_row, queries, positives)
    asked = exchange(sent, along(1))
    asked = exchange(jnp.broadcast_to(asked[None], (N_Z, N_Y, SENT, D)), along(0)).reshape(SPOTS, SENT, D)

    own_rows = call(normalize, struct((ROWS, PT, D), BF16), [vmem()], vmem())(passage_pool)
    other_rows = lax.ppermute(own_rows, "dp", swap)
    gathered = lax.all_gather(pos_unit, "group", axis=0, tiled=True)
    pos_weight = call(positive_weight, struct((1, QROWS), F32), [vmem(), vmem()], vmem())(q_unit, gathered)

    exps, factor, sums, codes = call(
        score,
        (
            struct((SPOTS, PT, QROWS), F32),
            struct((SPOTS, QROWS), F32),
            struct((SPOTS, QD, QROWS), F32),
            struct((8, SPOTS * 8), I32),
        ),
        [smem(), vmem(), vmem(), vmem(), vmem()],
        (anywhere(), vmem(), vmem(), smem()),
        [
            pltpu.VMEM((SPOTS, PT, QROWS), F32),
            pltpu.VMEM((SPOTS, QROWS), F32),
            pltpu.VMEM((SPOTS, QROWS), F32),
            pltpu.VMEM((8, SPOTS * 8), I32),
            pltpu.SemaphoreType.DMA((CHUNKS + 1,)),
        ],
    )(me, asked, own_rows, other_rows, pos_weight)
    sums = exchange(sums, planes())

    probs, back = call(
        terms,
        (struct((SPOTS, PT, QROWS), BF16), struct((SPOTS, QROWS, D), BF16)),
        [smem()] + [vmem()] * 4,
        (vmem(), vmem()),
    )(codes, own_rows, other_rows, exps, factor)
    arrived = exchange(back.reshape(N_Z, N_Y, QROWS, D), along(0))

    own_grad, other_grad, pos_grad, query_part, losses, weight_inv = call(
        weigh,
        (
            struct((ROWS, PT, D), F32),
            struct((ROWS, PT, D), BF16),
            struct((BATCH, PT, D), F32),
            struct((QROWS, D), F32),
            struct((1, QROWS), F32),
            struct((8, QROWS), F32),
        ),
        [smem(), smem(), vmem(), vmem(), vmem(), anywhere(), anywhere()],
        (vmem(),) * 5 + (smem(),),
        [
            pltpu.VMEM((ROWS, PT, D), F32),
            pltpu.VMEM((8, QROWS), F32),
            pltpu.VMEM((QD, QT, D), BF16),
            pltpu.VMEM((BATCH, PT, D), BF16),
            pltpu.SemaphoreType.DMA((3,)),
        ],
    )(me, codes, sums, asked, probs, q_unit, gathered)

    block = (QD + ROWS // GROUP, PT, D)
    kept, off1, off2, off3 = call(
        split,
        (struct(block, F32), struct(block, BF16), struct(block, BF16), struct(block, BF16)),
        [smem(), vmem(), vmem(), vmem()],
        (vmem(),) * 4,
    )(me, own_grad, lax.ppermute(other_grad, "dp", swap), pos_grad)
    total = kept
    for ahead, part in ((1, off1), (2, off2), (3, off3)):
        moved = lax.ppermute(part, "group", [(g, (g + ahead) % GROUP) for g in range(GROUP)])
        total = total + moved.astype(F32)

    arrived = call(add_blocks, struct((N_Y, QROWS, D), BF16), [vmem(), anywhere()], vmem())(arrived, total)
    arrived = exchange(arrived, along(1))
    query_grad = call(
        collect, struct((QD, QT, D), F32), [smem(), smem(), vmem(), vmem()], vmem()
    )(weight_inv, me, query_part, arrived)
    return losses.reshape(QD, QT)[:, 0], query_grad, total[:QD], total[QD:]


def solution(mesh):
    in_specs = (P(EVERY), P(EVERY), P("dp"), P(EVERY), P())
    out_specs = (P(EVERY), P(EVERY), P(EVERY), P(EVERY))
    return jax.shard_map(per_device, mesh=mesh, in_specs=in_specs, out_specs=out_specs, check_vma=False)
```

```python
import jax
import jax.numpy as jnp
from jax import lax
from jax.experimental import pallas as pl
from jax.experimental.pallas import tpu as pltpu
from jax.sharding import PartitionSpec as P

N_Z, N_Y, N_C, GROUP = 8, 8, 2, 4
N_DP = N_Z * N_Y * N_C
SPOTS = N_Z * N_Y
QD, QT, PT, D, NEG, ROWS = 4, 32, 64, 128, 7, 32
QROWS = QD * QT
SENT = QROWS + 8
BATCH = QD * GROUP
SLOTS = 4
VMEM = 16 * 1024 * 1024
F32, BF16, I32 = jnp.float32, jnp.bfloat16, jnp.int32
EXACT = lax.Precision.HIGHEST
EVERY = ("dp", "group")


def device(z, y, c, x):
    return ((z * N_Y + y) * N_C + c) * GROUP + x


def along(z_core):
    z_lines = [[device(z, y, z_core, x) for z in range(N_Z)] for y in range(N_Y) for x in range(GROUP)]
    y_lines = [[device(z, y, 1 - z_core, x) for y in range(N_Y)] for z in range(N_Z) for x in range(GROUP)]
    return z_lines + y_lines


def planes():
    first = [[device(z, y, 0, x) for z in range(N_Z) for y in range(N_Y)] for x in range(GROUP)]
    second = [[device(z, y, 1, x) for y in range(N_Y) for z in range(N_Z)] for x in range(GROUP)]
    return first + second


def exchange(blocks, groups):
    return lax.all_to_all(blocks, EVERY, split_axis=0, concat_axis=0, axis_index_groups=groups, tiled=True)


def call(body, out_shape, in_specs, out_specs, scratch=()):
    return pl.pallas_call(
        body,
        out_shape=out_shape,
        in_specs=in_specs,
        out_specs=out_specs,
        scratch_shapes=list(scratch),
        compiler_params=pltpu.CompilerParams(vmem_limit_bytes=VMEM),
    )


def vmem():
    return pl.BlockSpec(memory_space=pltpu.VMEM)


def anywhere():
    return pl.BlockSpec(memory_space=pl.ANY)


def hbm():
    return pl.BlockSpec(memory_space=pltpu.HBM)


def smem():
    return pl.BlockSpec(memory_space=pltpu.SMEM)


def unit(values):
    wide = values.astype(F32)
    return (wide * lax.rsqrt(jnp.sum(wide * wide, axis=-1, keepdims=True) + 1e-06)).astype(BF16)


def iota(shape, dim):
    return lax.broadcasted_iota(I32, shape, dim)


def dot(a, b, dims, precision=None):
    return lax.dot_general(a, b, ((dims[0], dims[1]), ((), ())), precision=precision, preferred_element_type=F32)


def token_sum_matrix():
    return (iota((QROWS, QROWS), 0) // QT == iota((QROWS, QROWS), 1) // QT).astype(F32)


def fetch(pairs, sems):
    copies = [pltpu.make_async_copy(src, dst, sems.at[i]) for i, (src, dst) in enumerate(pairs)]
    for copy in copies:
        copy.start()
    return copies


def prepare(ids_in, storage_in, queries_in, sent, q_unit, ids, storage, queries, sems, count):
    pairs = [(storage_in, storage), (ids_in, ids), (queries_in, queries)]
    for copy in fetch(pairs, sems):
        copy.wait()
    tiles = unit(queries[...])
    q_unit[...] = tiles
    homes = []
    for q in range(QD):
        for k in range(NEG):
            home = storage[ids[q, k]]
            owner = home // ROWS
            lane_of = (owner % N_C) * SPOTS + owner // N_C
            count[lane_of] = 0
            homes.append((lane_of, q * ROWS + home % ROWS + 1))
    lane = iota((8, N_DP), 1)
    sub = iota((8, N_DP), 0)
    codes = jnp.zeros((8, N_DP), F32)
    for lane_of, code in homes:
        rank = count[lane_of]
        count[lane_of] = rank + 1
        codes = jnp.where((lane == lane_of) & (sub == rank), code.astype(F32), codes)
    for copy in range(N_Y):
        sent[copy, 0:QROWS, :] = tiles.reshape(QROWS, D)
        sent[copy, QROWS:SENT, :] = codes.astype(BF16)


def normalize(values, out):
    out[...] = unit(values[...])


def positive_scores(q_unit, gathered):
    cands = gathered[...].reshape(BATCH * PT, D)
    exp_scores = jnp.exp(10.0 * dot(cands, q_unit, ((1,), (1,)))).reshape(BATCH, PT, QROWS)
    total = jnp.sum(exp_scores, axis=1)
    score = 0.1 * dot(jnp.log(total), token_sum_matrix(), ((1,), (0,)), EXACT)
    return cands, exp_scores, total, score


def positive_weight(q_tiles, positives, gathered, out):
    gathered[...] = unit(positives[...])
    score = positive_scores(q_tiles[...].reshape(QROWS, D), gathered)[3]
    out[...] = jnp.sum(jnp.exp(score), axis=0, keepdims=True)


def request(codes, source, slot):
    code = codes[slot // 2, source * 8 + slot % 2]
    spot = jnp.maximum(code - 1, 0)
    return code > 0, spot // ROWS, spot % ROWS


def passages(codes, own_rows, other_rows, source):
    picked = [request(codes, source, slot)[2] for slot in range(SLOTS)]
    return jnp.concatenate([own_rows[picked[0]], own_rows[picked[1]], other_rows[picked[2]], other_rows[picked[3]]], axis=0)


def asking(codes, asked, source):
    picked = [request(codes, source, slot)[1] for slot in range(SLOTS)]
    return jnp.concatenate([asked[source, pl.ds(pl.multiple_of(q * QT, QT), QT), :] for q in picked], axis=0)


def spread(packed):
    block = iota((PT, QROWS), 1) // QT
    return jnp.concatenate([jnp.where(block == b, packed, 0.0).astype(BF16) for b in range(SLOTS)], axis=0)


def read_codes(me, asked, table, codes, sem):
    rows = asked[:, QROWS:SENT, :].reshape(SPOTS * 8, N_DP)
    which = iota((8, N_DP), 0)
    spot = jnp.where(which == 0, me[2], me[3])
    pick = ((iota((8, N_DP), 1) == spot) & (which < 2)).astype(F32).astype(BF16)
    table[...] = dot(pick, rows, ((1,), (1,))).astype(I32)
    copy = pltpu.make_async_copy(table, codes, sem)
    copy.start()
    copy.wait()


def exponentials(codes, asked, own_rows, other_rows, source):
    block = iota((PT, QROWS), 1) // QT
    full = dot(passages(codes, own_rows, other_rows, source), asking(codes, asked, source), ((1,), (1,)))
    packed = full[0:PT]
    for b in range(1, SLOTS):
        packed = jnp.where(block == b, full[b * PT : (b + 1) * PT], packed)
    return jnp.exp(10.0 * packed)


def score(me, asked, own_rows, other_rows, pos_weight, factor, sums, table, totals, marks, codes, sem):
    read_codes(me, asked, table, codes, sem)
    lane = iota((1, QROWS), 1)

    def one(source, carry):
        mark = jnp.full((1, QROWS), -1.0, F32)
        for b in range(SLOTS):
            valid, q, _ = request(codes, source, b)
            mark = jnp.where((lane // QT == b) & valid, q.astype(F32), mark)
        exp_scores = exponentials(codes, asked, own_rows, other_rows, source)
        totals[pl.ds(source, 1), :] = jnp.sum(exp_scores, axis=0, keepdims=True)
        marks[pl.ds(source, 1), :] = mark
        return carry

    size = 8
    for chunk in range(SPOTS // size):
        lax.fori_loop(chunk * size, (chunk + 1) * size, one, 0, unroll=size)

    total = totals[...]
    mark = marks[...]
    weight = jnp.exp(0.1 * dot(jnp.log(total), token_sum_matrix(), ((1,), (0,)), EXACT))
    weight = jnp.where(mark >= 0.0, weight, 0.0)
    factor[...] = weight / total
    first = iota((SPOTS, QROWS), 1) % QT == 0
    pad = jnp.zeros((QROWS - SPOTS, QROWS), F32)
    ones = jnp.ones((8, QROWS), F32)
    parts = []
    for q in range(QD):
        mine = jnp.where((mark == float(q)) & first, weight, 0.0)
        part = dot(ones, jnp.concatenate([mine, pad], axis=0), ((1,), (1,)), EXACT)[0:1]
        own = jnp.sum(jnp.where(lane == q * QT, pos_weight[...], 0.0), axis=1, keepdims=True)
        parts.append(part + jnp.where(lane == me[0], own, 0.0))
    sums[...] = jnp.broadcast_to(jnp.concatenate(parts, axis=0)[None], (SPOTS, QD, QROWS))


def terms(codes, asked, own_rows, other_rows, factor, probs, back):
    def one(source, carry):
        packed = exponentials(codes, asked, own_rows, other_rows, source) * factor[pl.ds(source, 1), :]
        probs[source] = packed.astype(BF16)
        grads = dot(spread(packed), passages(codes, own_rows, other_rows, source), ((0,), (0,)))
        picked = [request(codes, source, slot)[1] for slot in range(SLOTS)]
        for q in range(QD):
            total = jnp.zeros((QT, D), F32)
            for b in range(SLOTS):
                total += grads[b * QT : (b + 1) * QT] * (picked[b] == q).astype(F32)
            back[source, q * QT : (q + 1) * QT, :] = total.astype(BF16)
        return carry

    lax.fori_loop(0, SPOTS, one, 0, unroll=8)


def weigh(
    me, codes, sums, asked, probs, q_in, gathered_in, own_grad, other_grad, pos_grad, query_part, losses, weight_inv,
    other_acc, inverse, q_tiles, gathered, sems,
):
    later = fetch([(q_in, q_tiles), (gathered_in, gathered)], sems)
    weight_sum = jnp.sum(sums[...], axis=0)
    inverse[...] = jnp.zeros_like(inverse)
    inverse[0:QD] = 1.0 / weight_sum
    copy = pltpu.make_async_copy(inverse, weight_inv, sems.at[2])
    copy.start()
    own_grad[...] = jnp.zeros_like(own_grad)
    other_acc[...] = jnp.zeros_like(other_acc)
    copy.wait()

    def add(source, carry):
        grads = dot(spread(probs[source].astype(F32)), asking(codes, asked, source), ((1,), (0,)))
        for b in range(SLOTS):
            _, q, row = request(codes, source, b)
            acc = own_grad if b < 2 else other_acc
            acc[row] += grads[b * PT : (b + 1) * PT] * weight_inv[q, source]
        return carry

    lax.fori_loop(0, SPOTS, add, 0, unroll=8)
    other_grad[...] = other_acc[...].astype(BF16)

    for copy in later:
        copy.wait()
    q_unit = q_tiles[...].reshape(QROWS, D)
    cands, exp_scores, total, scores = positive_scores(q_unit, gathered)
    lane = iota((1, QROWS), 1)
    mine = jnp.sum(jnp.where(lane == me[0], weight_sum, 0.0), axis=1, keepdims=True)
    own_sum = jnp.zeros((1, QROWS), F32)
    for q in range(QD):
        own_sum = jnp.where(lane // QT == q, mine[q : q + 1], own_sum)
    own = (iota((BATCH, QROWS), 0) == me[1] * QD + iota((BATCH, QROWS), 1) // QT).astype(F32)
    score_grad = jnp.exp(scores) / own_sum - own
    losses[...] = jnp.log(own_sum) - jnp.sum(scores * own, axis=0, keepdims=True)
    weight_grad = (exp_scores * (score_grad / total)[:, None, :]).astype(BF16).reshape(BATCH * PT, QROWS)
    query_part[...] = dot(weight_grad, cands, ((0,), (0,)))
    pos_grad[...] = dot(weight_grad, q_unit, ((1,), (0,))).reshape(BATCH, PT, D)


def split(me, own_grad, moved, pos_grad, kept, off1, off2, off3):
    share = ROWS // GROUP
    for ahead, out in enumerate((kept, off1, off2, off3)):
        g = (me[1] + ahead) % GROUP
        out[0:QD] = pos_grad[pl.ds(g * QD, QD)].astype(out.dtype)
        rows = pl.ds(g * share, share)
        out[QD:] = (own_grad[rows] + moved[rows].astype(F32)).astype(out.dtype)


def add_blocks(arrived, after, out, blocks, sems):
    del after
    pairs = [(arrived.at[:, pl.ds(2 * i, 2)], blocks.at[:, pl.ds(2 * i, 2)]) for i in range(N_Y // 2)]
    for i, copy in enumerate(fetch(pairs, sems)):
        copy.wait()
        part = slice(2 * i, 2 * i + 2)
        out[part] = jnp.sum(blocks[:, part].astype(F32), axis=0).astype(BF16)


def collect(weight_inv, me, query_part, arrived, out):
    total = jnp.sum(arrived[...].astype(F32), axis=0)
    for q in range(QD):
        rows = slice(q * QT, (q + 1) * QT)
        out[q] = query_part[rows, :] + total[rows] * weight_inv[q, me[0]]


def per_device(queries, positives, passage_pool, negative_ids, storage_row):
    struct = jax.ShapeDtypeStruct
    holder = lax.axis_index("dp")
    z, y, core = holder // (N_Y * N_C), (holder // N_C) % N_Y, holder % N_C
    source = jnp.where(core == 0, z * N_Y + y, y * N_Z + z)
    spot = holder // N_C
    me = jnp.stack([source, lax.axis_index("group"), core * SPOTS + spot, (1 - core) * SPOTS + spot]).astype(I32)
    swap = [(h, h ^ 1) for h in range(N_DP)]
    tiles = struct((QD, QT, D), BF16)

    sent, q_unit = call(
        prepare,
        (struct((N_Y, SENT, D), BF16), tiles),
        [hbm()] * 3,
        (vmem(), vmem()),
        [
            pltpu.SMEM(negative_ids.shape, I32),
            pltpu.SMEM(storage_row.shape, I32),
            pltpu.VMEM((QD, QT, D), BF16),
            pltpu.SemaphoreType.DMA((3,)),
            pltpu.SMEM((N_DP,), I32),
        ],
    )(negative_ids, storage_row, queries)
    asked = exchange(sent, along(1))
    asked = exchange(jnp.broadcast_to(asked[None], (N_Z, N_Y, SENT, D)), along(0)).reshape(SPOTS, SENT, D)

    own_rows = call(normalize, struct((ROWS, PT, D), BF16), [vmem()], vmem())(passage_pool)
    other_rows = lax.ppermute(own_rows, "dp", swap)
    gathered = lax.all_gather(positives, "group", axis=0, tiled=True)
    gathered, pos_weight = call(
        positive_weight, (struct((BATCH, PT, D), BF16), struct((1, QROWS), F32)), [vmem(), vmem()], (vmem(), vmem())
    )(q_unit, gathered)

    factor, sums, codes = call(
        score,
        (
            struct((SPOTS, QROWS), F32),
            struct((SPOTS, QD, QROWS), F32),
            struct((8, SPOTS * 8), I32),
        ),
        [smem(), vmem(), vmem(), vmem(), vmem()],
        (vmem(), vmem(), vmem()),
        [
            pltpu.VMEM((SPOTS, QROWS), F32),
            pltpu.VMEM((SPOTS, QROWS), F32),
            pltpu.SMEM((8, SPOTS * 8), I32),
            pltpu.SemaphoreType.DMA,
        ],
    )(me, asked, own_rows, other_rows, pos_weight)
    sums = exchange(sums, planes())

    probs, back = call(
        terms,
        (struct((SPOTS, PT, QROWS), BF16), struct((SPOTS, QROWS, D), BF16)),
        [smem()] + [vmem()] * 4,
        (vmem(), vmem()),
    )(codes, asked, own_rows, other_rows, factor)
    arrived = exchange(back.reshape(N_Z, N_Y, QROWS, D), along(0))

    own_grad, other_grad, pos_grad, query_part, losses, weight_inv = call(
        weigh,
        (
            struct((ROWS, PT, D), F32),
            struct((ROWS, PT, D), BF16),
            struct((BATCH, PT, D), F32),
            struct((QROWS, D), F32),
            struct((1, QROWS), F32),
            struct((8, QROWS), F32),
        ),
        [smem(), smem(), vmem(), vmem(), vmem(), hbm(), hbm()],
        (vmem(),) * 5 + (smem(),),
        [
            pltpu.VMEM((ROWS, PT, D), F32),
            pltpu.VMEM((8, QROWS), F32),
            pltpu.VMEM((QD, QT, D), BF16),
            pltpu.VMEM((BATCH, PT, D), BF16),
            pltpu.SemaphoreType.DMA((3,)),
        ],
    )(me, codes, sums, asked, probs, q_unit, gathered)

    block = (QD + ROWS // GROUP, PT, D)
    kept, off1, off2, off3 = call(
        split,
        (struct(block, F32), struct(block, BF16), struct(block, BF16), struct(block, BF16)),
        [smem(), vmem(), vmem(), vmem()],
        (vmem(),) * 4,
    )(me, own_grad, lax.ppermute(other_grad, "dp", swap), pos_grad)
    total = kept
    for ahead, part in ((1, off1), (2, off2), (3, off3)):
        moved = lax.ppermute(part, "group", [(g, (g + ahead) % GROUP) for g in range(GROUP)])
        total = total + moved.astype(F32)

    arrived = call(
        add_blocks,
        struct((N_Y, QROWS, D), BF16),
        [hbm(), anywhere()],
        vmem(),
        [pltpu.VMEM((N_Z, N_Y, QROWS, D), BF16), pltpu.SemaphoreType.DMA((N_Y // 2,))],
    )(arrived, total)
    arrived = exchange(arrived, along(1))
    query_grad = call(
        collect, struct((QD, QT, D), F32), [smem(), smem(), vmem(), vmem()], vmem()
    )(weight_inv, me, query_part, arrived)
    return losses.reshape(QD, QT)[:, 0], query_grad, total[:QD], total[QD:]


def solution(mesh):
    in_specs = (P(EVERY), P(EVERY), P("dp"), P(EVERY), P())
    out_specs = (P(EVERY), P(EVERY), P(EVERY), P(EVERY))
    return jax.shard_map(per_device, mesh=mesh, in_specs=in_specs, out_specs=out_specs, check_vma=False)
```

```python
import jax
import jax.numpy as jnp
from jax import lax
from jax.experimental import pallas as pl
from jax.experimental.pallas import tpu as pltpu
from jax.sharding import PartitionSpec as P

N_Z, N_Y, N_C, GROUP = 8, 8, 2, 4
N_DP = N_Z * N_Y * N_C
SPOTS = N_Z * N_Y
QD, QT, PT, D, NEG, ROWS = 4, 32, 64, 128, 7, 32
QROWS = QD * QT
SENT = QROWS + 8
BATCH = QD * GROUP
SLOTS = 4
VMEM = 16 * 1024 * 1024
F32, BF16, I32 = jnp.float32, jnp.bfloat16, jnp.int32
EXACT = lax.Precision.HIGHEST
EVERY = ("dp", "group")


def device(z, y, c, x):
    return ((z * N_Y + y) * N_C + c) * GROUP + x


def chip(far_z, far_y, near_z, near_y, core):
    return (2 * far_z + near_z + core) % N_Z, (2 * far_y + near_y + core) % N_Y


FAR, NEAR = range(4), range(2)
PAIRS = [(i, j) for i in NEAR for j in NEAR]


def along(z_core):
    groups = []
    for core in range(N_C):
        for x in range(GROUP):
            for i, j in PAIRS:
                for fixed in FAR:
                    if core == z_core:
                        chips = [chip(move, fixed, i, j, core) for move in FAR]
                    else:
                        chips = [chip(fixed, move, i, j, core) for move in FAR]
                    groups.append([device(z, y, core, x) for z, y in chips])
    return groups


def neighbours():
    return [
        [device(*chip(fz, fy, i, j, core), core, x) for i, j in PAIRS]
        for core in range(N_C) for x in range(GROUP) for fz in FAR for fy in FAR
    ]


def planes():
    return [
        [
            device(*(chip(f, g, i, j, core) if core == 0 else chip(g, f, i, j, core)), core, x)
            for i, j in PAIRS for f in FAR for g in FAR
        ]
        for core in range(N_C) for x in range(GROUP)
    ]


def exchange(blocks, groups):
    return lax.all_to_all(blocks, EVERY, split_axis=0, concat_axis=0, axis_index_groups=groups, tiled=True)


def call(body, out_shape, in_specs, out_specs, scratch=()):
    return pl.pallas_call(
        body,
        out_shape=out_shape,
        in_specs=in_specs,
        out_specs=out_specs,
        scratch_shapes=list(scratch),
        compiler_params=pltpu.CompilerParams(vmem_limit_bytes=VMEM),
    )


def vmem():
    return pl.BlockSpec(memory_space=pltpu.VMEM)


def anywhere():
    return pl.BlockSpec(memory_space=pl.ANY)


def hbm():
    return pl.BlockSpec(memory_space=pltpu.HBM)


def smem():
    return pl.BlockSpec(memory_space=pltpu.SMEM)


def unit(values):
    wide = values.astype(F32)
    return (wide * lax.rsqrt(jnp.sum(wide * wide, axis=-1, keepdims=True) + 1e-06)).astype(BF16)


def iota(shape, dim):
    return lax.broadcasted_iota(I32, shape, dim)


def dot(a, b, dims, precision=None):
    return lax.dot_general(a, b, ((dims[0], dims[1]), ((), ())), precision=precision, preferred_element_type=F32)


def token_sum_matrix():
    return (iota((QROWS, QROWS), 0) // QT == iota((QROWS, QROWS), 1) // QT).astype(F32)


def fetch(pairs, sems):
    copies = [pltpu.make_async_copy(src, dst, sems.at[i]) for i, (src, dst) in enumerate(pairs)]
    for copy in copies:
        copy.start()
    return copies


def prepare(ids_in, storage_in, queries_in, sent, q_unit, ids, storage, queries, sems, count):
    pairs = [(storage_in, storage), (ids_in, ids), (queries_in, queries)]
    for copy in fetch(pairs, sems):
        copy.wait()
    tiles = unit(queries[...])
    q_unit[...] = tiles
    homes = []
    for q in range(QD):
        for k in range(NEG):
            home = storage[ids[q, k]]
            owner = home // ROWS
            lane_of = (owner % N_C) * SPOTS + owner // N_C
            count[lane_of] = 0
            homes.append((lane_of, q * ROWS + home % ROWS + 1))
    lane = iota((8, N_DP), 1)
    sub = iota((8, N_DP), 0)
    codes = jnp.zeros((8, N_DP), F32)
    for lane_of, code in homes:
        rank = count[lane_of]
        count[lane_of] = rank + 1
        codes = jnp.where((lane == lane_of) & (sub == rank), code.astype(F32), codes)
    for copy in range(4):
        sent[copy, 0:QROWS, :] = tiles.reshape(QROWS, D)
        sent[copy, QROWS:SENT, :] = codes.astype(BF16)


def normalize(values, out):
    out[...] = unit(values[...])


def positive_scores(q_unit, gathered):
    cands = gathered[...].reshape(BATCH * PT, D)
    exp_scores = jnp.exp(10.0 * dot(cands, q_unit, ((1,), (1,)))).reshape(BATCH, PT, QROWS)
    total = jnp.sum(exp_scores, axis=1)
    score = 0.1 * dot(jnp.log(total), token_sum_matrix(), ((1,), (0,)), EXACT)
    return cands, exp_scores, total, score


def positive_weight(q_tiles, positives, gathered, out):
    gathered[...] = unit(positives[...])
    score = positive_scores(q_tiles[...].reshape(QROWS, D), gathered)[3]
    out[...] = jnp.sum(jnp.exp(score), axis=0, keepdims=True)


def request(codes, source, slot):
    code = codes[slot // 2, source * 8 + slot % 2]
    spot = jnp.maximum(code - 1, 0)
    return code > 0, spot // ROWS, spot % ROWS


def passages(codes, own_rows, other_rows, source):
    picked = [request(codes, source, slot)[2] for slot in range(SLOTS)]
    return jnp.concatenate([own_rows[picked[0]], own_rows[picked[1]], other_rows[picked[2]], other_rows[picked[3]]], axis=0)


def asking(codes, asked, source):
    picked = [request(codes, source, slot)[1] for slot in range(SLOTS)]
    return jnp.concatenate([asked[source, pl.ds(pl.multiple_of(q * QT, QT), QT), :] for q in picked], axis=0)


def spread(packed):
    block = iota((PT, QROWS), 1) // QT
    return jnp.concatenate([jnp.where(block == b, packed, 0.0).astype(BF16) for b in range(SLOTS)], axis=0)


def read_codes(me, asked, table, codes, sem):
    rows = asked[:, QROWS:SENT, :].reshape(SPOTS * 8, N_DP)
    which = iota((8, N_DP), 0)
    spot = jnp.where(which == 0, me[2], me[3])
    pick = ((iota((8, N_DP), 1) == spot) & (which < 2)).astype(F32).astype(BF16)
    table[...] = dot(pick, rows, ((1,), (1,))).astype(I32)
    copy = pltpu.make_async_copy(table, codes, sem)
    copy.start()
    copy.wait()


def exponentials(codes, asked, own_rows, other_rows, source):
    block = iota((PT, QROWS), 1) // QT
    full = dot(passages(codes, own_rows, other_rows, source), asking(codes, asked, source), ((1,), (1,)))
    packed = full[0:PT]
    for b in range(1, SLOTS):
        packed = jnp.where(block == b, full[b * PT : (b + 1) * PT], packed)
    return jnp.exp(10.0 * packed)


def score(me, asked, own_rows, other_rows, pos_weight, factor, sums, table, totals, marks, codes, sem):
    read_codes(me, asked, table, codes, sem)
    lane = iota((1, QROWS), 1)

    def one(source, carry):
        mark = jnp.full((1, QROWS), -1.0, F32)
        for b in range(SLOTS):
            valid, q, _ = request(codes, source, b)
            mark = jnp.where((lane // QT == b) & valid, q.astype(F32), mark)
        exp_scores = exponentials(codes, asked, own_rows, other_rows, source)
        totals[pl.ds(source, 1), :] = jnp.sum(exp_scores, axis=0, keepdims=True)
        marks[pl.ds(source, 1), :] = mark
        return carry

    size = 8
    for chunk in range(SPOTS // size):
        lax.fori_loop(chunk * size, (chunk + 1) * size, one, 0, unroll=size)

    total = totals[...]
    mark = marks[...]
    weight = jnp.exp(0.1 * dot(jnp.log(total), token_sum_matrix(), ((1,), (0,)), EXACT))
    weight = jnp.where(mark >= 0.0, weight, 0.0)
    factor[...] = weight / total
    first = iota((SPOTS, QROWS), 1) % QT == 0
    pad = jnp.zeros((QROWS - SPOTS, QROWS), F32)
    ones = jnp.ones((8, QROWS), F32)
    parts = []
    for q in range(QD):
        mine = jnp.where((mark == float(q)) & first, weight, 0.0)
        part = dot(ones, jnp.concatenate([mine, pad], axis=0), ((1,), (1,)), EXACT)[0:1]
        own = jnp.sum(jnp.where(lane == q * QT, pos_weight[...], 0.0), axis=1, keepdims=True)
        parts.append(part + jnp.where(lane == me[0], own, 0.0))
    sums[...] = jnp.broadcast_to(jnp.concatenate(parts, axis=0)[None], (SPOTS, QD, QROWS))


def terms(codes, asked, own_rows, other_rows, factor, probs, back):
    def one(source, carry):
        packed = exponentials(codes, asked, own_rows, other_rows, source) * factor[pl.ds(source, 1), :]
        probs[source] = packed.astype(BF16)
        grads = dot(spread(packed), passages(codes, own_rows, other_rows, source), ((0,), (0,)))
        picked = [request(codes, source, slot)[1] for slot in range(SLOTS)]
        for q in range(QD):
            total = jnp.zeros((QT, D), F32)
            for b in range(SLOTS):
                total += grads[b * QT : (b + 1) * QT] * (picked[b] == q).astype(F32)
            back[source, q * QT : (q + 1) * QT, :] = total.astype(BF16)
        return carry

    lax.fori_loop(0, SPOTS, one, 0, unroll=8)


def weigh(
    me, codes, sums, asked, probs, q_in, gathered_in, own_grad, other_grad, pos_grad, query_part, losses, weight_inv,
    other_acc, inverse, q_tiles, gathered, sems,
):
    later = fetch([(q_in, q_tiles), (gathered_in, gathered)], sems)
    weight_sum = jnp.sum(sums[...], axis=0)
    inverse[...] = jnp.zeros_like(inverse)
    inverse[0:QD] = 1.0 / weight_sum
    copy = pltpu.make_async_copy(inverse, weight_inv, sems.at[2])
    copy.start()
    own_grad[...] = jnp.zeros_like(own_grad)
    other_acc[...] = jnp.zeros_like(other_acc)
    copy.wait()

    def add(source, carry):
        grads = dot(spread(probs[source].astype(F32)), asking(codes, asked, source), ((1,), (0,)))
        for b in range(SLOTS):
            _, q, row = request(codes, source, b)
            acc = own_grad if b < 2 else other_acc
            acc[row] += grads[b * PT : (b + 1) * PT] * weight_inv[q, source]
        return carry

    lax.fori_loop(0, SPOTS, add, 0, unroll=8)
    other_grad[...] = other_acc[...].astype(BF16)

    for copy in later:
        copy.wait()
    q_unit = q_tiles[...].reshape(QROWS, D)
    cands, exp_scores, total, scores = positive_scores(q_unit, gathered)
    lane = iota((1, QROWS), 1)
    mine = jnp.sum(jnp.where(lane == me[0], weight_sum, 0.0), axis=1, keepdims=True)
    own_sum = jnp.zeros((1, QROWS), F32)
    for q in range(QD):
        own_sum = jnp.where(lane // QT == q, mine[q : q + 1], own_sum)
    own = (iota((BATCH, QROWS), 0) == me[1] * QD + iota((BATCH, QROWS), 1) // QT).astype(F32)
    score_grad = jnp.exp(scores) / own_sum - own
    losses[...] = jnp.log(own_sum) - jnp.sum(scores * own, axis=0, keepdims=True)
    weight_grad = (exp_scores * (score_grad / total)[:, None, :]).astype(BF16).reshape(BATCH * PT, QROWS)
    query_part[...] = dot(weight_grad, cands, ((0,), (0,)))
    pos_grad[...] = dot(weight_grad, q_unit, ((1,), (0,))).reshape(BATCH, PT, D)


def split(me, own_grad, moved, pos_grad, kept, off1, off2, off3):
    share = ROWS // GROUP
    for ahead, out in enumerate((kept, off1, off2, off3)):
        g = (me[1] + ahead) % GROUP
        out[0:QD] = pos_grad[pl.ds(g * QD, QD)].astype(out.dtype)
        rows = pl.ds(g * share, share)
        out[QD:] = (own_grad[rows] + moved[rows].astype(F32)).astype(out.dtype)


def add_blocks(arrived, after, out, blocks, sems):
    del after
    parts = [slice(i * out.shape[0] // 4, (i + 1) * out.shape[0] // 4) for i in range(4)]
    for part, copy in zip(parts, fetch([(arrived.at[:, part], blocks.at[:, part]) for part in parts], sems)):
        copy.wait()
        out[part] = jnp.sum(blocks[:, part].astype(F32), axis=0).astype(BF16)


def add_four(arrived, after):
    return call(
        add_blocks,
        jax.ShapeDtypeStruct(arrived.shape[1:], BF16),
        [hbm(), anywhere()],
        vmem(),
        [pltpu.VMEM(arrived.shape, BF16), pltpu.SemaphoreType.DMA((4,))],
    )(arrived, after)


def collect(weight_inv, me, query_part, arrived, out):
    total = jnp.sum(arrived[...].astype(F32), axis=0)
    for q in range(QD):
        rows = slice(q * QT, (q + 1) * QT)
        out[q] = query_part[rows, :] + total[rows] * weight_inv[q, me[0]]


def per_device(queries, positives, passage_pool, negative_ids, storage_row):
    struct = jax.ShapeDtypeStruct
    holder = lax.axis_index("dp")
    z, y, core = holder // (N_Y * N_C), (holder // N_C) % N_Y, holder % N_C
    z, y = (z - core) % N_Z, (y - core) % N_Y
    near = (z % 2) * 2 + y % 2
    source = near * 16 + jnp.where(core == 0, (z // 2) * 4 + y // 2, (y // 2) * 4 + z // 2)
    spot = holder // N_C
    me = jnp.stack([source, lax.axis_index("group"), core * SPOTS + spot, (1 - core) * SPOTS + spot]).astype(I32)
    swap = [(h, h ^ 1) for h in range(N_DP)]
    tiles = struct((QD, QT, D), BF16)

    sent, q_unit = call(
        prepare,
        (struct((4, SENT, D), BF16), tiles),
        [hbm()] * 3,
        (vmem(), vmem()),
        [
            pltpu.SMEM(negative_ids.shape, I32),
            pltpu.SMEM(storage_row.shape, I32),
            pltpu.VMEM((QD, QT, D), BF16),
            pltpu.SemaphoreType.DMA((3,)),
            pltpu.SMEM((N_DP,), I32),
        ],
    )(negative_ids, storage_row, queries)
    asked = exchange(sent, along(1))
    asked = exchange(jnp.broadcast_to(asked[None], (4, 4, SENT, D)), along(0)).reshape(16, SENT, D)
    asked = exchange(jnp.broadcast_to(asked[None], (4, 16, SENT, D)), neighbours()).reshape(SPOTS, SENT, D)

    own_rows = call(normalize, struct((ROWS, PT, D), BF16), [vmem()], vmem())(passage_pool)
    other_rows = lax.ppermute(own_rows, "dp", swap)
    gathered = lax.all_gather(positives, "group", axis=0, tiled=True)
    gathered, pos_weight = call(
        positive_weight, (struct((BATCH, PT, D), BF16), struct((1, QROWS), F32)), [vmem(), vmem()], (vmem(), vmem())
    )(q_unit, gathered)

    factor, sums, codes = call(
        score,
        (
            struct((SPOTS, QROWS), F32),
            struct((SPOTS, QD, QROWS), F32),
            struct((8, SPOTS * 8), I32),
        ),
        [smem(), vmem(), vmem(), vmem(), vmem()],
        (vmem(), vmem(), vmem()),
        [
            pltpu.VMEM((SPOTS, QROWS), F32),
            pltpu.VMEM((SPOTS, QROWS), F32),
            pltpu.SMEM((8, SPOTS * 8), I32),
            pltpu.SemaphoreType.DMA,
        ],
    )(me, asked, own_rows, other_rows, pos_weight)
    sums = exchange(sums, planes())

    probs, back = call(
        terms,
        (struct((SPOTS, PT, QROWS), BF16), struct((SPOTS, QROWS, D), BF16)),
        [smem()] + [vmem()] * 4,
        (vmem(), vmem()),
    )(codes, asked, own_rows, other_rows, factor)
    arrived = exchange(back.reshape(4, 16, QROWS, D), neighbours())

    own_grad, other_grad, pos_grad, query_part, losses, weight_inv = call(
        weigh,
        (
            struct((ROWS, PT, D), F32),
            struct((ROWS, PT, D), BF16),
            struct((BATCH, PT, D), F32),
            struct((QROWS, D), F32),
            struct((1, QROWS), F32),
            struct((8, QROWS), F32),
        ),
        [smem(), smem(), vmem(), vmem(), vmem(), hbm(), hbm()],
        (vmem(),) * 5 + (smem(),),
        [
            pltpu.VMEM((ROWS, PT, D), F32),
            pltpu.VMEM((8, QROWS), F32),
            pltpu.VMEM((QD, QT, D), BF16),
            pltpu.VMEM((BATCH, PT, D), BF16),
            pltpu.SemaphoreType.DMA((3,)),
        ],
    )(me, codes, sums, asked, probs, q_unit, gathered)

    block = (QD + ROWS // GROUP, PT, D)
    kept, off1, off2, off3 = call(
        split,
        (struct(block, F32), struct(block, BF16), struct(block, BF16), struct(block, BF16)),
        [smem(), vmem(), vmem(), vmem()],
        (vmem(),) * 4,
    )(me, own_grad, lax.ppermute(other_grad, "dp", swap), pos_grad)
    total = kept
    for ahead, part in ((1, off1), (2, off2), (3, off3)):
        moved = lax.ppermute(part, "group", [(g, (g + ahead) % GROUP) for g in range(GROUP)])
        total = total + moved.astype(F32)

    arrived = exchange(add_four(arrived, kept).reshape(4, 4, QROWS, D), along(0))
    arrived = exchange(add_four(arrived, total), along(1))
    query_grad = call(
        collect, struct((QD, QT, D), F32), [smem(), smem(), vmem(), vmem()], vmem()
    )(weight_inv, me, query_part, arrived)
    return losses.reshape(QD, QT)[:, 0], query_grad, total[:QD], total[QD:]


def solution(mesh):
    in_specs = (P(EVERY), P(EVERY), P("dp"), P(EVERY), P())
    out_specs = (P(EVERY), P(EVERY), P(EVERY), P(EVERY))
    return jax.shard_map(per_device, mesh=mesh, in_specs=in_specs, out_specs=out_specs, check_vma=False)
```

```python
import jax
import jax.numpy as jnp
from jax import lax
from jax.experimental import pallas as pl
from jax.experimental.pallas import tpu as pltpu
from jax.sharding import PartitionSpec as P

N_Z, N_Y, N_C, GROUP = 8, 8, 2, 4
N_DP = N_Z * N_Y * N_C
SPOTS = N_Z * N_Y
QD, QT, PT, D, NEG, ROWS = 4, 32, 64, 128, 7, 32
QROWS = QD * QT
SENT = QROWS + 8
BATCH = QD * GROUP
SLOTS = 4
VMEM = 6 * 1024 * 1024
F32, BF16, I32 = jnp.float32, jnp.bfloat16, jnp.int32
EXACT = lax.Precision.HIGHEST
EVERY = ("dp", "group")


def device(z, y, c, x):
    return ((z * N_Y + y) * N_C + c) * GROUP + x


def along(z_core):
    z_lines = [[device(z, y, z_core, x) for z in range(N_Z)] for y in range(N_Y) for x in range(GROUP)]
    y_lines = [[device(z, y, 1 - z_core, x) for y in range(N_Y)] for z in range(N_Z) for x in range(GROUP)]
    return z_lines + y_lines


def planes():
    first = [[device(z, y, 0, x) for z in range(N_Z) for y in range(N_Y)] for x in range(GROUP)]
    second = [[device(z, y, 1, x) for y in range(N_Y) for z in range(N_Z)] for x in range(GROUP)]
    return first + second


def exchange(blocks, groups):
    return lax.all_to_all(blocks, EVERY, split_axis=0, concat_axis=0, axis_index_groups=groups, tiled=True)


def call(body, out_shape, in_specs, out_specs, scratch=()):
    return pl.pallas_call(
        body,
        out_shape=out_shape,
        in_specs=in_specs,
        out_specs=out_specs,
        scratch_shapes=list(scratch),
        compiler_params=pltpu.CompilerParams(vmem_limit_bytes=VMEM),
    )


def vmem():
    return pl.BlockSpec(memory_space=pltpu.VMEM)


def anywhere():
    return pl.BlockSpec(memory_space=pl.ANY)


def hbm():
    return pl.BlockSpec(memory_space=pltpu.HBM)


def smem():
    return pl.BlockSpec(memory_space=pltpu.SMEM)


def unit(values):
    wide = values.astype(F32)
    return (wide * lax.rsqrt(jnp.sum(wide * wide, axis=-1, keepdims=True) + 1e-06)).astype(BF16)


def iota(shape, dim):
    return lax.broadcasted_iota(I32, shape, dim)


def dot(a, b, dims, precision=None):
    return lax.dot_general(a, b, ((dims[0], dims[1]), ((), ())), precision=precision, preferred_element_type=F32)


def token_sum_matrix():
    return (iota((QROWS, QROWS), 0) // QT == iota((QROWS, QROWS), 1) // QT).astype(F32)


def fetch(pairs, sems):
    copies = [pltpu.make_async_copy(src, dst, sems.at[i]) for i, (src, dst) in enumerate(pairs)]
    for copy in copies:
        copy.start()
    return copies


def position():
    holder = lax.axis_index("dp")
    spot, core = holder // N_C, holder % N_C
    source = jnp.where(core == 0, spot, (spot % N_Y) * N_Z + spot // N_Y)
    return spot, core, source


def prepare(ids_in, storage_in, queries_in, sent, q_unit, ids, storage, queries, sems, count):
    pairs = [(storage_in, storage), (ids_in, ids), (queries_in, queries)]
    for copy in fetch(pairs, sems):
        copy.wait()
    tiles = unit(queries[...])
    q_unit[...] = tiles
    homes = []
    for q in range(QD):
        for k in range(NEG):
            home = storage[ids[q, k]]
            owner = home // ROWS
            lane_of = (owner % N_C) * SPOTS + owner // N_C
            count[lane_of] = 0
            homes.append((lane_of, q * ROWS + home % ROWS + 1))
    lane = iota((8, N_DP), 1)
    sub = iota((8, N_DP), 0)
    codes = jnp.zeros((8, N_DP), F32)
    for lane_of, code in homes:
        rank = count[lane_of]
        count[lane_of] = rank + 1
        codes = jnp.where((lane == lane_of) & (sub == rank), code.astype(F32), codes)
    for copy in range(N_Y):
        sent[copy, 0:QROWS, :] = tiles.reshape(QROWS, D)
        sent[copy, QROWS:SENT, :] = codes.astype(BF16)


def normalize(values, out):
    out[...] = unit(values[...])


def positive_scores(q_unit, gathered):
    cands = gathered[...].reshape(BATCH * PT, D)
    exp_scores = jnp.exp(10.0 * dot(cands, q_unit, ((1,), (1,)))).reshape(BATCH, PT, QROWS)
    total = jnp.sum(exp_scores, axis=1)
    score = 0.1 * dot(jnp.log(total), token_sum_matrix(), ((1,), (0,)), EXACT)
    return cands, exp_scores, total, score


def positive_weight(q_tiles, positives, gathered, out):
    gathered[...] = unit(positives[...])
    score = positive_scores(q_tiles[...].reshape(QROWS, D), gathered)[3]
    out[...] = jnp.sum(jnp.exp(score), axis=0, keepdims=True)


def request(codes, source, slot):
    code = codes[slot // 2, source * 8 + slot % 2]
    spot = jnp.maximum(code - 1, 0)
    return code > 0, spot // ROWS, spot % ROWS


def passages(codes, own_rows, other_rows, source):
    picked = [request(codes, source, slot)[2] for slot in range(SLOTS)]
    return jnp.concatenate([own_rows[picked[0]], own_rows[picked[1]], other_rows[picked[2]], other_rows[picked[3]]], axis=0)


def asking(codes, asked, source):
    picked = [request(codes, source, slot)[1] for slot in range(SLOTS)]
    return jnp.concatenate([asked[source, pl.ds(pl.multiple_of(q * QT, QT), QT), :] for q in picked], axis=0)


def spread(packed):
    block = iota((PT, QROWS), 1) // QT
    return jnp.concatenate([jnp.where(block == b, packed, 0.0).astype(BF16) for b in range(SLOTS)], axis=0)


def read_codes(asked, table, codes, sem):
    spot, core, _ = position()
    rows = asked[:, QROWS:SENT, :].reshape(SPOTS * 8, N_DP)
    which = iota((8, N_DP), 0)
    lane = jnp.where(which == 0, core * SPOTS + spot, (1 - core) * SPOTS + spot)
    pick = ((iota((8, N_DP), 1) == lane) & (which < 2)).astype(F32).astype(BF16)
    table[...] = dot(pick, rows, ((1,), (1,))).astype(I32)
    copy = pltpu.make_async_copy(table, codes, sem)
    copy.start()
    copy.wait()


def exponentials(codes, asked, own_rows, other_rows, source):
    block = iota((PT, QROWS), 1) // QT
    full = dot(passages(codes, own_rows, other_rows, source), asking(codes, asked, source), ((1,), (1,)))
    packed = full[0:PT]
    for b in range(1, SLOTS):
        packed = jnp.where(block == b, full[b * PT : (b + 1) * PT], packed)
    return jnp.exp(10.0 * packed)


def score(asked, own_rows, other_rows, pos_weight, factor, sums, table, totals, marks, codes, sem):
    read_codes(asked, table, codes, sem)
    source_here = position()[2]
    lane = iota((1, QROWS), 1)

    def one(source, carry):
        mark = jnp.full((1, QROWS), -1.0, F32)
        for b in range(SLOTS):
            valid, q, _ = request(codes, source, b)
            mark = jnp.where((lane // QT == b) & valid, q.astype(F32), mark)
        exp_scores = exponentials(codes, asked, own_rows, other_rows, source)
        totals[pl.ds(source, 1), :] = jnp.sum(exp_scores, axis=0, keepdims=True)
        marks[pl.ds(source, 1), :] = mark
        return carry

    size = 8
    for chunk in range(SPOTS // size):
        lax.fori_loop(chunk * size, (chunk + 1) * size, one, 0, unroll=size)

    total = totals[...]
    mark = marks[...]
    weight = jnp.exp(0.1 * dot(jnp.log(total), token_sum_matrix(), ((1,), (0,)), EXACT))
    weight = jnp.where(mark >= 0.0, weight, 0.0)
    factor[...] = weight / total
    first = iota((SPOTS, QROWS), 1) % QT == 0
    pad = jnp.zeros((QROWS - SPOTS, QROWS), F32)
    ones = jnp.ones((8, QROWS), F32)
    parts = []
    for q in range(QD):
        mine = jnp.where((mark == float(q)) & first, weight, 0.0)
        part = dot(ones, jnp.concatenate([mine, pad], axis=0), ((1,), (1,)), EXACT)[0:1]
        own = jnp.sum(jnp.where(lane == q * QT, pos_weight[...], 0.0), axis=1, keepdims=True)
        parts.append(part + jnp.where(lane == source_here, own, 0.0))
    sums[...] = jnp.broadcast_to(jnp.concatenate(parts, axis=0)[None], (SPOTS, QD, QROWS))


def terms(codes, asked, own_rows, other_rows, factor, probs, back):
    def one(source, carry):
        packed = exponentials(codes, asked, own_rows, other_rows, source) * factor[pl.ds(source, 1), :]
        probs[source] = packed.astype(BF16)
        grads = dot(spread(packed), passages(codes, own_rows, other_rows, source), ((0,), (0,)))
        picked = [request(codes, source, slot)[1] for slot in range(SLOTS)]
        for q in range(QD):
            total = jnp.zeros((QT, D), F32)
            for b in range(SLOTS):
                total += grads[b * QT : (b + 1) * QT] * (picked[b] == q).astype(F32)
            back[source, q * QT : (q + 1) * QT, :] = total.astype(BF16)
        return carry

    lax.fori_loop(0, SPOTS, one, 0, unroll=8)


def weigh(
    codes, sums, asked, probs, q_in, gathered_in, own_grad, other_grad, pos_grad, query_part, losses, weight_inv,
    other_acc, inverse, q_tiles, gathered, sems,
):
    later = fetch([(q_in, q_tiles), (gathered_in, gathered)], sems)
    weight_sum = jnp.sum(sums[...], axis=0)
    inverse[...] = jnp.zeros_like(inverse)
    inverse[0:QD] = 1.0 / weight_sum
    copy = pltpu.make_async_copy(inverse, weight_inv, sems.at[2])
    copy.start()
    own_grad[...] = jnp.zeros_like(own_grad)
    other_acc[...] = jnp.zeros_like(other_acc)
    copy.wait()

    def add(source, carry):
        grads = dot(spread(probs[source].astype(F32)), asking(codes, asked, source), ((1,), (0,)))
        for b in range(SLOTS):
            _, q, row = request(codes, source, b)
            acc = own_grad if b < 2 else other_acc
            acc[row] += grads[b * PT : (b + 1) * PT] * weight_inv[q, source]
        return carry

    lax.fori_loop(0, SPOTS, add, 0, unroll=8)
    other_grad[...] = other_acc[...].astype(BF16)

    for copy in later:
        copy.wait()
    q_unit = q_tiles[...].reshape(QROWS, D)
    cands, exp_scores, total, scores = positive_scores(q_unit, gathered)
    lane = iota((1, QROWS), 1)
    mine = jnp.sum(jnp.where(lane == position()[2], weight_sum, 0.0), axis=1, keepdims=True)
    own_sum = jnp.zeros((1, QROWS), F32)
    for q in range(QD):
        own_sum = jnp.where(lane // QT == q, mine[q : q + 1], own_sum)
    own = (iota((BATCH, QROWS), 0) == lax.axis_index("group") * QD + iota((BATCH, QROWS), 1) // QT).astype(F32)
    score_grad = jnp.exp(scores) / own_sum - own
    losses[...] = jnp.log(own_sum) - jnp.sum(scores * own, axis=0, keepdims=True)
    weight_grad = (exp_scores * (score_grad / total)[:, None, :]).astype(BF16).reshape(BATCH * PT, QROWS)
    query_part[...] = dot(weight_grad, cands, ((0,), (0,)))
    pos_grad[...] = dot(weight_grad, q_unit, ((1,), (0,))).reshape(BATCH, PT, D)


def split(own_grad, moved, pos_grad, kept, off1, off2, off3):
    share = ROWS // GROUP
    for ahead, out in enumerate((kept, off1, off2, off3)):
        g = (lax.axis_index("group") + ahead) % GROUP
        out[0:QD] = pos_grad[pl.ds(g * QD, QD)].astype(out.dtype)
        rows = pl.ds(g * share, share)
        out[QD:] = (own_grad[rows] + moved[rows].astype(F32)).astype(out.dtype)


def add_blocks(arrived, after, out):
    del after
    for part in range(N_Y):
        out[part] = jnp.sum(arrived[:, part].astype(F32), axis=0).astype(BF16)


def collect(weight_inv, query_part, arrived, out):
    source = position()[2]
    total = jnp.sum(arrived[...].astype(F32), axis=0)
    for q in range(QD):
        rows = slice(q * QT, (q + 1) * QT)
        out[q] = query_part[rows, :] + total[rows] * weight_inv[q, source]


def per_device(queries, positives, passage_pool, negative_ids, storage_row):
    struct = jax.ShapeDtypeStruct
    swap = [(h, h ^ 1) for h in range(N_DP)]
    tiles = struct((QD, QT, D), BF16)

    sent, q_unit = call(
        prepare,
        (struct((N_Y, SENT, D), BF16), tiles),
        [hbm()] * 3,
        (vmem(), vmem()),
        [
            pltpu.SMEM(negative_ids.shape, I32),
            pltpu.SMEM(storage_row.shape, I32),
            pltpu.VMEM((QD, QT, D), BF16),
            pltpu.SemaphoreType.DMA((3,)),
            pltpu.SMEM((N_DP,), I32),
        ],
    )(negative_ids, storage_row, queries)
    asked = exchange(sent, along(1))
    asked = exchange(jnp.broadcast_to(asked[None], (N_Z, N_Y, SENT, D)), along(0)).reshape(SPOTS, SENT, D)

    own_rows = call(normalize, struct((ROWS, PT, D), BF16), [vmem()], vmem())(passage_pool)
    other_rows = lax.ppermute(own_rows, "dp", swap)
    gathered = lax.all_gather(positives, "group", axis=0, tiled=True)
    gathered, pos_weight = call(
        positive_weight, (struct((BATCH, PT, D), BF16), struct((1, QROWS), F32)), [vmem(), vmem()], (vmem(), vmem())
    )(q_unit, gathered)

    factor, sums, codes = call(
        score,
        (
            struct((SPOTS, QROWS), F32),
            struct((SPOTS, QD, QROWS), F32),
            struct((8, SPOTS * 8), I32),
        ),
        [vmem(), vmem(), vmem(), vmem()],
        (vmem(), vmem(), vmem()),
        [
            pltpu.VMEM((SPOTS, QROWS), F32),
            pltpu.VMEM((SPOTS, QROWS), F32),
            pltpu.SMEM((8, SPOTS * 8), I32),
            pltpu.SemaphoreType.DMA,
        ],
    )(asked, own_rows, other_rows, pos_weight)
    sums = exchange(sums, planes())

    probs, back = call(
        terms,
        (struct((SPOTS, PT, QROWS), BF16), struct((SPOTS, QROWS, D), BF16)),
        [smem()] + [vmem()] * 4,
        (vmem(), vmem()),
    )(codes, asked, own_rows, other_rows, factor)
    arrived = exchange(back.reshape(N_Z, N_Y, QROWS, D), along(0))

    own_grad, other_grad, pos_grad, query_part, losses, weight_inv = call(
        weigh,
        (
            struct((ROWS, PT, D), F32),
            struct((ROWS, PT, D), BF16),
            struct((BATCH, PT, D), F32),
            struct((QROWS, D), F32),
            struct((1, QROWS), F32),
            struct((8, QROWS), F32),
        ),
        [smem(), vmem(), vmem(), vmem(), hbm(), hbm()],
        (vmem(),) * 5 + (smem(),),
        [
            pltpu.VMEM((ROWS, PT, D), F32),
            pltpu.VMEM((8, QROWS), F32),
            pltpu.VMEM((QD, QT, D), BF16),
            pltpu.VMEM((BATCH, PT, D), BF16),
            pltpu.SemaphoreType.DMA((3,)),
        ],
    )(codes, sums, asked, probs, q_unit, gathered)

    block = (QD + ROWS // GROUP, PT, D)
    kept, off1, off2, off3 = call(
        split,
        (struct(block, F32), struct(block, BF16), struct(block, BF16), struct(block, BF16)),
        [vmem(), vmem(), vmem()],
        (vmem(),) * 4,
    )(own_grad, lax.ppermute(other_grad, "dp", swap), pos_grad)
    total = kept
    for ahead, part in ((1, off1), (2, off2), (3, off3)):
        moved = lax.ppermute(part, "group", [(g, (g + ahead) % GROUP) for g in range(GROUP)])
        total = total + moved.astype(F32)

    arrived = call(add_blocks, struct((N_Y, QROWS, D), BF16), [vmem(), anywhere()], vmem())(arrived, total)
    arrived = exchange(arrived, along(1))
    query_grad = call(
        collect, struct((QD, QT, D), F32), [smem(), vmem(), vmem()], vmem()
    )(weight_inv, query_part, arrived)
    return losses.reshape(QD, QT)[:, 0], query_grad, total[:QD], total[QD:]


def solution(mesh):
    in_specs = (P(EVERY), P(EVERY), P("dp"), P(EVERY), P())
    out_specs = (P(EVERY), P(EVERY), P(EVERY), P(EVERY))
    return jax.shard_map(per_device, mesh=mesh, in_specs=in_specs, out_specs=out_specs, check_vma=False)
```

```python
import jax
import jax.numpy as jnp
from jax import lax
from jax.experimental import pallas as pl
from jax.experimental.pallas import tpu as pltpu
from jax.sharding import PartitionSpec as P

N_Z, N_Y, N_C, GROUP = 8, 8, 2, 4
N_DP = N_Z * N_Y * N_C
SPOTS = N_Z * N_Y
QD, QT, PT, D, NEG, ROWS = 4, 32, 64, 128, 7, 32
QROWS = QD * QT
SENT = QROWS + 8
BATCH = QD * GROUP
SLOTS = 4
VMEM = 6 * 1024 * 1024
F32, BF16, I32 = jnp.float32, jnp.bfloat16, jnp.int32
EXACT = lax.Precision.HIGHEST
EVERY = ("dp", "group")


def device(z, y, c, x):
    return ((z * N_Y + y) * N_C + c) * GROUP + x


def along(z_core):
    z_lines = [[device(z, y, z_core, x) for z in range(N_Z)] for y in range(N_Y) for x in range(GROUP)]
    y_lines = [[device(z, y, 1 - z_core, x) for y in range(N_Y)] for z in range(N_Z) for x in range(GROUP)]
    return z_lines + y_lines


def planes():
    first = [[device(z, y, 0, x) for z in range(N_Z) for y in range(N_Y)] for x in range(GROUP)]
    second = [[device(z, y, 1, x) for y in range(N_Y) for z in range(N_Z)] for x in range(GROUP)]
    return first + second


def exchange(blocks, groups):
    return lax.all_to_all(blocks, EVERY, split_axis=0, concat_axis=0, axis_index_groups=groups, tiled=True)


def call(body, out_shape, in_specs, out_specs, scratch=()):
    return pl.pallas_call(
        body,
        out_shape=out_shape,
        in_specs=in_specs,
        out_specs=out_specs,
        scratch_shapes=list(scratch),
        compiler_params=pltpu.CompilerParams(vmem_limit_bytes=VMEM),
    )


def vmem():
    return pl.BlockSpec(memory_space=pltpu.VMEM)


def anywhere():
    return pl.BlockSpec(memory_space=pl.ANY)


def hbm():
    return pl.BlockSpec(memory_space=pltpu.HBM)


def smem():
    return pl.BlockSpec(memory_space=pltpu.SMEM)


def unit(values):
    wide = values.astype(F32)
    return (wide * lax.rsqrt(jnp.sum(wide * wide, axis=-1, keepdims=True) + 1e-06)).astype(BF16)


def iota(shape, dim):
    return lax.broadcasted_iota(I32, shape, dim)


def dot(a, b, dims, precision=None):
    return lax.dot_general(a, b, ((dims[0], dims[1]), ((), ())), precision=precision, preferred_element_type=F32)


def token_sum_matrix():
    return (iota((QROWS, QROWS), 0) // QT == iota((QROWS, QROWS), 1) // QT).astype(F32)


def fetch(pairs, sems):
    copies = [pltpu.make_async_copy(src, dst, sems.at[i]) for i, (src, dst) in enumerate(pairs)]
    for copy in copies:
        copy.start()
    return copies


def position():
    holder = lax.axis_index("dp")
    spot, core = holder // N_C, holder % N_C
    source = jnp.where(core == 0, spot, (spot % N_Y) * N_Z + spot // N_Y)
    return spot, core, source


def prepare(ids_in, storage_in, queries_in, sent, q_unit, ids, storage, queries, sems, count):
    pairs = [(storage_in, storage), (ids_in, ids), (queries_in, queries)]
    for copy in fetch(pairs, sems):
        copy.wait()
    tiles = unit(queries[...])
    q_unit[...] = tiles
    homes = []
    for q in range(QD):
        for k in range(NEG):
            home = storage[ids[q, k]]
            owner = home // ROWS
            lane_of = (owner % N_C) * SPOTS + owner // N_C
            count[lane_of] = 0
            homes.append((lane_of, q * ROWS + home % ROWS + 1))
    lane = iota((8, N_DP), 1)
    sub = iota((8, N_DP), 0)
    codes = jnp.zeros((8, N_DP), F32)
    for lane_of, code in homes:
        rank = count[lane_of]
        count[lane_of] = rank + 1
        codes = jnp.where((lane == lane_of) & (sub == rank), code.astype(F32), codes)
    for copy in range(N_Y):
        sent[copy, 0:QROWS, :] = tiles.reshape(QROWS, D)
        sent[copy, QROWS:SENT, :] = codes.astype(BF16)


def normalize(values, out):
    out[...] = unit(values[...])


def positive_scores(q_unit, gathered):
    cands = gathered[...].reshape(BATCH * PT, D)
    exp_scores = jnp.exp(10.0 * dot(cands, q_unit, ((1,), (1,)))).reshape(BATCH, PT, QROWS)
    total = jnp.sum(exp_scores, axis=1)
    score = 0.1 * dot(jnp.log(total), token_sum_matrix(), ((1,), (0,)), EXACT)
    return cands, exp_scores, total, score


def positive_weight(q_tiles, positives, gathered, out):
    gathered[...] = unit(positives[...])
    score = positive_scores(q_tiles[...].reshape(QROWS, D), gathered)[3]
    out[...] = jnp.sum(jnp.exp(score), axis=0, keepdims=True)


def request(codes, source, slot):
    code = codes[slot // 2, source * 8 + slot % 2]
    spot = jnp.maximum(code - 1, 0)
    return code > 0, spot // ROWS, spot % ROWS


def passages(codes, own_rows, other_rows, source):
    picked = [request(codes, source, slot)[2] for slot in range(SLOTS)]
    return jnp.concatenate([own_rows[picked[0]], own_rows[picked[1]], other_rows[picked[2]], other_rows[picked[3]]], axis=0)


def asking(codes, asked, source):
    picked = [request(codes, source, slot)[1] for slot in range(SLOTS)]
    return jnp.concatenate([asked[source, pl.ds(pl.multiple_of(q * QT, QT), QT), :] for q in picked], axis=0)


def spread(packed):
    block = iota((PT, QROWS), 1) // QT
    return jnp.concatenate([jnp.where(block == b, packed, 0.0).astype(BF16) for b in range(SLOTS)], axis=0)


def for_sources(step):
    for first in range(0, SPOTS, 8):
        lax.fori_loop(first, first + 8, step, 0, unroll=8)


def read_codes(asked, table, codes, sem):
    spot, core, _ = position()
    rows = asked[:, QROWS:SENT, :].reshape(SPOTS * 8, N_DP)
    which = iota((8, N_DP), 0)
    lane = jnp.where(which == 0, core * SPOTS + spot, (1 - core) * SPOTS + spot)
    pick = ((iota((8, N_DP), 1) == lane) & (which < 2)).astype(F32).astype(BF16)
    table[...] = dot(pick, rows, ((1,), (1,))).astype(I32)
    copy = pltpu.make_async_copy(table, codes, sem)
    copy.start()
    copy.wait()


def exponentials(codes, asked, own_rows, other_rows, source):
    block = iota((PT, QROWS), 1) // QT
    full = dot(passages(codes, own_rows, other_rows, source), asking(codes, asked, source), ((1,), (1,)))
    packed = full[0:PT]
    for b in range(1, SLOTS):
        packed = jnp.where(block == b, full[b * PT : (b + 1) * PT], packed)
    return jnp.exp(10.0 * packed)


def score(asked, own_rows, other_rows, pos_weight, factor, sums, table, totals, marks, codes, sem):
    read_codes(asked, table, codes, sem)
    source_here = position()[2]
    lane = iota((1, QROWS), 1)

    def one(source, carry):
        mark = jnp.full((1, QROWS), -1.0, F32)
        for b in range(SLOTS):
            valid, q, _ = request(codes, source, b)
            mark = jnp.where((lane // QT == b) & valid, q.astype(F32), mark)
        exp_scores = exponentials(codes, asked, own_rows, other_rows, source)
        totals[pl.ds(source, 1), :] = jnp.sum(exp_scores, axis=0, keepdims=True)
        marks[pl.ds(source, 1), :] = mark
        return carry

    for_sources(one)

    total = totals[...]
    mark = marks[...]
    weight = jnp.exp(0.1 * dot(jnp.log(total), token_sum_matrix(), ((1,), (0,)), EXACT))
    weight = jnp.where(mark >= 0.0, weight, 0.0)
    factor[...] = weight / total
    first = iota((SPOTS, QROWS), 1) % QT == 0
    pad = jnp.zeros((QROWS - SPOTS, QROWS), F32)
    ones = jnp.ones((8, QROWS), F32)
    parts = []
    for q in range(QD):
        mine = jnp.where((mark == float(q)) & first, weight, 0.0)
        part = dot(ones, jnp.concatenate([mine, pad], axis=0), ((1,), (1,)), EXACT)[0:1]
        own = jnp.sum(jnp.where(lane == q * QT, pos_weight[...], 0.0), axis=1, keepdims=True)
        parts.append(part + jnp.where(lane == source_here, own, 0.0))
    sums[...] = jnp.broadcast_to(jnp.concatenate(parts, axis=0)[None], (SPOTS, QD, QROWS))


def terms(codes, asked, own_rows, other_rows, factor, probs, back):
    def one(source, carry):
        packed = exponentials(codes, asked, own_rows, other_rows, source) * factor[pl.ds(source, 1), :]
        probs[source] = packed.astype(BF16)
        grads = dot(spread(packed), passages(codes, own_rows, other_rows, source), ((0,), (0,)))
        picked = [request(codes, source, slot)[1] for slot in range(SLOTS)]
        for q in range(QD):
            total = jnp.zeros((QT, D), F32)
            for b in range(SLOTS):
                total += grads[b * QT : (b + 1) * QT] * (picked[b] == q).astype(F32)
            back[source, q * QT : (q + 1) * QT, :] = total.astype(BF16)
        return carry

    for_sources(one)


def weigh(
    codes, sums, asked, probs, q_in, gathered_in, own_grad, other_grad, pos_grad, query_part, losses, weight_inv,
    other_acc, inverse, q_tiles, gathered, sems,
):
    later = fetch([(q_in, q_tiles), (gathered_in, gathered)], sems)
    weight_sum = jnp.sum(sums[...], axis=0)
    inverse[...] = jnp.zeros_like(inverse)
    inverse[0:QD] = 1.0 / weight_sum
    copy = pltpu.make_async_copy(inverse, weight_inv, sems.at[2])
    copy.start()
    own_grad[...] = jnp.zeros_like(own_grad)
    other_acc[...] = jnp.zeros_like(other_acc)
    copy.wait()

    def add(source, carry):
        grads = dot(spread(probs[source].astype(F32)), asking(codes, asked, source), ((1,), (0,)))
        for b in range(SLOTS):
            _, q, row = request(codes, source, b)
            acc = own_grad if b < 2 else other_acc
            acc[row] += grads[b * PT : (b + 1) * PT] * weight_inv[q, source]
        return carry

    for_sources(add)
    other_grad[...] = other_acc[...].astype(BF16)

    for copy in later:
        copy.wait()
    q_unit = q_tiles[...].reshape(QROWS, D)
    cands, exp_scores, total, scores = positive_scores(q_unit, gathered)
    lane = iota((1, QROWS), 1)
    mine = jnp.sum(jnp.where(lane == position()[2], weight_sum, 0.0), axis=1, keepdims=True)
    own_sum = jnp.zeros((1, QROWS), F32)
    for q in range(QD):
        own_sum = jnp.where(lane // QT == q, mine[q : q + 1], own_sum)
    own = (iota((BATCH, QROWS), 0) == lax.axis_index("group") * QD + iota((BATCH, QROWS), 1) // QT).astype(F32)
    score_grad = jnp.exp(scores) / own_sum - own
    losses[...] = jnp.log(own_sum) - jnp.sum(scores * own, axis=0, keepdims=True)
    weight_grad = (exp_scores * (score_grad / total)[:, None, :]).astype(BF16).reshape(BATCH * PT, QROWS)
    query_part[...] = dot(weight_grad, cands, ((0,), (0,)))
    pos_grad[...] = dot(weight_grad, q_unit, ((1,), (0,))).reshape(BATCH, PT, D)


def split(own_grad, moved, pos_grad, kept, off1, off2, off3):
    share = ROWS // GROUP
    for ahead, out in enumerate((kept, off1, off2, off3)):
        g = (lax.axis_index("group") + ahead) % GROUP
        out[0:QD] = pos_grad[pl.ds(g * QD, QD)].astype(out.dtype)
        rows = pl.ds(g * share, share)
        out[QD:] = (own_grad[rows] + moved[rows].astype(F32)).astype(out.dtype)


def add_blocks(arrived, after, out):
    del after
    for part in range(N_Y):
        out[part] = jnp.sum(arrived[:, part].astype(F32), axis=0).astype(BF16)


def collect(weight_inv, query_part, arrived, out):
    source = position()[2]
    total = jnp.sum(arrived[...].astype(F32), axis=0)
    for q in range(QD):
        rows = slice(q * QT, (q + 1) * QT)
        out[q] = query_part[rows, :] + total[rows] * weight_inv[q, source]


def per_device(queries, positives, passage_pool, negative_ids, storage_row):
    struct = jax.ShapeDtypeStruct
    swap = [(h, h ^ 1) for h in range(N_DP)]
    tiles = struct((QD, QT, D), BF16)

    sent, q_unit = call(
        prepare,
        (struct((N_Y, SENT, D), BF16), tiles),
        [hbm()] * 3,
        (vmem(), vmem()),
        [
            pltpu.SMEM(negative_ids.shape, I32),
            pltpu.SMEM(storage_row.shape, I32),
            pltpu.VMEM((QD, QT, D), BF16),
            pltpu.SemaphoreType.DMA((3,)),
            pltpu.SMEM((N_DP,), I32),
        ],
    )(negative_ids, storage_row, queries)
    asked = exchange(sent, along(1))
    asked = exchange(jnp.broadcast_to(asked[None], (N_Z, N_Y, SENT, D)), along(0)).reshape(SPOTS, SENT, D)

    own_rows = call(normalize, struct((ROWS, PT, D), BF16), [vmem()], vmem())(passage_pool)
    other_rows = lax.ppermute(own_rows, "dp", swap)
    gathered = lax.all_gather(positives, "group", axis=0, tiled=True)
    gathered, pos_weight = call(
        positive_weight, (struct((BATCH, PT, D), BF16), struct((1, QROWS), F32)), [vmem(), vmem()], (vmem(), vmem())
    )(q_unit, gathered)

    factor, sums, codes = call(
        score,
        (
            struct((SPOTS, QROWS), F32),
            struct((SPOTS, QD, QROWS), F32),
            struct((8, SPOTS * 8), I32),
        ),
        [vmem(), vmem(), vmem(), vmem()],
        (vmem(), vmem(), vmem()),
        [
            pltpu.VMEM((SPOTS, QROWS), F32),
            pltpu.VMEM((SPOTS, QROWS), F32),
            pltpu.SMEM((8, SPOTS * 8), I32),
            pltpu.SemaphoreType.DMA,
        ],
    )(asked, own_rows, other_rows, pos_weight)
    sums = exchange(sums, planes())

    probs, back = call(
        terms,
        (struct((SPOTS, PT, QROWS), BF16), struct((SPOTS, QROWS, D), BF16)),
        [smem()] + [vmem()] * 4,
        (vmem(), vmem()),
    )(codes, asked, own_rows, other_rows, factor)
    arrived = exchange(back.reshape(N_Z, N_Y, QROWS, D), along(0))

    own_grad, other_grad, pos_grad, query_part, losses, weight_inv = call(
        weigh,
        (
            struct((ROWS, PT, D), F32),
            struct((ROWS, PT, D), BF16),
            struct((BATCH, PT, D), F32),
            struct((QROWS, D), F32),
            struct((1, QROWS), F32),
            struct((8, QROWS), F32),
        ),
        [smem(), vmem(), vmem(), vmem(), hbm(), hbm()],
        (vmem(),) * 5 + (smem(),),
        [
            pltpu.VMEM((ROWS, PT, D), F32),
            pltpu.VMEM((8, QROWS), F32),
            pltpu.VMEM((QD, QT, D), BF16),
            pltpu.VMEM((BATCH, PT, D), BF16),
            pltpu.SemaphoreType.DMA((3,)),
        ],
    )(codes, sums, asked, probs, q_unit, gathered)

    block = (QD + ROWS // GROUP, PT, D)
    kept, off1, off2, off3 = call(
        split,
        (struct(block, F32), struct(block, BF16), struct(block, BF16), struct(block, BF16)),
        [vmem(), vmem(), vmem()],
        (vmem(),) * 4,
    )(own_grad, lax.ppermute(other_grad, "dp", swap), pos_grad)
    moved = [
        lax.ppermute(part, "group", [(g, (g + ahead) % GROUP) for g in range(GROUP)]).astype(F32)
        for ahead, part in ((2, off2), (1, off1), (3, off3))
    ]
    total = kept + moved[0] + moved[1]
    arrived = call(add_blocks, struct((N_Y, QROWS, D), BF16), [vmem(), anywhere()], vmem())(arrived, total)
    arrived = exchange(arrived, along(1))
    query_grad = call(
        collect, struct((QD, QT, D), F32), [smem(), vmem(), vmem()], vmem()
    )(weight_inv, query_part, arrived)
    total = total + moved[2]
    return losses.reshape(QD, QT)[:, 0], query_grad, total[:QD], total[QD:]


def solution(mesh):
    in_specs = (P(EVERY), P(EVERY), P("dp"), P(EVERY), P())
    out_specs = (P(EVERY), P(EVERY), P(EVERY), P(EVERY))
    return jax.shard_map(per_device, mesh=mesh, in_specs=in_specs, out_specs=out_specs, check_vma=False)
```

```python
import jax
import jax.numpy as jnp
from jax import lax
from jax.experimental import pallas as pl
from jax.experimental.pallas import tpu as pltpu
from jax.sharding import PartitionSpec as P

N_Z, N_Y, N_C, GROUP = 8, 8, 2, 4
N_DP = N_Z * N_Y * N_C
SPOTS = N_Z * N_Y
QD, QT, PT, D, NEG, ROWS = 4, 32, 64, 128, 7, 32
QROWS = QD * QT
PASSAGE_ROWS = 4096 // 128
SENT = QROWS + 8
BATCH = QD * GROUP
SLOTS = 4
VMEM = 6 * 1024 * 1024
F32, BF16, I32 = jnp.float32, jnp.bfloat16, jnp.int32
EXACT = lax.Precision.HIGHEST
EVERY = ("dp", "group")


def device(z, y, c, x):
    return ((z * N_Y + y) * N_C + c) * GROUP + x


def along(z_core):
    z_lines = [[device(z, y, z_core, x) for z in range(N_Z)] for y in range(N_Y) for x in range(GROUP)]
    y_lines = [[device(z, y, 1 - z_core, x) for y in range(N_Y)] for z in range(N_Z) for x in range(GROUP)]
    return z_lines + y_lines


def planes():
    first = [[device(z, y, 0, x) for z in range(N_Z) for y in range(N_Y)] for x in range(GROUP)]
    second = [[device(z, y, 1, x) for y in range(N_Y) for z in range(N_Z)] for x in range(GROUP)]
    return first + second


def exchange(blocks, groups):
    return lax.all_to_all(blocks, EVERY, split_axis=0, concat_axis=0, axis_index_groups=groups, tiled=True)


def call(body, out_shape, in_specs, out_specs, scratch=()):
    return pl.pallas_call(
        body,
        out_shape=out_shape,
        in_specs=in_specs,
        out_specs=out_specs,
        scratch_shapes=list(scratch),
        compiler_params=pltpu.CompilerParams(vmem_limit_bytes=VMEM),
    )


def vmem():
    return pl.BlockSpec(memory_space=pltpu.VMEM)


def anywhere():
    return pl.BlockSpec(memory_space=pl.ANY)


def hbm():
    return pl.BlockSpec(memory_space=pltpu.HBM)


def smem():
    return pl.BlockSpec(memory_space=pltpu.SMEM)


def unit(values):
    wide = values.astype(F32)
    return (wide * lax.rsqrt(jnp.sum(wide * wide, axis=-1, keepdims=True) + 1e-06)).astype(BF16)


def iota(shape, dim):
    return lax.broadcasted_iota(I32, shape, dim)


def dot(a, b, dims, precision=None):
    return lax.dot_general(a, b, ((dims[0], dims[1]), ((), ())), precision=precision, preferred_element_type=F32)


def token_sum_matrix():
    return (iota((QROWS, QROWS), 0) // QT == iota((QROWS, QROWS), 1) // QT).astype(F32)


def fetch(pairs, sems):
    copies = [pltpu.make_async_copy(src, dst, sems.at[i]) for i, (src, dst) in enumerate(pairs)]
    for copy in copies:
        copy.start()
    return copies


def position():
    holder = lax.axis_index("dp")
    spot, core = holder // N_C, holder % N_C
    source = jnp.where(core == 0, spot, (spot % N_Y) * N_Z + spot // N_Y)
    return spot, core, source


def prepare(table_in, queries_in, sent, q_unit, table, queries, sems, count):
    pairs = [(table_in, table), (queries_in, queries)]
    for copy in fetch(pairs, sems):
        copy.wait()
    tiles = unit(queries[...])
    q_unit[...] = tiles
    homes = []
    for q in range(QD):
        for k in range(NEG):
            passage = table[PASSAGE_ROWS + q, k]
            home = table[passage // 128, passage % 128]
            owner = home // ROWS
            lane_of = (owner % N_C) * SPOTS + owner // N_C
            count[lane_of] = 0
            homes.append((lane_of, q * ROWS + home % ROWS + 1))
    lane = iota((8, N_DP), 1)
    sub = iota((8, N_DP), 0)
    codes = jnp.zeros((8, N_DP), F32)
    for lane_of, code in homes:
        rank = count[lane_of]
        count[lane_of] = rank + 1
        codes = jnp.where((lane == lane_of) & (sub == rank), code.astype(F32), codes)
    for copy in range(N_Y):
        sent[copy, 0:QROWS, :] = tiles.reshape(QROWS, D)
        sent[copy, QROWS:SENT, :] = codes.astype(BF16)


def normalize(values, out):
    out[...] = unit(values[...])


def positive_scores(q_unit, gathered):
    cands = gathered[...].reshape(BATCH * PT, D)
    exp_scores = jnp.exp(10.0 * dot(cands, q_unit, ((1,), (1,)))).reshape(BATCH, PT, QROWS)
    total = jnp.sum(exp_scores, axis=1)
    score = 0.1 * dot(jnp.log(total), token_sum_matrix(), ((1,), (0,)), EXACT)
    return cands, exp_scores, total, score


def positive_weight(q_tiles, positives, gathered, out):
    gathered[...] = unit(positives[...])
    score = positive_scores(q_tiles[...].reshape(QROWS, D), gathered)[3]
    out[...] = jnp.sum(jnp.exp(score), axis=0, keepdims=True)


def request(codes, source, slot):
    code = codes[slot // 2, source * 8 + slot % 2]
    spot = jnp.maximum(code - 1, 0)
    return code > 0, spot // ROWS, spot % ROWS


def passages(codes, own_rows, other_rows, source):
    picked = [request(codes, source, slot)[2] for slot in range(SLOTS)]
    return jnp.concatenate([own_rows[picked[0]], own_rows[picked[1]], other_rows[picked[2]], other_rows[picked[3]]], axis=0)


def asking(codes, asked, source):
    picked = [request(codes, source, slot)[1] for slot in range(SLOTS)]
    return jnp.concatenate([asked[source, pl.ds(pl.multiple_of(q * QT, QT), QT), :] for q in picked], axis=0)


def spread(packed):
    block = iota((PT, QROWS), 1) // QT
    return jnp.concatenate([jnp.where(block == b, packed, 0.0).astype(BF16) for b in range(SLOTS)], axis=0)


def for_sources(step):
    for first in range(0, SPOTS, 8):
        lax.fori_loop(first, first + 8, step, 0, unroll=8)


def read_codes(asked, table, codes, sem):
    spot, core, _ = position()
    rows = asked[:, QROWS:SENT, :].reshape(SPOTS * 8, N_DP)
    which = iota((8, N_DP), 0)
    lane = jnp.where(which == 0, core * SPOTS + spot, (1 - core) * SPOTS + spot)
    pick = ((iota((8, N_DP), 1) == lane) & (which < 2)).astype(F32).astype(BF16)
    table[...] = dot(pick, rows, ((1,), (1,))).astype(I32)
    copy = pltpu.make_async_copy(table, codes, sem)
    copy.start()
    copy.wait()


def exponentials(codes, asked, own_rows, other_rows, source):
    block = iota((PT, QROWS), 1) // QT
    full = dot(passages(codes, own_rows, other_rows, source), asking(codes, asked, source), ((1,), (1,)))
    packed = full[0:PT]
    for b in range(1, SLOTS):
        packed = jnp.where(block == b, full[b * PT : (b + 1) * PT], packed)
    return jnp.exp(10.0 * packed)


def score(asked, own_rows, other_rows, pos_weight, factor, sums, table, totals, marks, codes, sem):
    read_codes(asked, table, codes, sem)
    source_here = position()[2]
    lane = iota((1, QROWS), 1)

    def one(source, carry):
        mark = jnp.full((1, QROWS), -1.0, F32)
        for b in range(SLOTS):
            valid, q, _ = request(codes, source, b)
            mark = jnp.where((lane // QT == b) & valid, q.astype(F32), mark)
        exp_scores = exponentials(codes, asked, own_rows, other_rows, source)
        totals[pl.ds(source, 1), :] = jnp.sum(exp_scores, axis=0, keepdims=True)
        marks[pl.ds(source, 1), :] = mark
        return carry

    for_sources(one)

    total = totals[...]
    mark = marks[...]
    weight = jnp.exp(0.1 * dot(jnp.log(total), token_sum_matrix(), ((1,), (0,)), EXACT))
    weight = jnp.where(mark >= 0.0, weight, 0.0)
    factor[...] = weight / total
    first = iota((SPOTS, QROWS), 1) % QT == 0
    pad = jnp.zeros((QROWS - SPOTS, QROWS), F32)
    ones = jnp.ones((8, QROWS), F32)
    parts = []
    for q in range(QD):
        mine = jnp.where((mark == float(q)) & first, weight, 0.0)
        part = dot(ones, jnp.concatenate([mine, pad], axis=0), ((1,), (1,)), EXACT)[0:1]
        own = jnp.sum(jnp.where(lane == q * QT, pos_weight[...], 0.0), axis=1, keepdims=True)
        parts.append(part + jnp.where(lane == source_here, own, 0.0))
    sums[...] = jnp.broadcast_to(jnp.concatenate(parts, axis=0)[None], (SPOTS, QD, QROWS))


def terms(codes, asked, own_rows, other_rows, factor, probs, back):
    def one(source, carry):
        packed = exponentials(codes, asked, own_rows, other_rows, source) * factor[pl.ds(source, 1), :]
        probs[source] = packed.astype(BF16)
        grads = dot(spread(packed), passages(codes, own_rows, other_rows, source), ((0,), (0,)))
        picked = [request(codes, source, slot)[1] for slot in range(SLOTS)]
        for q in range(QD):
            total = jnp.zeros((QT, D), F32)
            for b in range(SLOTS):
                total += grads[b * QT : (b + 1) * QT] * (picked[b] == q).astype(F32)
            back[source, q * QT : (q + 1) * QT, :] = total.astype(BF16)
        return carry

    for_sources(one)


def weigh(
    codes, sums, asked, probs, q_in, gathered_in, own_grad, other_grad, pos_grad, query_part, losses, weight_inv,
    other_acc, inverse, q_tiles, gathered, sems,
):
    later = fetch([(q_in, q_tiles), (gathered_in, gathered)], sems)
    weight_sum = jnp.sum(sums[...], axis=0)
    inverse[...] = jnp.zeros_like(inverse)
    inverse[0:QD] = 1.0 / weight_sum
    copy = pltpu.make_async_copy(inverse, weight_inv, sems.at[2])
    copy.start()
    own_grad[...] = jnp.zeros_like(own_grad)
    other_acc[...] = jnp.zeros_like(other_acc)
    copy.wait()

    def add(source, carry):
        grads = dot(spread(probs[source].astype(F32)), asking(codes, asked, source), ((1,), (0,)))
        for b in range(SLOTS):
            _, q, row = request(codes, source, b)
            acc = own_grad if b < 2 else other_acc
            acc[row] += grads[b * PT : (b + 1) * PT] * weight_inv[q, source]
        return carry

    for_sources(add)
    other_grad[...] = other_acc[...].astype(BF16)

    for copy in later:
        copy.wait()
    q_unit = q_tiles[...].reshape(QROWS, D)
    cands, exp_scores, total, scores = positive_scores(q_unit, gathered)
    lane = iota((1, QROWS), 1)
    mine = jnp.sum(jnp.where(lane == position()[2], weight_sum, 0.0), axis=1, keepdims=True)
    own_sum = jnp.zeros((1, QROWS), F32)
    for q in range(QD):
        own_sum = jnp.where(lane // QT == q, mine[q : q + 1], own_sum)
    own = (iota((BATCH, QROWS), 0) == lax.axis_index("group") * QD + iota((BATCH, QROWS), 1) // QT).astype(F32)
    score_grad = jnp.exp(scores) / own_sum - own
    losses[...] = jnp.log(own_sum) - jnp.sum(scores * own, axis=0, keepdims=True)
    weight_grad = (exp_scores * (score_grad / total)[:, None, :]).astype(BF16).reshape(BATCH * PT, QROWS)
    query_part[...] = dot(weight_grad, cands, ((0,), (0,)))
    pos_grad[...] = dot(weight_grad, q_unit, ((1,), (0,))).reshape(BATCH, PT, D)


def split(own_grad, moved, pos_grad, kept, off1, off2, off3):
    share = ROWS // GROUP
    for ahead, out in enumerate((kept, off1, off2, off3)):
        g = (lax.axis_index("group") + ahead) % GROUP
        out[0:QD] = pos_grad[pl.ds(g * QD, QD)].astype(out.dtype)
        rows = pl.ds(g * share, share)
        out[QD:] = (own_grad[rows] + moved[rows].astype(F32)).astype(out.dtype)


def add_blocks(arrived, first, second, out):
    del first, second
    for part in range(N_Y):
        out[part] = jnp.sum(arrived[:, part].astype(F32), axis=0).astype(BF16)


def collect(weight_inv, query_part, arrived, out):
    source = position()[2]
    total = jnp.sum(arrived[...].astype(F32), axis=0)
    for q in range(QD):
        rows = slice(q * QT, (q + 1) * QT)
        out[q] = query_part[rows, :] + total[rows] * weight_inv[q, source]


def per_device(queries, positives, passage_pool, negative_ids, storage_row):
    struct = jax.ShapeDtypeStruct
    swap = [(h, h ^ 1) for h in range(N_DP)]
    tiles = struct((QD, QT, D), BF16)

    table = jnp.concatenate([storage_row.reshape(PASSAGE_ROWS, 128), jnp.pad(negative_ids, ((0, 4), (0, 121)))], axis=0)
    sent, q_unit = call(
        prepare,
        (struct((N_Y, SENT, D), BF16), tiles),
        [hbm()] * 2,
        (vmem(), vmem()),
        [
            pltpu.SMEM(table.shape, I32),
            pltpu.VMEM((QD, QT, D), BF16),
            pltpu.SemaphoreType.DMA((2,)),
            pltpu.SMEM((N_DP,), I32),
        ],
    )(table, queries)
    asked = exchange(sent, along(1))
    asked = exchange(jnp.broadcast_to(asked[None], (N_Z, N_Y, SENT, D)), along(0)).reshape(SPOTS, SENT, D)

    own_rows = call(normalize, struct((ROWS, PT, D), BF16), [vmem()], vmem())(passage_pool)
    other_rows = lax.ppermute(own_rows, "dp", swap)
    gathered = lax.all_gather(positives, "group", axis=0, tiled=True)
    gathered, pos_weight = call(
        positive_weight, (struct((BATCH, PT, D), BF16), struct((1, QROWS), F32)), [vmem(), vmem()], (vmem(), vmem())
    )(q_unit, gathered)

    factor, sums, codes = call(
        score,
        (
            struct((SPOTS, QROWS), F32),
            struct((SPOTS, QD, QROWS), F32),
            struct((8, SPOTS * 8), I32),
        ),
        [vmem(), vmem(), vmem(), vmem()],
        (vmem(), vmem(), vmem()),
        [
            pltpu.VMEM((SPOTS, QROWS), F32),
            pltpu.VMEM((SPOTS, QROWS), F32),
            pltpu.SMEM((8, SPOTS * 8), I32),
            pltpu.SemaphoreType.DMA,
        ],
    )(asked, own_rows, other_rows, pos_weight)
    sums = exchange(sums, planes())

    probs, back = call(
        terms,
        (struct((SPOTS, PT, QROWS), BF16), struct((SPOTS, QROWS, D), BF16)),
        [smem()] + [vmem()] * 4,
        (vmem(), vmem()),
    )(codes, asked, own_rows, other_rows, factor)
    arrived = exchange(back.reshape(N_Z, N_Y, QROWS, D), along(0))

    own_grad, other_grad, pos_grad, query_part, losses, weight_inv = call(
        weigh,
        (
            struct((ROWS, PT, D), F32),
            struct((ROWS, PT, D), BF16),
            struct((BATCH, PT, D), F32),
            struct((QROWS, D), F32),
            struct((1, QROWS), F32),
            struct((8, QROWS), F32),
        ),
        [smem(), vmem(), vmem(), vmem(), hbm(), hbm()],
        (vmem(),) * 5 + (smem(),),
        [
            pltpu.VMEM((ROWS, PT, D), F32),
            pltpu.VMEM((8, QROWS), F32),
            pltpu.VMEM((QD, QT, D), BF16),
            pltpu.VMEM((BATCH, PT, D), BF16),
            pltpu.SemaphoreType.DMA((3,)),
        ],
    )(codes, sums, asked, probs, q_unit, gathered)

    block = (QD + ROWS // GROUP, PT, D)
    kept, off1, off2, off3 = call(
        split,
        (struct(block, F32), struct(block, BF16), struct(block, BF16), struct(block, BF16)),
        [vmem(), vmem(), vmem()],
        (vmem(),) * 4,
    )(own_grad, lax.ppermute(other_grad, "dp", swap), pos_grad)
    moved = [
        lax.ppermute(part, "group", [(g, (g + ahead) % GROUP) for g in range(GROUP)])
        for ahead, part in ((2, off2), (1, off1), (3, off3))
    ]
    arrived = call(
        add_blocks, struct((N_Y, QROWS, D), BF16), [vmem(), anywhere(), anywhere()], vmem()
    )(arrived, moved[0], moved[1])
    arrived = exchange(arrived, along(1))
    query_grad = call(
        collect, struct((QD, QT, D), F32), [smem(), vmem(), vmem()], vmem()
    )(weight_inv, query_part, arrived)
    total = kept + moved[0].astype(F32) + moved[1].astype(F32) + moved[2].astype(F32)
    return losses.reshape(QD, QT)[:, 0], query_grad, total[:QD], total[QD:]


def solution(mesh):
    in_specs = (P(EVERY), P(EVERY), P("dp"), P(EVERY), P())
    out_specs = (P(EVERY), P(EVERY), P(EVERY), P(EVERY))
    return jax.shard_map(per_device, mesh=mesh, in_specs=in_specs, out_specs=out_specs, check_vma=False)
```

```python
import jax
import jax.numpy as jnp
from jax import lax
from jax.experimental import pallas as pl
from jax.experimental.pallas import tpu as pltpu
from jax.sharding import PartitionSpec as P

N_Z, N_Y, N_C, GROUP = 8, 8, 2, 4
N_DP = N_Z * N_Y * N_C
SPOTS = N_Z * N_Y
QD, QT, PT, D, NEG, ROWS = 4, 32, 64, 128, 7, 32
QROWS = QD * QT
PASSAGE_ROWS = 4096 // 128
SENT = QROWS + 8
BATCH = QD * GROUP
SLOTS = 4
VMEM = 6 * 1024 * 1024
F32, BF16, I32 = jnp.float32, jnp.bfloat16, jnp.int32
EXACT = lax.Precision.HIGHEST
EVERY = ("dp", "group")
DOWN = range(N_Z - 1, -1, -1)


def device(z, y, c, x):
    return ((z * N_Y + y) * N_C + c) * GROUP + x


def along(z_core):
    z_lines = [[device(z, y, z_core, x) for z in DOWN] for y in range(N_Y) for x in range(GROUP)]
    y_lines = [[device(z, y, 1 - z_core, x) for y in range(N_Y)] for z in range(N_Z) for x in range(GROUP)]
    return z_lines + y_lines


def planes():
    first = [[device(z, y, 0, x) for z in DOWN for y in range(N_Y)] for x in range(GROUP)]
    second = [[device(z, y, 1, x) for y in range(N_Y) for z in DOWN] for x in range(GROUP)]
    return first + second


def exchange(blocks, groups):
    return lax.all_to_all(blocks, EVERY, split_axis=0, concat_axis=0, axis_index_groups=groups, tiled=True)


def call(body, out_shape, in_specs, out_specs, scratch=()):
    return pl.pallas_call(
        body,
        out_shape=out_shape,
        in_specs=in_specs,
        out_specs=out_specs,
        scratch_shapes=list(scratch),
        compiler_params=pltpu.CompilerParams(vmem_limit_bytes=VMEM),
    )


def vmem():
    return pl.BlockSpec(memory_space=pltpu.VMEM)


def anywhere():
    return pl.BlockSpec(memory_space=pl.ANY)


def hbm():
    return pl.BlockSpec(memory_space=pltpu.HBM)


def smem():
    return pl.BlockSpec(memory_space=pltpu.SMEM)


def unit(values):
    wide = values.astype(F32)
    return (wide * lax.rsqrt(jnp.sum(wide * wide, axis=-1, keepdims=True) + 1e-06)).astype(BF16)


def iota(shape, dim):
    return lax.broadcasted_iota(I32, shape, dim)


def dot(a, b, dims, precision=None):
    return lax.dot_general(a, b, ((dims[0], dims[1]), ((), ())), precision=precision, preferred_element_type=F32)


def token_sum_matrix():
    return (iota((QROWS, QROWS), 0) // QT == iota((QROWS, QROWS), 1) // QT).astype(F32)


def fetch(pairs, sems):
    copies = [pltpu.make_async_copy(src, dst, sems.at[i]) for i, (src, dst) in enumerate(pairs)]
    for copy in copies:
        copy.start()
    return copies


def position():
    holder = lax.axis_index("dp")
    spot, core = holder // N_C, holder % N_C
    z, y = N_Z - 1 - spot // N_Y, spot % N_Y
    source = jnp.where(core == 0, z * N_Y + y, y * N_Z + z)
    return spot, core, source


def prepare(table_in, queries_in, sent, q_unit, table, queries, sems, count):
    pairs = [(table_in, table), (queries_in, queries)]
    for copy in fetch(pairs, sems):
        copy.wait()
    tiles = unit(queries[...])
    q_unit[...] = tiles
    homes = []
    for q in range(QD):
        for k in range(NEG):
            passage = table[PASSAGE_ROWS + q, k]
            home = table[passage // 128, passage % 128]
            owner = home // ROWS
            lane_of = (owner % N_C) * SPOTS + owner // N_C
            count[lane_of] = 0
            homes.append((lane_of, q * ROWS + home % ROWS + 1))
    lane = iota((8, N_DP), 1)
    sub = iota((8, N_DP), 0)
    codes = jnp.zeros((8, N_DP), F32)
    for lane_of, code in homes:
        rank = count[lane_of]
        count[lane_of] = rank + 1
        codes = jnp.where((lane == lane_of) & (sub == rank), code.astype(F32), codes)
    for copy in range(N_Y):
        sent[copy, 0:QROWS, :] = tiles.reshape(QROWS, D)
        sent[copy, QROWS:SENT, :] = codes.astype(BF16)


def normalize(values, out):
    out[...] = unit(values[...])


def positive_scores(q_unit, gathered):
    cands = gathered[...].reshape(BATCH * PT, D)
    exp_scores = jnp.exp(10.0 * dot(cands, q_unit, ((1,), (1,)))).reshape(BATCH, PT, QROWS)
    total = jnp.sum(exp_scores, axis=1)
    score = 0.1 * dot(jnp.log(total), token_sum_matrix(), ((1,), (0,)), EXACT)
    return cands, exp_scores, total, score


def positive_weight(q_tiles, positives, gathered, out):
    gathered[...] = unit(positives[...])
    score = positive_scores(q_tiles[...].reshape(QROWS, D), gathered)[3]
    out[...] = jnp.sum(jnp.exp(score), axis=0, keepdims=True)


def request(codes, source, slot):
    code = codes[slot // 2, source * 8 + slot % 2]
    spot = jnp.maximum(code - 1, 0)
    return code > 0, spot // ROWS, spot % ROWS


def passages(codes, own_rows, other_rows, source):
    picked = [request(codes, source, slot)[2] for slot in range(SLOTS)]
    return jnp.concatenate([own_rows[picked[0]], own_rows[picked[1]], other_rows[picked[2]], other_rows[picked[3]]], axis=0)


def asking(codes, asked, source):
    picked = [request(codes, source, slot)[1] for slot in range(SLOTS)]
    return jnp.concatenate([asked[source, pl.ds(pl.multiple_of(q * QT, QT), QT), :] for q in picked], axis=0)


def spread(packed):
    block = iota((PT, QROWS), 1) // QT
    return jnp.concatenate([jnp.where(block == b, packed, 0.0).astype(BF16) for b in range(SLOTS)], axis=0)


def for_sources(step):
    for first in range(0, SPOTS, 8):
        lax.fori_loop(first, first + 8, step, 0, unroll=8)


def read_codes(asked, table, codes, sem):
    spot, core, _ = position()
    rows = asked[:, QROWS:SENT, :].reshape(SPOTS * 8, N_DP)
    which = iota((8, N_DP), 0)
    lane = jnp.where(which == 0, core * SPOTS + spot, (1 - core) * SPOTS + spot)
    pick = ((iota((8, N_DP), 1) == lane) & (which < 2)).astype(F32).astype(BF16)
    table[...] = dot(pick, rows, ((1,), (1,))).astype(I32)
    copy = pltpu.make_async_copy(table, codes, sem)
    copy.start()
    copy.wait()


def exponentials(codes, asked, own_rows, other_rows, source):
    block = iota((PT, QROWS), 1) // QT
    full = dot(passages(codes, own_rows, other_rows, source), asking(codes, asked, source), ((1,), (1,)))
    packed = full[0:PT]
    for b in range(1, SLOTS):
        packed = jnp.where(block == b, full[b * PT : (b + 1) * PT], packed)
    return jnp.exp(10.0 * packed)


def score(asked, own_rows, other_rows, pos_weight, factor, sums, table, totals, marks, codes, sem):
    read_codes(asked, table, codes, sem)
    source_here = position()[2]
    lane = iota((1, QROWS), 1)

    def one(source, carry):
        mark = jnp.full((1, QROWS), -1.0, F32)
        for b in range(SLOTS):
            valid, q, _ = request(codes, source, b)
            mark = jnp.where((lane // QT == b) & valid, q.astype(F32), mark)
        exp_scores = exponentials(codes, asked, own_rows, other_rows, source)
        totals[pl.ds(source, 1), :] = jnp.sum(exp_scores, axis=0, keepdims=True)
        marks[pl.ds(source, 1), :] = mark
        return carry

    for_sources(one)

    total = totals[...]
    mark = marks[...]
    weight = jnp.exp(0.1 * dot(jnp.log(total), token_sum_matrix(), ((1,), (0,)), EXACT))
    weight = jnp.where(mark >= 0.0, weight, 0.0)
    factor[...] = weight / total
    first = iota((SPOTS, QROWS), 1) % QT == 0
    pad = jnp.zeros((QROWS - SPOTS, QROWS), F32)
    ones = jnp.ones((8, QROWS), F32)
    parts = []
    for q in range(QD):
        mine = jnp.where((mark == float(q)) & first, weight, 0.0)
        part = dot(ones, jnp.concatenate([mine, pad], axis=0), ((1,), (1,)), EXACT)[0:1]
        own = jnp.sum(jnp.where(lane == q * QT, pos_weight[...], 0.0), axis=1, keepdims=True)
        parts.append(part + jnp.where(lane == source_here, own, 0.0))
    sums[...] = jnp.broadcast_to(jnp.concatenate(parts, axis=0)[None], (SPOTS, QD, QROWS))


def terms(codes, asked, own_rows, other_rows, factor, probs, back):
    def one(source, carry):
        packed = exponentials(codes, asked, own_rows, other_rows, source) * factor[pl.ds(source, 1), :]
        probs[source] = packed.astype(BF16)
        grads = dot(spread(packed), passages(codes, own_rows, other_rows, source), ((0,), (0,)))
        picked = [request(codes, source, slot)[1] for slot in range(SLOTS)]
        for q in range(QD):
            total = jnp.zeros((QT, D), F32)
            for b in range(SLOTS):
                total += grads[b * QT : (b + 1) * QT] * (picked[b] == q).astype(F32)
            back[source, q * QT : (q + 1) * QT, :] = total.astype(BF16)
        return carry

    for_sources(one)


def weigh(
    codes, sums, asked, probs, q_in, gathered_in, own_grad, other_grad, pos_grad, query_part, losses, weight_inv,
    other_acc, inverse, q_tiles, gathered, sems,
):
    later = fetch([(q_in, q_tiles), (gathered_in, gathered)], sems)
    weight_sum = jnp.sum(sums[...], axis=0)
    inverse[...] = jnp.zeros_like(inverse)
    inverse[0:QD] = 1.0 / weight_sum
    copy = pltpu.make_async_copy(inverse, weight_inv, sems.at[2])
    copy.start()
    own_grad[...] = jnp.zeros_like(own_grad)
    other_acc[...] = jnp.zeros_like(other_acc)
    copy.wait()

    def add(source, carry):
        grads = dot(spread(probs[source].astype(F32)), asking(codes, asked, source), ((1,), (0,)))
        for b in range(SLOTS):
            _, q, row = request(codes, source, b)
            acc = own_grad if b < 2 else other_acc
            acc[row] += grads[b * PT : (b + 1) * PT] * weight_inv[q, source]
        return carry

    for_sources(add)
    other_grad[...] = other_acc[...].astype(BF16)

    for copy in later:
        copy.wait()
    q_unit = q_tiles[...].reshape(QROWS, D)
    cands, exp_scores, total, scores = positive_scores(q_unit, gathered)
    lane = iota((1, QROWS), 1)
    mine = jnp.sum(jnp.where(lane == position()[2], weight_sum, 0.0), axis=1, keepdims=True)
    own_sum = jnp.zeros((1, QROWS), F32)
    for q in range(QD):
        own_sum = jnp.where(lane // QT == q, mine[q : q + 1], own_sum)
    own = (iota((BATCH, QROWS), 0) == lax.axis_index("group") * QD + iota((BATCH, QROWS), 1) // QT).astype(F32)
    score_grad = jnp.exp(scores) / own_sum - own
    loss = jnp.log(own_sum) - jnp.sum(scores * own, axis=0, keepdims=True)
    for q in range(QD):
        losses[q] = jnp.sum(jnp.where(lane == q * QT, loss, 0.0))
    weight_grad = (exp_scores * (score_grad / total)[:, None, :]).astype(BF16).reshape(BATCH * PT, QROWS)
    query_part[...] = dot(weight_grad, cands, ((0,), (0,)))
    pos_grad[...] = dot(weight_grad, q_unit, ((1,), (0,))).reshape(BATCH, PT, D)


def split(own_grad, moved, pos_grad, kept, off1, off2, off3):
    share = ROWS // GROUP
    for ahead, out in enumerate((kept, off1, off2, off3)):
        g = (lax.axis_index("group") + ahead) % GROUP
        out[0:QD] = pos_grad[pl.ds(g * QD, QD)].astype(out.dtype)
        rows = pl.ds(g * share, share)
        out[QD:] = (own_grad[rows] + moved[rows].astype(F32)).astype(out.dtype)


def add_blocks(arrived, first, second, third, out):
    del first, second, third
    for part in range(N_Y):
        out[part] = jnp.sum(arrived[:, part].astype(F32), axis=0).astype(BF16)


def collect(weight_inv, query_part, arrived, out):
    source = position()[2]
    total = jnp.sum(arrived[...].astype(F32), axis=0)
    for q in range(QD):
        rows = slice(q * QT, (q + 1) * QT)
        out[q] = query_part[rows, :] + total[rows] * weight_inv[q, source]


def per_device(queries, positives, passage_pool, negative_ids, storage_row):
    struct = jax.ShapeDtypeStruct
    swap = [(h, h ^ 1) for h in range(N_DP)]
    tiles = struct((QD, QT, D), BF16)

    table = jnp.concatenate([storage_row.reshape(PASSAGE_ROWS, 128), jnp.pad(negative_ids, ((0, 4), (0, 121)))], axis=0)
    sent, q_unit = call(
        prepare,
        (struct((N_Y, SENT, D), BF16), tiles),
        [hbm()] * 2,
        (vmem(), vmem()),
        [
            pltpu.SMEM(table.shape, I32),
            pltpu.VMEM((QD, QT, D), BF16),
            pltpu.SemaphoreType.DMA((2,)),
            pltpu.SMEM((N_DP,), I32),
        ],
    )(table, queries)
    asked = exchange(sent, along(1))
    asked = exchange(jnp.broadcast_to(asked[None], (N_Z, N_Y, SENT, D)), along(0)).reshape(SPOTS, SENT, D)

    own_rows = call(normalize, struct((ROWS, PT, D), BF16), [vmem()], vmem())(passage_pool)
    other_rows = lax.ppermute(own_rows, "dp", swap)
    gathered = lax.all_gather(positives, "group", axis=0, tiled=True)
    gathered, pos_weight = call(
        positive_weight, (struct((BATCH, PT, D), BF16), struct((1, QROWS), F32)), [vmem(), vmem()], (vmem(), vmem())
    )(q_unit, gathered)

    factor, sums, codes = call(
        score,
        (
            struct((SPOTS, QROWS), F32),
            struct((SPOTS, QD, QROWS), F32),
            struct((8, SPOTS * 8), I32),
        ),
        [vmem(), vmem(), vmem(), vmem()],
        (vmem(), vmem(), vmem()),
        [
            pltpu.VMEM((SPOTS, QROWS), F32),
            pltpu.VMEM((SPOTS, QROWS), F32),
            pltpu.SMEM((8, SPOTS * 8), I32),
            pltpu.SemaphoreType.DMA,
        ],
    )(asked, own_rows, other_rows, pos_weight)
    sums = exchange(sums, planes())

    probs, back = call(
        terms,
        (struct((SPOTS, PT, QROWS), BF16), struct((SPOTS, QROWS, D), BF16)),
        [smem()] + [vmem()] * 4,
        (vmem(), vmem()),
    )(codes, asked, own_rows, other_rows, factor)
    arrived = exchange(back.reshape(N_Z, N_Y, QROWS, D), along(0))

    own_grad, other_grad, pos_grad, query_part, losses, weight_inv = call(
        weigh,
        (
            struct((ROWS, PT, D), F32),
            struct((ROWS, PT, D), BF16),
            struct((BATCH, PT, D), F32),
            struct((QROWS, D), F32),
            struct((QD,), F32),
            struct((8, QROWS), F32),
        ),
        [smem(), vmem(), vmem(), vmem(), hbm(), hbm()],
        (vmem(),) * 4 + (smem(),) * 2,
        [
            pltpu.VMEM((ROWS, PT, D), F32),
            pltpu.VMEM((8, QROWS), F32),
            pltpu.VMEM((QD, QT, D), BF16),
            pltpu.VMEM((BATCH, PT, D), BF16),
            pltpu.SemaphoreType.DMA((3,)),
        ],
    )(codes, sums, asked, probs, q_unit, gathered)

    block = (QD + ROWS // GROUP, PT, D)
    kept, off1, off2, off3 = call(
        split,
        (struct(block, F32), struct(block, BF16), struct(block, BF16), struct(block, BF16)),
        [vmem(), vmem(), vmem()],
        (vmem(),) * 4,
    )(own_grad, lax.ppermute(other_grad, "dp", swap), pos_grad)
    moved = [
        lax.ppermute(part, "group", [(g, (g + ahead) % GROUP) for g in range(GROUP)])
        for ahead, part in ((2, off2), (1, off1), (3, off3))
    ]
    arrived = call(
        add_blocks, struct((N_Y, QROWS, D), BF16), [vmem(), anywhere(), anywhere(), anywhere()], vmem()
    )(arrived, *moved)
    arrived = exchange(arrived, along(1))
    query_grad = call(
        collect, struct((QD, QT, D), F32), [smem(), vmem(), vmem()], vmem()
    )(weight_inv, query_part, arrived)
    total = kept + moved[0].astype(F32) + moved[1].astype(F32) + moved[2].astype(F32)
    return losses, query_grad, total[:QD], total[QD:]


def solution(mesh):
    in_specs = (P(EVERY), P(EVERY), P("dp"), P(EVERY), P())
    out_specs = (P(EVERY), P(EVERY), P(EVERY), P(EVERY))
    return jax.shard_map(per_device, mesh=mesh, in_specs=in_specs, out_specs=out_specs, check_vma=False)
```

```python
import jax
import jax.numpy as jnp
from jax import lax
from jax.experimental import pallas as pl
from jax.experimental.pallas import tpu as pltpu
from jax.sharding import PartitionSpec as P

N_Z, N_Y, N_C, GROUP = 8, 8, 2, 4
N_DP = N_Z * N_Y * N_C
SPOTS = N_Z * N_Y
QD, QT, PT, D, NEG, ROWS = 4, 32, 64, 128, 7, 32
QROWS = QD * QT
PASSAGE_ROWS = 4096 // 128
SENT = QROWS + 8
BATCH = QD * GROUP
SLOTS = 4
VMEM = 6 * 1024 * 1024
F32, BF16, I32 = jnp.float32, jnp.bfloat16, jnp.int32
EXACT = lax.Precision.HIGHEST
EVERY = ("dp", "group")
DOWN = range(N_Z - 1, -1, -1)


def device(z, y, c, x):
    return ((z * N_Y + y) * N_C + c) * GROUP + x


def along(z_core):
    z_lines = [[device(z, y, z_core, x) for z in DOWN] for y in range(N_Y) for x in range(GROUP)]
    y_lines = [[device(z, y, 1 - z_core, x) for y in range(N_Y)] for z in range(N_Z) for x in range(GROUP)]
    return z_lines + y_lines


def planes():
    first = [[device(z, y, 0, x) for z in DOWN for y in range(N_Y)] for x in range(GROUP)]
    second = [[device(z, y, 1, x) for y in range(N_Y) for z in DOWN] for x in range(GROUP)]
    return first + second


def exchange(blocks, groups):
    return lax.all_to_all(blocks, EVERY, split_axis=0, concat_axis=0, axis_index_groups=groups, tiled=True)


def call(body, out_shape, in_specs, out_specs, scratch=()):
    return pl.pallas_call(
        body,
        out_shape=out_shape,
        in_specs=in_specs,
        out_specs=out_specs,
        scratch_shapes=list(scratch),
        compiler_params=pltpu.CompilerParams(vmem_limit_bytes=VMEM),
    )


def vmem():
    return pl.BlockSpec(memory_space=pltpu.VMEM)


def anywhere():
    return pl.BlockSpec(memory_space=pl.ANY)


def hbm():
    return pl.BlockSpec(memory_space=pltpu.HBM)


def smem():
    return pl.BlockSpec(memory_space=pltpu.SMEM)


def unit(values):
    wide = values.astype(F32)
    return (wide * lax.rsqrt(jnp.sum(wide * wide, axis=-1, keepdims=True) + 1e-06)).astype(BF16)


def iota(shape, dim):
    return lax.broadcasted_iota(I32, shape, dim)


def dot(a, b, dims, precision=None):
    return lax.dot_general(a, b, ((dims[0], dims[1]), ((), ())), precision=precision, preferred_element_type=F32)


def token_sum_matrix():
    return (iota((QROWS, QROWS), 0) // QT == iota((QROWS, QROWS), 1) // QT).astype(F32)


def fetch(pairs, sems):
    copies = [pltpu.make_async_copy(src, dst, sems.at[i]) for i, (src, dst) in enumerate(pairs)]
    for copy in copies:
        copy.start()
    return copies


def position():
    holder = lax.axis_index("dp")
    spot, core = holder // N_C, holder % N_C
    z, y = N_Z - 1 - spot // N_Y, spot % N_Y
    source = jnp.where(core == 0, z * N_Y + y, y * N_Z + z)
    return spot, core, source


def prepare(table_in, queries_in, sent, q_unit, table, queries, sems, count):
    pairs = [(table_in, table), (queries_in, queries)]
    for copy in fetch(pairs, sems):
        copy.wait()
    tiles = unit(queries[...])
    q_unit[...] = tiles
    homes = []
    for q in range(QD):
        for k in range(NEG):
            passage = table[PASSAGE_ROWS + q, k]
            home = table[passage // 128, passage % 128]
            owner = home // ROWS
            lane_of = (owner % N_C) * SPOTS + owner // N_C
            count[lane_of] = 0
            homes.append((lane_of, q * ROWS + home % ROWS + 1))
    lane = iota((8, N_DP), 1)
    sub = iota((8, N_DP), 0)
    codes = jnp.zeros((8, N_DP), F32)
    for lane_of, code in homes:
        rank = count[lane_of]
        count[lane_of] = rank + 1
        codes = jnp.where((lane == lane_of) & (sub == rank), code.astype(F32), codes)
    for copy in range(N_Y):
        sent[copy, 0:QROWS, :] = tiles.reshape(QROWS, D)
        sent[copy, QROWS:SENT, :] = codes.astype(BF16)


def normalize(values, out):
    out[...] = unit(values[...])


def positive_scores(q_unit, gathered):
    cands = gathered[...].reshape(BATCH * PT, D)
    exp_scores = jnp.exp(10.0 * dot(cands, q_unit, ((1,), (1,)))).reshape(BATCH, PT, QROWS)
    total = jnp.sum(exp_scores, axis=1)
    score = 0.1 * dot(jnp.log(total), token_sum_matrix(), ((1,), (0,)), EXACT)
    return cands, exp_scores, total, score


def positive_weight(q_tiles, positives, gathered, out):
    gathered[...] = unit(positives[...])
    score = positive_scores(q_tiles[...].reshape(QROWS, D), gathered)[3]
    out[...] = jnp.sum(jnp.exp(score), axis=0, keepdims=True)


def request(codes, source, slot):
    code = codes[slot // 2, source * 8 + slot % 2]
    spot = jnp.maximum(code - 1, 0)
    return code > 0, spot // ROWS, spot % ROWS


def passages(codes, own_rows, other_rows, source):
    picked = [request(codes, source, slot)[2] for slot in range(SLOTS)]
    return jnp.concatenate([own_rows[picked[0]], own_rows[picked[1]], other_rows[picked[2]], other_rows[picked[3]]], axis=0)


def asking(codes, asked, source):
    picked = [request(codes, source, slot)[1] for slot in range(SLOTS)]
    return jnp.concatenate([asked[source, pl.ds(pl.multiple_of(q * QT, QT), QT), :] for q in picked], axis=0)


def spread(packed):
    block = iota((PT, QROWS), 1) // QT
    return jnp.concatenate([jnp.where(block == b, packed, 0.0).astype(BF16) for b in range(SLOTS)], axis=0)


def for_sources(step):
    for first in range(0, SPOTS, 8):
        lax.fori_loop(first, first + 8, step, 0, unroll=8)


def read_codes(asked, table, codes, sem):
    spot, core, _ = position()
    rows = asked[:, QROWS:SENT, :].reshape(SPOTS * 8, N_DP)
    which = iota((8, N_DP), 0)
    lane = jnp.where(which == 0, core * SPOTS + spot, (1 - core) * SPOTS + spot)
    pick = ((iota((8, N_DP), 1) == lane) & (which < 2)).astype(F32).astype(BF16)
    table[...] = dot(pick, rows, ((1,), (1,))).astype(I32)
    copy = pltpu.make_async_copy(table, codes, sem)
    copy.start()
    copy.wait()


def exponentials(codes, asked, own_rows, other_rows, source):
    block = iota((PT, QROWS), 1) // QT
    full = dot(passages(codes, own_rows, other_rows, source), asking(codes, asked, source), ((1,), (1,)))
    packed = full[0:PT]
    for b in range(1, SLOTS):
        packed = jnp.where(block == b, full[b * PT : (b + 1) * PT], packed)
    return jnp.exp(10.0 * packed)


def score(asked, own_rows, other_rows, pos_weight, factor, sums, table, totals, marks, codes, sem):
    read_codes(asked, table, codes, sem)
    source_here = position()[2]
    lane = iota((1, QROWS), 1)

    def one(source, carry):
        mark = jnp.full((1, QROWS), -1.0, F32)
        for b in range(SLOTS):
            valid, q, _ = request(codes, source, b)
            mark = jnp.where((lane // QT == b) & valid, q.astype(F32), mark)
        exp_scores = exponentials(codes, asked, own_rows, other_rows, source)
        totals[pl.ds(source, 1), :] = jnp.sum(exp_scores, axis=0, keepdims=True)
        marks[pl.ds(source, 1), :] = mark
        return carry

    for_sources(one)

    total = totals[...]
    mark = marks[...]
    weight = jnp.exp(0.1 * dot(jnp.log(total), token_sum_matrix(), ((1,), (0,)), EXACT))
    weight = jnp.where(mark >= 0.0, weight, 0.0)
    factor[...] = weight / total
    first = iota((SPOTS, QROWS), 1) % QT == 0
    pad = jnp.zeros((QROWS - SPOTS, QROWS), F32)
    ones = jnp.ones((8, QROWS), F32)
    parts = []
    for q in range(QD):
        mine = jnp.where((mark == float(q)) & first, weight, 0.0)
        part = dot(ones, jnp.concatenate([mine, pad], axis=0), ((1,), (1,)), EXACT)[0:1]
        own = jnp.sum(jnp.where(lane == q * QT, pos_weight[...], 0.0), axis=1, keepdims=True)
        parts.append(part + jnp.where(lane == source_here, own, 0.0))
    sums[...] = jnp.broadcast_to(jnp.concatenate(parts, axis=0)[None], (SPOTS, QD, QROWS))


def terms(codes, asked, own_rows, other_rows, factor, probs, back):
    def one(source, carry):
        packed = exponentials(codes, asked, own_rows, other_rows, source) * factor[pl.ds(source, 1), :]
        probs[source] = packed.astype(BF16)
        grads = dot(spread(packed), passages(codes, own_rows, other_rows, source), ((0,), (0,)))
        picked = [request(codes, source, slot)[1] for slot in range(SLOTS)]
        for q in range(QD):
            total = jnp.zeros((QT, D), F32)
            for b in range(SLOTS):
                total += grads[b * QT : (b + 1) * QT] * (picked[b] == q).astype(F32)
            back[source, q * QT : (q + 1) * QT, :] = total.astype(BF16)
        return carry

    for_sources(one)


def weigh(codes, sums, asked, probs, own_grad, other_grad, own_sum, weight_inv, other_acc, inverse, sem):
    weight_sum = jnp.sum(sums[...], axis=0)
    inverse[...] = jnp.zeros_like(inverse)
    inverse[0:QD] = 1.0 / weight_sum
    copy = pltpu.make_async_copy(inverse, weight_inv, sem)
    copy.start()
    lane = iota((1, QROWS), 1)
    mine = jnp.sum(jnp.where(lane == position()[2], weight_sum, 0.0), axis=1, keepdims=True)
    spread_sum = jnp.zeros((1, QROWS), F32)
    for q in range(QD):
        spread_sum = jnp.where(lane // QT == q, mine[q : q + 1], spread_sum)
    own_sum[...] = spread_sum
    own_grad[...] = jnp.zeros_like(own_grad)
    other_acc[...] = jnp.zeros_like(other_acc)
    copy.wait()

    def add(source, carry):
        grads = dot(spread(probs[source].astype(F32)), asking(codes, asked, source), ((1,), (0,)))
        for b in range(SLOTS):
            _, q, row = request(codes, source, b)
            acc = own_grad if b < 2 else other_acc
            acc[row] += grads[b * PT : (b + 1) * PT] * weight_inv[q, source]
        return carry

    for_sources(add)
    other_grad[...] = other_acc[...].astype(BF16)


def weigh_positives(own_sum, q_tiles, gathered, pos_grad, query_part, losses):
    q_unit = q_tiles[...].reshape(QROWS, D)
    cands, exp_scores, total, scores = positive_scores(q_unit, gathered)
    lane = iota((1, QROWS), 1)
    own = (iota((BATCH, QROWS), 0) == lax.axis_index("group") * QD + iota((BATCH, QROWS), 1) // QT).astype(F32)
    score_grad = jnp.exp(scores) / own_sum[...] - own
    loss = jnp.log(own_sum[...]) - jnp.sum(scores * own, axis=0, keepdims=True)
    for q in range(QD):
        losses[q] = jnp.sum(jnp.where(lane == q * QT, loss, 0.0))
    weight_grad = (exp_scores * (score_grad / total)[:, None, :]).astype(BF16).reshape(BATCH * PT, QROWS)
    query_part[...] = dot(weight_grad, cands, ((0,), (0,)))
    pos_grad[...] = dot(weight_grad, q_unit, ((1,), (0,))).reshape(BATCH, PT, D)


def split(own_grad, moved, pos_grad, kept, off1, off2, off3):
    share = ROWS // GROUP
    for ahead, out in enumerate((kept, off1, off2, off3)):
        g = (lax.axis_index("group") + ahead) % GROUP
        out[0:QD] = pos_grad[pl.ds(g * QD, QD)].astype(out.dtype)
        rows = pl.ds(g * share, share)
        out[QD:] = (own_grad[rows] + moved[rows].astype(F32)).astype(out.dtype)


def add_blocks(arrived, first, second, out):
    del first, second
    for part in range(N_Y):
        out[part] = jnp.sum(arrived[:, part].astype(F32), axis=0).astype(BF16)


def collect(weight_inv, query_part, arrived, out):
    source = position()[2]
    total = jnp.sum(arrived[...].astype(F32), axis=0)
    for q in range(QD):
        rows = slice(q * QT, (q + 1) * QT)
        out[q] = query_part[rows, :] + total[rows] * weight_inv[q, source]


def per_device(queries, positives, passage_pool, negative_ids, storage_row):
    struct = jax.ShapeDtypeStruct
    swap = [(h, h ^ 1) for h in range(N_DP)]
    tiles = struct((QD, QT, D), BF16)

    table = jnp.concatenate([storage_row.reshape(PASSAGE_ROWS, 128), jnp.pad(negative_ids, ((0, 4), (0, 121)))], axis=0)
    sent, q_unit = call(
        prepare,
        (struct((N_Y, SENT, D), BF16), tiles),
        [hbm()] * 2,
        (vmem(), vmem()),
        [
            pltpu.SMEM(table.shape, I32),
            pltpu.VMEM((QD, QT, D), BF16),
            pltpu.SemaphoreType.DMA((2,)),
            pltpu.SMEM((N_DP,), I32),
        ],
    )(table, queries)
    asked = exchange(sent, along(1))
    asked = exchange(jnp.broadcast_to(asked[None], (N_Z, N_Y, SENT, D)), along(0)).reshape(SPOTS, SENT, D)

    own_rows = call(normalize, struct((ROWS, PT, D), BF16), [vmem()], vmem())(passage_pool)
    other_rows = lax.ppermute(own_rows, "dp", swap)
    gathered = lax.all_gather(positives, "group", axis=0, tiled=True)
    gathered, pos_weight = call(
        positive_weight, (struct((BATCH, PT, D), BF16), struct((1, QROWS), F32)), [vmem(), vmem()], (vmem(), vmem())
    )(q_unit, gathered)

    factor, sums, codes = call(
        score,
        (
            struct((SPOTS, QROWS), F32),
            struct((SPOTS, QD, QROWS), F32),
            struct((8, SPOTS * 8), I32),
        ),
        [vmem(), vmem(), vmem(), vmem()],
        (vmem(), vmem(), vmem()),
        [
            pltpu.VMEM((SPOTS, QROWS), F32),
            pltpu.VMEM((SPOTS, QROWS), F32),
            pltpu.SMEM((8, SPOTS * 8), I32),
            pltpu.SemaphoreType.DMA,
        ],
    )(asked, own_rows, other_rows, pos_weight)
    sums = exchange(sums, planes())

    probs, back = call(
        terms,
        (struct((SPOTS, PT, QROWS), BF16), struct((SPOTS, QROWS, D), BF16)),
        [smem()] + [vmem()] * 4,
        (vmem(), vmem()),
    )(codes, asked, own_rows, other_rows, factor)
    arrived = exchange(back.reshape(N_Z, N_Y, QROWS, D), along(0))

    own_grad, other_grad, own_sum, weight_inv = call(
        weigh,
        (
            struct((ROWS, PT, D), F32),
            struct((ROWS, PT, D), BF16),
            struct((1, QROWS), F32),
            struct((8, QROWS), F32),
        ),
        [smem(), vmem(), vmem(), vmem()],
        (vmem(), vmem(), vmem(), smem()),
        [pltpu.VMEM((ROWS, PT, D), F32), pltpu.VMEM((8, QROWS), F32), pltpu.SemaphoreType.DMA],
    )(codes, sums, asked, probs)
    pos_grad, query_part, losses = call(
        weigh_positives,
        (struct((BATCH, PT, D), F32), struct((QROWS, D), F32), struct((QD,), F32)),
        [vmem()] * 3,
        (vmem(), vmem(), smem()),
    )(own_sum, q_unit, gathered)

    block = (QD + ROWS // GROUP, PT, D)
    kept, off1, off2, off3 = call(
        split,
        (struct(block, F32), struct(block, BF16), struct(block, BF16), struct(block, BF16)),
        [vmem(), vmem(), vmem()],
        (vmem(),) * 4,
    )(own_grad, lax.ppermute(other_grad, "dp", swap), pos_grad)
    moved = [
        lax.ppermute(part, "group", [(g, (g + ahead) % GROUP) for g in range(GROUP)])
        for ahead, part in ((2, off2), (1, off1), (3, off3))
    ]
    arrived = call(
        add_blocks, struct((N_Y, QROWS, D), BF16), [vmem(), anywhere(), anywhere()], vmem()
    )(arrived, moved[0], moved[1])
    arrived = exchange(arrived, along(1))
    query_grad = call(
        collect, struct((QD, QT, D), F32), [smem(), vmem(), vmem()], vmem()
    )(weight_inv, query_part, arrived)
    total = kept + moved[0].astype(F32) + moved[1].astype(F32) + moved[2].astype(F32)
    return losses, query_grad, total[:QD], total[QD:]


def solution(mesh):
    in_specs = (P(EVERY), P(EVERY), P("dp"), P(EVERY), P())
    out_specs = (P(EVERY), P(EVERY), P(EVERY), P(EVERY))
    return jax.shard_map(per_device, mesh=mesh, in_specs=in_specs, out_specs=out_specs, check_vma=False)
```

```python
import jax
import jax.numpy as jnp
from jax import lax
from jax.experimental import pallas as pl
from jax.experimental.pallas import tpu as pltpu
from jax.sharding import PartitionSpec as P

N_Z, N_Y, N_C, GROUP = 8, 8, 2, 4
N_DP = N_Z * N_Y * N_C
SPOTS = N_Z * N_Y
QD, QT, PT, D, NEG, ROWS = 4, 32, 64, 128, 7, 32
QROWS = QD * QT
PASSAGE_ROWS = 4096 // 128
SENT = QROWS + 8
BATCH = QD * GROUP
SLOTS = 4
VMEM = 6 * 1024 * 1024
F32, BF16, I32 = jnp.float32, jnp.bfloat16, jnp.int32
EXACT = lax.Precision.HIGHEST
EVERY = ("dp", "group")
DOWN = range(7, -1, -1)


def device(z, y, c, x):
    return ((z * N_Y + y) * N_C + c) * GROUP + x


def along(z_core):
    z_lines = [[device(z, y, z_core, x) for z in DOWN] for y in range(N_Y) for x in range(GROUP)]
    y_lines = [[device(z, y, 1 - z_core, x) for y in DOWN] for z in range(N_Z) for x in range(GROUP)]
    return z_lines + y_lines


def planes():
    first = [[device(z, y, 0, x) for z in DOWN for y in DOWN] for x in range(GROUP)]
    second = [[device(z, y, 1, x) for y in DOWN for z in DOWN] for x in range(GROUP)]
    return first + second


def exchange(blocks, groups):
    return lax.all_to_all(blocks, EVERY, split_axis=0, concat_axis=0, axis_index_groups=groups, tiled=True)


def call(body, out_shape, in_specs, out_specs, scratch=()):
    return pl.pallas_call(
        body,
        out_shape=out_shape,
        in_specs=in_specs,
        out_specs=out_specs,
        scratch_shapes=list(scratch),
        compiler_params=pltpu.CompilerParams(vmem_limit_bytes=VMEM),
    )


def vmem():
    return pl.BlockSpec(memory_space=pltpu.VMEM)


def anywhere():
    return pl.BlockSpec(memory_space=pl.ANY)


def hbm():
    return pl.BlockSpec(memory_space=pltpu.HBM)


def smem():
    return pl.BlockSpec(memory_space=pltpu.SMEM)


def unit(values):
    wide = values.astype(F32)
    return (wide * lax.rsqrt(jnp.sum(wide * wide, axis=-1, keepdims=True) + 1e-06)).astype(BF16)


def iota(shape, dim):
    return lax.broadcasted_iota(I32, shape, dim)


def dot(a, b, dims, precision=None):
    return lax.dot_general(a, b, ((dims[0], dims[1]), ((), ())), precision=precision, preferred_element_type=F32)


def token_sum_matrix():
    return (iota((QROWS, QROWS), 0) // QT == iota((QROWS, QROWS), 1) // QT).astype(F32)


def fetch(pairs, sems):
    copies = [pltpu.make_async_copy(src, dst, sems.at[i]) for i, (src, dst) in enumerate(pairs)]
    for copy in copies:
        copy.start()
    return copies


def position():
    holder = lax.axis_index("dp")
    spot, core = holder // N_C, holder % N_C
    z, y = N_Z - 1 - spot // N_Y, N_Y - 1 - spot % N_Y
    source = jnp.where(core == 0, z * N_Y + y, y * N_Z + z)
    return spot, core, source


def prepare(table_in, queries_in, sent, q_unit, table, queries, sems, count):
    pairs = [(table_in, table), (queries_in, queries)]
    for copy in fetch(pairs, sems):
        copy.wait()
    tiles = unit(queries[...])
    q_unit[...] = tiles
    homes = []
    for q in range(QD):
        for k in range(NEG):
            passage = table[PASSAGE_ROWS + q, k]
            home = table[passage // 128, passage % 128]
            owner = home // ROWS
            lane_of = (owner % N_C) * SPOTS + owner // N_C
            count[lane_of] = 0
            homes.append((lane_of, q * ROWS + home % ROWS + 1))
    lane = iota((8, N_DP), 1)
    sub = iota((8, N_DP), 0)
    codes = jnp.zeros((8, N_DP), F32)
    for lane_of, code in homes:
        rank = count[lane_of]
        count[lane_of] = rank + 1
        codes = jnp.where((lane == lane_of) & (sub == rank), code.astype(F32), codes)
    for copy in range(N_Y):
        sent[copy, 0:QROWS, :] = tiles.reshape(QROWS, D)
        sent[copy, QROWS:SENT, :] = codes.astype(BF16)


def normalize(values, out):
    out[...] = unit(values[...])


def positive_scores(q_unit, gathered):
    cands = gathered[...].reshape(BATCH * PT, D)
    exp_scores = jnp.exp(10.0 * dot(cands, q_unit, ((1,), (1,)))).reshape(BATCH, PT, QROWS)
    total = jnp.sum(exp_scores, axis=1)
    score = 0.1 * dot(jnp.log(total), token_sum_matrix(), ((1,), (0,)), EXACT)
    return cands, exp_scores, total, score


def positive_weight(q_tiles, positives, gathered, out):
    gathered[...] = unit(positives[...])
    score = positive_scores(q_tiles[...].reshape(QROWS, D), gathered)[3]
    out[...] = jnp.sum(jnp.exp(score), axis=0, keepdims=True)


def request(codes, source, slot):
    code = codes[slot // 2, source * 8 + slot % 2]
    spot = jnp.maximum(code - 1, 0)
    return code > 0, spot // ROWS, spot % ROWS


def passages(codes, own_rows, other_rows, source):
    picked = [request(codes, source, slot)[2] for slot in range(SLOTS)]
    return jnp.concatenate([own_rows[picked[0]], own_rows[picked[1]], other_rows[picked[2]], other_rows[picked[3]]], axis=0)


def asking(codes, asked, source):
    picked = [request(codes, source, slot)[1] for slot in range(SLOTS)]
    return jnp.concatenate([asked[source, pl.ds(pl.multiple_of(q * QT, QT), QT), :] for q in picked], axis=0)


def spread(packed):
    block = iota((PT, QROWS), 1) // QT
    return jnp.concatenate([jnp.where(block == b, packed, 0.0).astype(BF16) for b in range(SLOTS)], axis=0)


def for_sources(step):
    for first in range(0, SPOTS, 8):
        lax.fori_loop(first, first + 8, step, 0, unroll=8)


def read_codes(asked, table, codes, sem):
    spot, core, _ = position()
    rows = asked[:, QROWS:SENT, :].reshape(SPOTS * 8, N_DP)
    which = iota((8, N_DP), 0)
    lane = jnp.where(which == 0, core * SPOTS + spot, (1 - core) * SPOTS + spot)
    pick = ((iota((8, N_DP), 1) == lane) & (which < 2)).astype(F32).astype(BF16)
    table[...] = dot(pick, rows, ((1,), (1,))).astype(I32)
    copy = pltpu.make_async_copy(table, codes, sem)
    copy.start()
    copy.wait()


def exponentials(codes, asked, own_rows, other_rows, source):
    block = iota((PT, QROWS), 1) // QT
    full = dot(passages(codes, own_rows, other_rows, source), asking(codes, asked, source), ((1,), (1,)))
    packed = full[0:PT]
    for b in range(1, SLOTS):
        packed = jnp.where(block == b, full[b * PT : (b + 1) * PT], packed)
    return jnp.exp(10.0 * packed)


def score(asked, own_rows, other_rows, pos_weight, factor, sums, table, totals, marks, codes, sem):
    read_codes(asked, table, codes, sem)
    source_here = position()[2]
    lane = iota((1, QROWS), 1)

    def one(source, carry):
        mark = jnp.full((1, QROWS), -1.0, F32)
        for b in range(SLOTS):
            valid, q, _ = request(codes, source, b)
            mark = jnp.where((lane // QT == b) & valid, q.astype(F32), mark)
        exp_scores = exponentials(codes, asked, own_rows, other_rows, source)
        totals[pl.ds(source, 1), :] = jnp.sum(exp_scores, axis=0, keepdims=True)
        marks[pl.ds(source, 1), :] = mark
        return carry

    for_sources(one)

    total = totals[...]
    mark = marks[...]
    weight = jnp.exp(0.1 * dot(jnp.log(total), token_sum_matrix(), ((1,), (0,)), EXACT))
    weight = jnp.where(mark >= 0.0, weight, 0.0)
    factor[...] = weight / total
    first = iota((SPOTS, QROWS), 1) % QT == 0
    pad = jnp.zeros((QROWS - SPOTS, QROWS), F32)
    ones = jnp.ones((8, QROWS), F32)
    parts = []
    for q in range(QD):
        mine = jnp.where((mark == float(q)) & first, weight, 0.0)
        part = dot(ones, jnp.concatenate([mine, pad], axis=0), ((1,), (1,)), EXACT)[0:1]
        own = jnp.sum(jnp.where(lane == q * QT, pos_weight[...], 0.0), axis=1, keepdims=True)
        parts.append(part + jnp.where(lane == source_here, own, 0.0))
    sums[...] = jnp.broadcast_to(jnp.concatenate(parts, axis=0)[None], (SPOTS, QD, QROWS))


def terms(codes, asked, own_rows, other_rows, factor, probs, back):
    def one(source, carry):
        packed = exponentials(codes, asked, own_rows, other_rows, source) * factor[pl.ds(source, 1), :]
        probs[source] = packed.astype(BF16)
        grads = dot(spread(packed), passages(codes, own_rows, other_rows, source), ((0,), (0,)))
        picked = [request(codes, source, slot)[1] for slot in range(SLOTS)]
        for q in range(QD):
            total = jnp.zeros((QT, D), F32)
            for b in range(SLOTS):
                total += grads[b * QT : (b + 1) * QT] * (picked[b] == q).astype(F32)
            back[source, q * QT : (q + 1) * QT, :] = total.astype(BF16)
        return carry

    for_sources(one)


def weigh(codes, sums, asked, probs, own_grad, other_grad, own_sum, weight_inv, other_acc, inverse, sem):
    weight_sum = jnp.sum(sums[...], axis=0)
    inverse[...] = jnp.zeros_like(inverse)
    inverse[0:QD] = 1.0 / weight_sum
    copy = pltpu.make_async_copy(inverse, weight_inv, sem)
    copy.start()
    lane = iota((1, QROWS), 1)
    mine = jnp.sum(jnp.where(lane == position()[2], weight_sum, 0.0), axis=1, keepdims=True)
    spread_sum = jnp.zeros((1, QROWS), F32)
    for q in range(QD):
        spread_sum = jnp.where(lane // QT == q, mine[q : q + 1], spread_sum)
    own_sum[...] = spread_sum
    own_grad[...] = jnp.zeros_like(own_grad)
    other_acc[...] = jnp.zeros_like(other_acc)
    copy.wait()

    def add(source, carry):
        grads = dot(spread(probs[source].astype(F32)), asking(codes, asked, source), ((1,), (0,)))
        for b in range(SLOTS):
            _, q, row = request(codes, source, b)
            acc = own_grad if b < 2 else other_acc
            acc[row] += grads[b * PT : (b + 1) * PT] * weight_inv[q, source]
        return carry

    for_sources(add)
    other_grad[...] = other_acc[...].astype(BF16)


def weigh_positives(own_sum, q_tiles, gathered, pos_grad, query_part, losses):
    q_unit = q_tiles[...].reshape(QROWS, D)
    cands, exp_scores, total, scores = positive_scores(q_unit, gathered)
    lane = iota((1, QROWS), 1)
    own = (iota((BATCH, QROWS), 0) == lax.axis_index("group") * QD + iota((BATCH, QROWS), 1) // QT).astype(F32)
    score_grad = jnp.exp(scores) / own_sum[...] - own
    loss = jnp.log(own_sum[...]) - jnp.sum(scores * own, axis=0, keepdims=True)
    for q in range(QD):
        losses[q] = jnp.sum(jnp.where(lane == q * QT, loss, 0.0))
    weight_grad = (exp_scores * (score_grad / total)[:, None, :]).astype(BF16).reshape(BATCH * PT, QROWS)
    query_part[...] = dot(weight_grad, cands, ((0,), (0,)))
    pos_grad[...] = dot(weight_grad, q_unit, ((1,), (0,))).reshape(BATCH, PT, D)


def split(own_grad, moved, pos_grad, kept, off1, off2, off3):
    share = ROWS // GROUP
    for ahead, out in enumerate((kept, off1, off2, off3)):
        g = (lax.axis_index("group") + ahead) % GROUP
        out[0:QD] = pos_grad[pl.ds(g * QD, QD)].astype(out.dtype)
        rows = pl.ds(g * share, share)
        out[QD:] = (own_grad[rows] + moved[rows].astype(F32)).astype(out.dtype)


def add_blocks(arrived, first, second, out, blocks, sems):
    del first, second
    for part, copy in enumerate(fetch([(arrived.at[:, part], blocks.at[:, part]) for part in range(N_Y)], sems)):
        copy.wait()
        out[part] = jnp.sum(blocks[:, part].astype(F32), axis=0).astype(BF16)


def collect(weight_inv, query_part, arrived, out):
    source = position()[2]
    total = jnp.sum(arrived[...].astype(F32), axis=0)
    for q in range(QD):
        rows = slice(q * QT, (q + 1) * QT)
        out[q] = query_part[rows, :] + total[rows] * weight_inv[q, source]


def per_device(queries, positives, passage_pool, negative_ids, storage_row):
    struct = jax.ShapeDtypeStruct
    swap = [(h, h ^ 1) for h in range(N_DP)]
    tiles = struct((QD, QT, D), BF16)

    table = jnp.concatenate([storage_row.reshape(PASSAGE_ROWS, 128), jnp.pad(negative_ids, ((0, 4), (0, 121)))], axis=0)
    sent, q_unit = call(
        prepare,
        (struct((N_Y, SENT, D), BF16), tiles),
        [hbm()] * 2,
        (vmem(), vmem()),
        [
            pltpu.SMEM(table.shape, I32),
            pltpu.VMEM((QD, QT, D), BF16),
            pltpu.SemaphoreType.DMA((2,)),
            pltpu.SMEM((N_DP,), I32),
        ],
    )(table, queries)
    asked = exchange(sent, along(1))
    asked = exchange(jnp.broadcast_to(asked[None], (N_Z, N_Y, SENT, D)), along(0)).reshape(SPOTS, SENT, D)

    own_rows = call(normalize, struct((ROWS, PT, D), BF16), [vmem()], vmem())(passage_pool)
    other_rows = lax.ppermute(own_rows, "dp", swap)
    gathered = lax.all_gather(positives, "group", axis=0, tiled=True)
    gathered, pos_weight = call(
        positive_weight, (struct((BATCH, PT, D), BF16), struct((1, QROWS), F32)), [vmem(), vmem()], (vmem(), vmem())
    )(q_unit, gathered)

    factor, sums, codes = call(
        score,
        (
            struct((SPOTS, QROWS), F32),
            struct((SPOTS, QD, QROWS), F32),
            struct((8, SPOTS * 8), I32),
        ),
        [vmem(), vmem(), vmem(), vmem()],
        (vmem(), vmem(), vmem()),
        [
            pltpu.VMEM((SPOTS, QROWS), F32),
            pltpu.VMEM((SPOTS, QROWS), F32),
            pltpu.SMEM((8, SPOTS * 8), I32),
            pltpu.SemaphoreType.DMA,
        ],
    )(asked, own_rows, other_rows, pos_weight)
    sums = exchange(sums, planes())

    probs, back = call(
        terms,
        (struct((SPOTS, PT, QROWS), BF16), struct((SPOTS, QROWS, D), BF16)),
        [smem()] + [vmem()] * 4,
        (vmem(), vmem()),
    )(codes, asked, own_rows, other_rows, factor)
    arrived = exchange(back.reshape(N_Z, N_Y, QROWS, D), along(0))

    own_grad, other_grad, own_sum, weight_inv = call(
        weigh,
        (
            struct((ROWS, PT, D), F32),
            struct((ROWS, PT, D), BF16),
            struct((1, QROWS), F32),
            struct((8, QROWS), F32),
        ),
        [smem(), vmem(), vmem(), vmem()],
        (vmem(), vmem(), vmem(), smem()),
        [pltpu.VMEM((ROWS, PT, D), F32), pltpu.VMEM((8, QROWS), F32), pltpu.SemaphoreType.DMA],
    )(codes, sums, asked, probs)
    pos_grad, query_part, losses = call(
        weigh_positives,
        (struct((BATCH, PT, D), F32), struct((QROWS, D), F32), struct((QD,), F32)),
        [vmem()] * 3,
        (vmem(), vmem(), smem()),
    )(own_sum, q_unit, gathered)

    block = (QD + ROWS // GROUP, PT, D)
    kept, off1, off2, off3 = call(
        split,
        (struct(block, F32), struct(block, BF16), struct(block, BF16), struct(block, BF16)),
        [vmem(), vmem(), vmem()],
        (vmem(),) * 4,
    )(own_grad, lax.ppermute(other_grad, "dp", swap), pos_grad)
    moved = [
        lax.ppermute(part, "group", [(g, (g + ahead) % GROUP) for g in range(GROUP)])
        for ahead, part in ((2, off2), (1, off1), (3, off3))
    ]
    arrived = call(
        add_blocks,
        struct((N_Y, QROWS, D), BF16),
        [hbm(), anywhere(), anywhere()],
        vmem(),
        [pltpu.VMEM((N_Z, N_Y, QROWS, D), BF16), pltpu.SemaphoreType.DMA((N_Y,))],
    )(arrived, moved[0], moved[1])
    arrived = exchange(arrived, along(1))
    query_grad = call(
        collect, struct((QD, QT, D), F32), [smem(), vmem(), vmem()], vmem()
    )(weight_inv, query_part, arrived)
    total = kept + moved[0].astype(F32) + moved[1].astype(F32) + moved[2].astype(F32)
    return losses, query_grad, total[:QD], total[QD:]


def solution(mesh):
    in_specs = (P(EVERY), P(EVERY), P("dp"), P(EVERY), P())
    out_specs = (P(EVERY), P(EVERY), P(EVERY), P(EVERY))
    return jax.shard_map(per_device, mesh=mesh, in_specs=in_specs, out_specs=out_specs, check_vma=False)
```

```python
import jax
import jax.numpy as jnp
from jax import lax
from jax.experimental import pallas as pl
from jax.experimental.pallas import tpu as pltpu
from jax.sharding import PartitionSpec as P

N_Z, N_Y, N_C, GROUP = 8, 8, 2, 4
N_DP = N_Z * N_Y * N_C
SPOTS = N_Z * N_Y
QD, QT, PT, D, NEG, ROWS = 4, 32, 64, 128, 7, 32
QROWS = QD * QT
PASSAGE_ROWS = 4096 // 128
SENT = QROWS + 8
BATCH = QD * GROUP
SLOTS = 4
VMEM = 6 * 1024 * 1024
F32, BF16, I32 = jnp.float32, jnp.bfloat16, jnp.int32
EXACT = lax.Precision.HIGHEST
EVERY = ("dp", "group")
DOWN = range(7, -1, -1)


def device(z, y, c, x):
    return ((z * N_Y + y) * N_C + c) * GROUP + x


def along(z_core):
    z_lines = [[device(z, y, z_core, x) for z in DOWN] for y in range(N_Y) for x in range(GROUP)]
    y_lines = [[device(z, y, 1 - z_core, x) for y in DOWN] for z in range(N_Z) for x in range(GROUP)]
    return z_lines + y_lines


def planes():
    first = [[device(z, y, 0, x) for z in DOWN for y in DOWN] for x in range(GROUP)]
    second = [[device(z, y, 1, x) for y in DOWN for z in DOWN] for x in range(GROUP)]
    return first + second


def exchange(blocks, groups):
    return lax.all_to_all(blocks, EVERY, split_axis=0, concat_axis=0, axis_index_groups=groups, tiled=True)


def call(body, out_shape, in_specs, out_specs, scratch=()):
    return pl.pallas_call(
        body,
        out_shape=out_shape,
        in_specs=in_specs,
        out_specs=out_specs,
        scratch_shapes=list(scratch),
        compiler_params=pltpu.CompilerParams(vmem_limit_bytes=VMEM),
    )


def vmem():
    return pl.BlockSpec(memory_space=pltpu.VMEM)


def anywhere():
    return pl.BlockSpec(memory_space=pl.ANY)


def hbm():
    return pl.BlockSpec(memory_space=pltpu.HBM)


def smem():
    return pl.BlockSpec(memory_space=pltpu.SMEM)


def unit(values):
    wide = values.astype(F32)
    return (wide * lax.rsqrt(jnp.sum(wide * wide, axis=-1, keepdims=True) + 1e-06)).astype(BF16)


def iota(shape, dim):
    return lax.broadcasted_iota(I32, shape, dim)


def dot(a, b, dims, precision=None):
    return lax.dot_general(a, b, ((dims[0], dims[1]), ((), ())), precision=precision, preferred_element_type=F32)


def token_sum_matrix():
    return (iota((QROWS, QROWS), 0) // QT == iota((QROWS, QROWS), 1) // QT).astype(F32)


def fetch(pairs, sems):
    copies = [pltpu.make_async_copy(src, dst, sems.at[i]) for i, (src, dst) in enumerate(pairs)]
    for copy in copies:
        copy.start()
    return copies


def position():
    holder = lax.axis_index("dp")
    spot, core = holder // N_C, holder % N_C
    z, y = N_Z - 1 - spot // N_Y, N_Y - 1 - spot % N_Y
    source = jnp.where(core == 0, z * N_Y + y, y * N_Z + z)
    return spot, core, source


def prepare(table_in, queries_in, sent, q_unit, table, queries, sems, count):
    pairs = [(table_in, table), (queries_in, queries)]
    for copy in fetch(pairs, sems):
        copy.wait()
    tiles = unit(queries[...])
    q_unit[...] = tiles
    homes = []
    for q in range(QD):
        for k in range(NEG):
            passage = table[PASSAGE_ROWS + q, k]
            home = table[passage // 128, passage % 128]
            owner = home // ROWS
            lane_of = (owner % N_C) * SPOTS + owner // N_C
            count[lane_of] = 0
            homes.append((lane_of, q * ROWS + home % ROWS + 1))
    lane = iota((8, N_DP), 1)
    sub = iota((8, N_DP), 0)
    codes = jnp.zeros((8, N_DP), F32)
    for lane_of, code in homes:
        rank = count[lane_of]
        count[lane_of] = rank + 1
        codes = jnp.where((lane == lane_of) & (sub == rank), code.astype(F32), codes)
    for copy in range(N_Y):
        sent[copy, 0:QROWS, :] = tiles.reshape(QROWS, D)
        sent[copy, QROWS:SENT, :] = codes.astype(BF16)


def normalize(values, out):
    out[...] = unit(values[...])


def positive_scores(q_unit, gathered):
    cands = gathered[...].reshape(BATCH * PT, D)
    exp_scores = jnp.exp(10.0 * dot(cands, q_unit, ((1,), (1,)))).reshape(BATCH, PT, QROWS)
    total = jnp.sum(exp_scores, axis=1)
    score = 0.1 * dot(jnp.log(total), token_sum_matrix(), ((1,), (0,)), EXACT)
    return cands, exp_scores, total, score


def positive_weight(q_tiles, positives, gathered, out):
    gathered[...] = unit(positives[...])
    score = positive_scores(q_tiles[...].reshape(QROWS, D), gathered)[3]
    out[...] = jnp.sum(jnp.exp(score), axis=0, keepdims=True)


def request(codes, source, slot):
    code = codes[slot // 2, source * 8 + slot % 2]
    spot = jnp.maximum(code - 1, 0)
    return code > 0, spot // ROWS, spot % ROWS


def passages(codes, own_rows, other_rows, source):
    picked = [request(codes, source, slot)[2] for slot in range(SLOTS)]
    return jnp.concatenate([own_rows[picked[0]], own_rows[picked[1]], other_rows[picked[2]], other_rows[picked[3]]], axis=0)


def asking(codes, asked, source):
    picked = [request(codes, source, slot)[1] for slot in range(SLOTS)]
    return jnp.concatenate([asked[source, pl.ds(pl.multiple_of(q * QT, QT), QT), :] for q in picked], axis=0)


def spread(packed):
    block = iota((PT, QROWS), 1) // QT
    return jnp.concatenate([jnp.where(block == b, packed, 0.0).astype(BF16) for b in range(SLOTS)], axis=0)


def for_sources(step):
    for first in range(0, SPOTS, 8):
        lax.fori_loop(first, first + 8, step, 0, unroll=8)


def read_codes(asked, table, codes, sem):
    spot, core, _ = position()
    rows = asked[:, QROWS:SENT, :].reshape(SPOTS * 8, N_DP)
    which = iota((8, N_DP), 0)
    lane = jnp.where(which == 0, core * SPOTS + spot, (1 - core) * SPOTS + spot)
    pick = ((iota((8, N_DP), 1) == lane) & (which < 2)).astype(F32).astype(BF16)
    table[...] = dot(pick, rows, ((1,), (1,))).astype(I32)
    copy = pltpu.make_async_copy(table, codes, sem)
    copy.start()
    copy.wait()


def exponentials(codes, asked, own_rows, other_rows, source):
    block = iota((PT, QROWS), 1) // QT
    full = dot(passages(codes, own_rows, other_rows, source), asking(codes, asked, source), ((1,), (1,)))
    packed = full[0:PT]
    for b in range(1, SLOTS):
        packed = jnp.where(block == b, full[b * PT : (b + 1) * PT], packed)
    return jnp.exp(10.0 * packed)


def score(asked, own_rows, other_rows, pos_weight, factor, sums, table, totals, marks, codes, sem):
    read_codes(asked, table, codes, sem)
    source_here = position()[2]
    lane = iota((1, QROWS), 1)

    def one(source, carry):
        mark = jnp.full((1, QROWS), -1.0, F32)
        for b in range(SLOTS):
            valid, q, _ = request(codes, source, b)
            mark = jnp.where((lane // QT == b) & valid, q.astype(F32), mark)
        exp_scores = exponentials(codes, asked, own_rows, other_rows, source)
        totals[pl.ds(source, 1), :] = jnp.sum(exp_scores, axis=0, keepdims=True)
        marks[pl.ds(source, 1), :] = mark
        return carry

    for_sources(one)

    total = totals[...]
    mark = marks[...]
    weight = jnp.exp(0.1 * dot(jnp.log(total), token_sum_matrix(), ((1,), (0,)), EXACT))
    weight = jnp.where(mark >= 0.0, weight, 0.0)
    factor[...] = weight / total
    first = iota((SPOTS, QROWS), 1) % QT == 0
    pad = jnp.zeros((QROWS - SPOTS, QROWS), F32)
    ones = jnp.ones((8, QROWS), F32)
    parts = []
    for q in range(QD):
        mine = jnp.where((mark == float(q)) & first, weight, 0.0)
        part = dot(ones, jnp.concatenate([mine, pad], axis=0), ((1,), (1,)), EXACT)[0:1]
        own = jnp.sum(jnp.where(lane == q * QT, pos_weight[...], 0.0), axis=1, keepdims=True)
        parts.append(part + jnp.where(lane == source_here, own, 0.0))
    sums[...] = jnp.broadcast_to(jnp.concatenate(parts, axis=0)[None], (SPOTS, QD, QROWS))


def terms(codes, asked, own_rows, other_rows, factor, probs, back):
    def one(source, carry):
        packed = exponentials(codes, asked, own_rows, other_rows, source) * factor[pl.ds(source, 1), :]
        probs[source] = packed.astype(BF16)
        grads = dot(spread(packed), passages(codes, own_rows, other_rows, source), ((0,), (0,)))
        picked = [request(codes, source, slot)[1] for slot in range(SLOTS)]
        for q in range(QD):
            total = jnp.zeros((QT, D), F32)
            for b in range(SLOTS):
                total += grads[b * QT : (b + 1) * QT] * (picked[b] == q).astype(F32)
            back[source, q * QT : (q + 1) * QT, :] = total.astype(BF16)
        return carry

    for_sources(one)


def weigh(codes, sums, asked, probs, own_grad, other_grad, own_sum, weight_inv, other_acc, inverse, sem):
    weight_sum = jnp.sum(sums[...], axis=0)
    inverse[...] = jnp.zeros_like(inverse)
    inverse[0:QD] = 1.0 / weight_sum
    copy = pltpu.make_async_copy(inverse, weight_inv, sem)
    copy.start()
    lane = iota((1, QROWS), 1)
    mine = jnp.sum(jnp.where(lane == position()[2], weight_sum, 0.0), axis=1, keepdims=True)
    spread_sum = jnp.zeros((1, QROWS), F32)
    for q in range(QD):
        spread_sum = jnp.where(lane // QT == q, mine[q : q + 1], spread_sum)
    own_sum[...] = spread_sum
    own_grad[...] = jnp.zeros_like(own_grad)
    other_acc[...] = jnp.zeros_like(other_acc)
    copy.wait()

    def add(source, carry):
        grads = dot(spread(probs[source].astype(F32)), asking(codes, asked, source), ((1,), (0,)))
        for b in range(SLOTS):
            _, q, row = request(codes, source, b)
            acc = own_grad if b < 2 else other_acc
            acc[row] += grads[b * PT : (b + 1) * PT] * weight_inv[q, source]
        return carry

    for_sources(add)
    other_grad[...] = other_acc[...].astype(BF16)


def weigh_positives(own_sum, q_tiles, gathered, pos_grad, query_part, losses):
    q_unit = q_tiles[...].reshape(QROWS, D)
    cands, exp_scores, total, scores = positive_scores(q_unit, gathered)
    lane = iota((1, QROWS), 1)
    own = (iota((BATCH, QROWS), 0) == lax.axis_index("group") * QD + iota((BATCH, QROWS), 1) // QT).astype(F32)
    score_grad = jnp.exp(scores) / own_sum[...] - own
    loss = jnp.log(own_sum[...]) - jnp.sum(scores * own, axis=0, keepdims=True)
    for q in range(QD):
        losses[q] = jnp.sum(jnp.where(lane == q * QT, loss, 0.0))
    weight_grad = (exp_scores * (score_grad / total)[:, None, :]).astype(BF16).reshape(BATCH * PT, QROWS)
    query_part[...] = dot(weight_grad, cands, ((0,), (0,)))
    pos_grad[...] = dot(weight_grad, q_unit, ((1,), (0,))).reshape(BATCH, PT, D)


def split(own_grad, moved, pos_grad, kept, off1, off2, off3):
    share = ROWS // GROUP
    for ahead, out in enumerate((kept, off1, off2, off3)):
        g = (lax.axis_index("group") + ahead) % GROUP
        out[0:QD] = pos_grad[pl.ds(g * QD, QD)].astype(out.dtype)
        rows = pl.ds(g * share, share)
        out[QD:] = (own_grad[rows] + moved[rows].astype(F32)).astype(out.dtype)


def add_blocks(arrived, first, second, third, out, blocks, sems):
    del first, second, third
    for part, copy in enumerate(fetch([(arrived.at[:, part], blocks.at[:, part]) for part in range(N_Y)], sems)):
        copy.wait()
        out[part] = jnp.sum(blocks[:, part].astype(F32), axis=0).astype(BF16)


def collect(weight_inv, query_part, arrived, out):
    source = position()[2]
    total = jnp.sum(arrived[...].astype(F32), axis=0)
    for q in range(QD):
        rows = slice(q * QT, (q + 1) * QT)
        out[q] = query_part[rows, :] + total[rows] * weight_inv[q, source]


def per_device(queries, positives, passage_pool, negative_ids, storage_row):
    struct = jax.ShapeDtypeStruct
    swap = [(h, h ^ 1) for h in range(N_DP)]
    tiles = struct((QD, QT, D), BF16)

    table = jnp.concatenate([storage_row.reshape(PASSAGE_ROWS, 128), jnp.pad(negative_ids, ((0, 4), (0, 121)))], axis=0)
    sent, q_unit = call(
        prepare,
        (struct((N_Y, SENT, D), BF16), tiles),
        [hbm()] * 2,
        (vmem(), vmem()),
        [
            pltpu.SMEM(table.shape, I32),
            pltpu.VMEM((QD, QT, D), BF16),
            pltpu.SemaphoreType.DMA((2,)),
            pltpu.SMEM((N_DP,), I32),
        ],
    )(table, queries)
    asked = exchange(sent, along(1))
    asked = exchange(jnp.broadcast_to(asked[None], (N_Z, N_Y, SENT, D)), along(0)).reshape(SPOTS, SENT, D)

    own_rows = call(normalize, struct((ROWS, PT, D), BF16), [vmem()], vmem())(passage_pool)
    other_rows = lax.ppermute(own_rows, "dp", swap)
    gathered = lax.all_gather(positives, "group", axis=0, tiled=True)
    gathered, pos_weight = call(
        positive_weight, (struct((BATCH, PT, D), BF16), struct((1, QROWS), F32)), [vmem(), vmem()], (vmem(), vmem())
    )(q_unit, gathered)

    factor, sums, codes = call(
        score,
        (
            struct((SPOTS, QROWS), F32),
            struct((SPOTS, QD, QROWS), F32),
            struct((8, SPOTS * 8), I32),
        ),
        [vmem(), vmem(), vmem(), vmem()],
        (vmem(), vmem(), vmem()),
        [
            pltpu.VMEM((SPOTS, QROWS), F32),
            pltpu.VMEM((SPOTS, QROWS), F32),
            pltpu.SMEM((8, SPOTS * 8), I32),
            pltpu.SemaphoreType.DMA,
        ],
    )(asked, own_rows, other_rows, pos_weight)
    sums = exchange(sums, planes())

    probs, back = call(
        terms,
        (struct((SPOTS, PT, QROWS), BF16), struct((SPOTS, QROWS, D), BF16)),
        [smem()] + [vmem()] * 4,
        (vmem(), vmem()),
    )(codes, asked, own_rows, other_rows, factor)
    arrived = exchange(back.reshape(N_Z, N_Y, QROWS, D), along(0))

    own_grad, other_grad, own_sum, weight_inv = call(
        weigh,
        (
            struct((ROWS, PT, D), F32),
            struct((ROWS, PT, D), BF16),
            struct((1, QROWS), F32),
            struct((8, QROWS), F32),
        ),
        [smem(), vmem(), vmem(), vmem()],
        (vmem(), vmem(), vmem(), smem()),
        [pltpu.VMEM((ROWS, PT, D), F32), pltpu.VMEM((8, QROWS), F32), pltpu.SemaphoreType.DMA],
    )(codes, sums, asked, probs)
    pos_grad, query_part, losses = call(
        weigh_positives,
        (struct((BATCH, PT, D), F32), struct((QROWS, D), F32), struct((QD,), F32)),
        [vmem()] * 3,
        (vmem(), vmem(), smem()),
    )(own_sum, q_unit, gathered)

    block = (QD + ROWS // GROUP, PT, D)
    kept, off1, off2, off3 = call(
        split,
        (struct(block, F32), struct(block, BF16), struct(block, BF16), struct(block, BF16)),
        [vmem(), vmem(), vmem()],
        (vmem(),) * 4,
    )(own_grad, lax.ppermute(other_grad, "dp", swap), pos_grad)
    moved = [
        lax.ppermute(part, "group", [(g, (g + ahead) % GROUP) for g in range(GROUP)])
        for ahead, part in ((2, off2), (1, off1), (3, off3))
    ]
    arrived = call(
        add_blocks,
        struct((N_Y, QROWS, D), BF16),
        [hbm()] + [anywhere()] * 3,
        vmem(),
        [pltpu.VMEM((N_Z, N_Y, QROWS, D), BF16), pltpu.SemaphoreType.DMA((N_Y,))],
    )(arrived, *moved)
    arrived = exchange(arrived, along(1))
    query_grad = call(
        collect, struct((QD, QT, D), F32), [smem(), vmem(), vmem()], vmem()
    )(weight_inv, query_part, arrived)
    total = kept + moved[0].astype(F32) + moved[1].astype(F32) + moved[2].astype(F32)
    return losses, query_grad, total[:QD], total[QD:]


def solution(mesh):
    in_specs = (P(EVERY), P(EVERY), P("dp"), P(EVERY), P())
    out_specs = (P(EVERY), P(EVERY), P(EVERY), P(EVERY))
    return jax.shard_map(per_device, mesh=mesh, in_specs=in_specs, out_specs=out_specs, check_vma=False)
```

```python
import jax
import jax.numpy as jnp
from jax import lax
from jax.experimental import pallas as pl
from jax.experimental.pallas import tpu as pltpu
from jax.sharding import PartitionSpec as P

N_Z, N_Y, N_C, GROUP = 8, 8, 2, 4
N_DP = N_Z * N_Y * N_C
SPOTS = N_Z * N_Y
QD, QT, PT, D, NEG, ROWS = 4, 32, 64, 128, 7, 32
QROWS = QD * QT
PASSAGE_ROWS = 4096 // 128
SENT = QROWS + 8
BATCH = QD * GROUP
SLOTS = 4
VMEM = 6 * 1024 * 1024
F32, BF16, I32 = jnp.float32, jnp.bfloat16, jnp.int32
EXACT = lax.Precision.HIGHEST
EVERY = ("dp", "group")
DOWN = range(7, -1, -1)


def device(z, y, c, x):
    return ((z * N_Y + y) * N_C + c) * GROUP + x


def along(z_core):
    z_lines = [[device(z, y, z_core, x) for z in DOWN] for y in range(N_Y) for x in range(GROUP)]
    y_lines = [[device(z, y, 1 - z_core, x) for y in DOWN] for z in range(N_Z) for x in range(GROUP)]
    return z_lines + y_lines


def planes():
    first = [[device(z, y, 0, x) for z in DOWN for y in DOWN] for x in range(GROUP)]
    second = [[device(z, y, 1, x) for y in DOWN for z in DOWN] for x in range(GROUP)]
    return first + second


def exchange(blocks, groups):
    return lax.all_to_all(blocks, EVERY, split_axis=0, concat_axis=0, axis_index_groups=groups, tiled=True)


def call(body, out_shape, in_specs, out_specs, scratch=()):
    return pl.pallas_call(
        body,
        out_shape=out_shape,
        in_specs=in_specs,
        out_specs=out_specs,
        scratch_shapes=list(scratch),
        compiler_params=pltpu.CompilerParams(vmem_limit_bytes=VMEM),
    )


def vmem():
    return pl.BlockSpec(memory_space=pltpu.VMEM)


def anywhere():
    return pl.BlockSpec(memory_space=pl.ANY)


def hbm():
    return pl.BlockSpec(memory_space=pltpu.HBM)


def smem():
    return pl.BlockSpec(memory_space=pltpu.SMEM)


def unit(values):
    wide = values.astype(F32)
    return (wide * lax.rsqrt(jnp.sum(wide * wide, axis=-1, keepdims=True) + 1e-06)).astype(BF16)


def iota(shape, dim):
    return lax.broadcasted_iota(I32, shape, dim)


def dot(a, b, dims, precision=None):
    return lax.dot_general(a, b, ((dims[0], dims[1]), ((), ())), precision=precision, preferred_element_type=F32)


def token_sum_matrix():
    return (iota((QROWS, QROWS), 0) // QT == iota((QROWS, QROWS), 1) // QT).astype(F32)


def fetch(pairs, sems):
    copies = [pltpu.make_async_copy(src, dst, sems.at[i]) for i, (src, dst) in enumerate(pairs)]
    for copy in copies:
        copy.start()
    return copies


def position():
    holder = lax.axis_index("dp")
    spot, core = holder // N_C, holder % N_C
    z, y = N_Z - 1 - spot // N_Y, N_Y - 1 - spot % N_Y
    source = jnp.where(core == 0, z * N_Y + y, y * N_Z + z)
    return spot, core, source


def prepare(table_in, queries_in, sent, q_unit, table, queries, sems, count):
    pairs = [(table_in, table), (queries_in, queries)]
    for copy in fetch(pairs, sems):
        copy.wait()
    tiles = unit(queries[...])
    q_unit[...] = tiles
    homes = []
    for q in range(QD):
        for k in range(NEG):
            passage = table[PASSAGE_ROWS + q, k]
            home = table[passage // 128, passage % 128]
            owner = home // ROWS
            lane_of = (owner % N_C) * SPOTS + owner // N_C
            count[lane_of] = 0
            homes.append((lane_of, q * ROWS + home % ROWS + 1))
    lane = iota((8, N_DP), 1)
    sub = iota((8, N_DP), 0)
    codes = jnp.zeros((8, N_DP), F32)
    for lane_of, code in homes:
        rank = count[lane_of]
        count[lane_of] = rank + 1
        codes = jnp.where((lane == lane_of) & (sub == rank), code.astype(F32), codes)
    for copy in range(N_Y):
        sent[copy, 0:QROWS, :] = tiles.reshape(QROWS, D)
        sent[copy, QROWS:SENT, :] = codes.astype(BF16)


def normalize(values, out):
    out[...] = unit(values[...])


def positive_scores(q_unit, gathered):
    cands = gathered[...].reshape(BATCH * PT, D)
    exp_scores = jnp.exp(10.0 * dot(cands, q_unit, ((1,), (1,)))).reshape(BATCH, PT, QROWS)
    total = jnp.sum(exp_scores, axis=1)
    score = 0.1 * dot(jnp.log(total), token_sum_matrix(), ((1,), (0,)), EXACT)
    return cands, exp_scores, total, score


def positive_weight(q_tiles, positives, gathered, out):
    gathered[...] = unit(positives[...])
    score = positive_scores(q_tiles[...].reshape(QROWS, D), gathered)[3]
    out[...] = jnp.sum(jnp.exp(score), axis=0, keepdims=True)


def request(codes, source, slot):
    code = codes[slot // 2, source * 8 + slot % 2]
    spot = jnp.maximum(code - 1, 0)
    return code > 0, spot // ROWS, spot % ROWS


def passages(codes, own_rows, other_rows, source):
    picked = [request(codes, source, slot)[2] for slot in range(SLOTS)]
    return jnp.concatenate([own_rows[picked[0]], own_rows[picked[1]], other_rows[picked[2]], other_rows[picked[3]]], axis=0)


def asking(codes, asked, source):
    picked = [request(codes, source, slot)[1] for slot in range(SLOTS)]
    return jnp.concatenate([asked[source, pl.ds(pl.multiple_of(q * QT, QT), QT), :] for q in picked], axis=0)


def spread(packed):
    block = iota((PT, QROWS), 1) // QT
    return jnp.concatenate([jnp.where(block == b, packed, 0.0).astype(BF16) for b in range(SLOTS)], axis=0)


def for_sources(step):
    for first in range(0, SPOTS, 8):
        lax.fori_loop(first, first + 8, step, 0, unroll=8)


def read_codes(asked, table, codes, sem):
    spot, core, _ = position()
    rows = asked[:, QROWS:SENT, :].reshape(SPOTS * 8, N_DP)
    which = iota((8, N_DP), 0)
    lane = jnp.where(which == 0, core * SPOTS + spot, (1 - core) * SPOTS + spot)
    pick = ((iota((8, N_DP), 1) == lane) & (which < 2)).astype(F32).astype(BF16)
    table[...] = dot(pick, rows, ((1,), (1,)))[0:2].astype(I32)
    copy = pltpu.make_async_copy(table, codes, sem)
    copy.start()
    copy.wait()


def exponentials(codes, asked, own_rows, other_rows, source):
    block = iota((PT, QROWS), 1) // QT
    full = dot(passages(codes, own_rows, other_rows, source), asking(codes, asked, source), ((1,), (1,)))
    packed = full[0:PT]
    for b in range(1, SLOTS):
        packed = jnp.where(block == b, full[b * PT : (b + 1) * PT], packed)
    return jnp.exp(10.0 * packed)


def score(asked, own_rows, other_rows, pos_weight, factor, sums, table, totals, marks, codes, sem):
    read_codes(asked, table, codes, sem)
    source_here = position()[2]
    lane = iota((1, QROWS), 1)

    def one(source, carry):
        mark = jnp.full((1, QROWS), -1.0, F32)
        for b in range(SLOTS):
            valid, q, _ = request(codes, source, b)
            mark = jnp.where((lane // QT == b) & valid, q.astype(F32), mark)
        exp_scores = exponentials(codes, asked, own_rows, other_rows, source)
        totals[pl.ds(source, 1), :] = jnp.sum(exp_scores, axis=0, keepdims=True)
        marks[pl.ds(source, 1), :] = mark
        return carry

    for_sources(one)

    total = totals[...]
    mark = marks[...]
    weight = jnp.exp(0.1 * dot(jnp.log(total), token_sum_matrix(), ((1,), (0,)), EXACT))
    weight = jnp.where(mark >= 0.0, weight, 0.0)
    factor[...] = weight / total
    first = iota((SPOTS, QROWS), 1) % QT == 0
    pad = jnp.zeros((QROWS - SPOTS, QROWS), F32)
    ones = jnp.ones((8, QROWS), F32)
    parts = []
    for q in range(QD):
        mine = jnp.where((mark == float(q)) & first, weight, 0.0)
        part = dot(ones, jnp.concatenate([mine, pad], axis=0), ((1,), (1,)), EXACT)[0:1]
        own = jnp.sum(jnp.where(lane == q * QT, pos_weight[...], 0.0), axis=1, keepdims=True)
        parts.append(part + jnp.where(lane == source_here, own, 0.0))
    sums[...] = jnp.broadcast_to(jnp.concatenate(parts, axis=0)[None], (SPOTS, QD, QROWS))


def terms(codes, asked, own_rows, other_rows, factor, probs, back):
    def one(source, carry):
        packed = exponentials(codes, asked, own_rows, other_rows, source) * factor[pl.ds(source, 1), :]
        probs[source] = packed.astype(BF16)
        grads = dot(spread(packed), passages(codes, own_rows, other_rows, source), ((0,), (0,)))
        picked = [request(codes, source, slot)[1] for slot in range(SLOTS)]
        for q in range(QD):
            total = jnp.zeros((QT, D), F32)
            for b in range(SLOTS):
                total += grads[b * QT : (b + 1) * QT] * (picked[b] == q).astype(F32)
            back[source, q * QT : (q + 1) * QT, :] = total.astype(BF16)
        return carry

    for_sources(one)


def weigh(codes, sums, asked, probs, own_grad, other_grad, own_sum, other_acc, inverse, weight_inv, sem):
    weight_sum = jnp.sum(sums[...], axis=0)
    inverse[...] = jnp.zeros_like(inverse)
    inverse[0:QD] = 1.0 / weight_sum
    copy = pltpu.make_async_copy(inverse, weight_inv, sem)
    copy.start()
    lane = iota((1, QROWS), 1)
    mine = jnp.sum(jnp.where(lane == position()[2], weight_sum, 0.0), axis=1, keepdims=True)
    spread_sum = jnp.zeros((1, QROWS), F32)
    for q in range(QD):
        spread_sum = jnp.where(lane // QT == q, mine[q : q + 1], spread_sum)
    own_sum[...] = spread_sum
    own_grad[...] = jnp.zeros_like(own_grad)
    other_acc[...] = jnp.zeros_like(other_acc)
    copy.wait()

    def add(source, carry):
        grads = dot(spread(probs[source].astype(F32)), asking(codes, asked, source), ((1,), (0,)))
        for b in range(SLOTS):
            _, q, row = request(codes, source, b)
            acc = own_grad if b < 2 else other_acc
            acc[row] += grads[b * PT : (b + 1) * PT] * weight_inv[q, source]
        return carry

    for_sources(add)
    other_grad[...] = other_acc[...].astype(BF16)


def weigh_positives(own_sum, q_tiles, gathered, pos_grad, query_part, scale, losses):
    q_unit = q_tiles[...].reshape(QROWS, D)
    cands, exp_scores, total, scores = positive_scores(q_unit, gathered)
    lane = iota((1, QROWS), 1)
    own = (iota((BATCH, QROWS), 0) == lax.axis_index("group") * QD + iota((BATCH, QROWS), 1) // QT).astype(F32)
    score_grad = jnp.exp(scores) / own_sum[...] - own
    loss = jnp.log(own_sum[...]) - jnp.sum(scores * own, axis=0, keepdims=True)
    for q in range(QD):
        losses[q] = jnp.sum(jnp.where(lane == q * QT, loss, 0.0))
    weight_grad = (exp_scores * (score_grad / total)[:, None, :]).astype(BF16).reshape(BATCH * PT, QROWS)
    query_part[...] = dot(weight_grad, cands, ((0,), (0,)))
    scale[...] = jnp.transpose(jnp.broadcast_to(1.0 / own_sum[...], (QROWS, D)))
    pos_grad[...] = dot(weight_grad, q_unit, ((1,), (0,))).reshape(BATCH, PT, D)


def split(own_grad, moved, pos_grad, kept, off1, off2, off3):
    share = ROWS // GROUP
    for ahead, out in enumerate((kept, off1, off2, off3)):
        g = (lax.axis_index("group") + ahead) % GROUP
        out[0:QD] = pos_grad[pl.ds(g * QD, QD)].astype(out.dtype)
        rows = pl.ds(g * share, share)
        out[QD:] = (own_grad[rows] + moved[rows].astype(F32)).astype(out.dtype)


def add_blocks(arrived, first, second, third, out, blocks, sems):
    del first, second, third
    for part, copy in enumerate(fetch([(arrived.at[:, part], blocks.at[:, part]) for part in range(N_Y)], sems)):
        copy.wait()
        out[part] = jnp.sum(blocks[:, part].astype(F32), axis=0).astype(BF16)


def collect(scale, query_part, arrived, out):
    total = jnp.sum(arrived[...].astype(F32), axis=0)
    out[...] = (query_part[...] + total * scale[...]).reshape(QD, QT, D)


def per_device(queries, positives, passage_pool, negative_ids, storage_row):
    struct = jax.ShapeDtypeStruct
    swap = [(h, h ^ 1) for h in range(N_DP)]
    tiles = struct((QD, QT, D), BF16)

    table = jnp.concatenate([storage_row.reshape(PASSAGE_ROWS, 128), jnp.pad(negative_ids, ((0, 4), (0, 121)))], axis=0)
    sent, q_unit = call(
        prepare,
        (struct((N_Y, SENT, D), BF16), tiles),
        [hbm()] * 2,
        (vmem(), vmem()),
        [
            pltpu.SMEM(table.shape, I32),
            pltpu.VMEM((QD, QT, D), BF16),
            pltpu.SemaphoreType.DMA((2,)),
            pltpu.SMEM((N_DP,), I32),
        ],
    )(table, queries)
    asked = exchange(sent, along(1))
    asked = exchange(jnp.broadcast_to(asked[None], (N_Z, N_Y, SENT, D)), along(0)).reshape(SPOTS, SENT, D)

    own_rows = call(normalize, struct((ROWS, PT, D), BF16), [vmem()], vmem())(passage_pool)
    other_rows = lax.ppermute(own_rows, "dp", swap)
    gathered = lax.all_gather(positives, "group", axis=0, tiled=True)
    gathered, pos_weight = call(
        positive_weight, (struct((BATCH, PT, D), BF16), struct((1, QROWS), F32)), [vmem(), vmem()], (vmem(), vmem())
    )(q_unit, gathered)

    factor, sums, codes = call(
        score,
        (
            struct((SPOTS, QROWS), F32),
            struct((SPOTS, QD, QROWS), F32),
            struct((2, SPOTS * 8), I32),
        ),
        [vmem(), vmem(), vmem(), vmem()],
        (vmem(), vmem(), vmem()),
        [
            pltpu.VMEM((SPOTS, QROWS), F32),
            pltpu.VMEM((SPOTS, QROWS), F32),
            pltpu.SMEM((2, SPOTS * 8), I32),
            pltpu.SemaphoreType.DMA,
        ],
    )(asked, own_rows, other_rows, pos_weight)
    sums = exchange(sums, planes())

    probs, back = call(
        terms,
        (struct((SPOTS, PT, QROWS), BF16), struct((SPOTS, QROWS, D), BF16)),
        [smem()] + [vmem()] * 4,
        (vmem(), vmem()),
    )(codes, asked, own_rows, other_rows, factor)
    arrived = exchange(back.reshape(N_Z, N_Y, QROWS, D), along(0))

    own_grad, other_grad, own_sum = call(
        weigh,
        (
            struct((ROWS, PT, D), F32),
            struct((ROWS, PT, D), BF16),
            struct((1, QROWS), F32),
        ),
        [smem(), vmem(), vmem(), vmem()],
        (vmem(), vmem(), vmem()),
        [
            pltpu.VMEM((ROWS, PT, D), F32),
            pltpu.VMEM((8, QROWS), F32),
            pltpu.SMEM((8, QROWS), F32),
            pltpu.SemaphoreType.DMA,
        ],
    )(codes, sums, asked, probs)
    pos_grad, query_part, scale, losses = call(
        weigh_positives,
        (struct((BATCH, PT, D), F32), struct((QROWS, D), F32), struct((QROWS, D), F32), struct((QD,), F32)),
        [vmem()] * 3,
        (vmem(), vmem(), vmem(), smem()),
    )(own_sum, q_unit, gathered)

    block = (QD + ROWS // GROUP, PT, D)
    kept, off1, off2, off3 = call(
        split,
        (struct(block, F32), struct(block, BF16), struct(block, BF16), struct(block, BF16)),
        [vmem(), vmem(), vmem()],
        (vmem(),) * 4,
    )(own_grad, lax.ppermute(other_grad, "dp", swap), pos_grad)
    moved = [
        lax.ppermute(part, "group", [(g, (g + ahead) % GROUP) for g in range(GROUP)])
        for ahead, part in ((2, off2), (1, off1), (3, off3))
    ]
    arrived = call(
        add_blocks,
        struct((N_Y, QROWS, D), BF16),
        [hbm()] + [anywhere()] * 3,
        vmem(),
        [pltpu.VMEM((N_Z, N_Y, QROWS, D), BF16), pltpu.SemaphoreType.DMA((N_Y,))],
    )(arrived, *moved)
    arrived = exchange(arrived, along(1))
    query_grad = call(
        collect, struct((QD, QT, D), F32), [vmem()] * 3, vmem()
    )(scale, query_part, arrived)
    total = kept + moved[0].astype(F32) + moved[1].astype(F32) + moved[2].astype(F32)
    return losses, query_grad, total[:QD], total[QD:]


def solution(mesh):
    in_specs = (P(EVERY), P(EVERY), P("dp"), P(EVERY), P())
    out_specs = (P(EVERY), P(EVERY), P(EVERY), P(EVERY))
    return jax.shard_map(per_device, mesh=mesh, in_specs=in_specs, out_specs=out_specs, check_vma=False)
```
